32 devices in a mesh: groups: 2 (over y), expert: 4 (over x, core), inner: 4 (over z).
Axes of the slice: x: 2, y: 2, z: 4, core: 2. Of those that a mesh axis runs over, the one named last changes fastest.
Arguments:
- queries: bfloat16 [256, 8192], P(('groups', 'expert', 'inner')), parts along dimension 0, may hold values from -6 to 6
- new_key_value: bfloat16 [256, 1024], P(('groups', 'expert', 'inner')), parts along dimension 0, may hold values from -6 to 6
- cached_key_value: bfloat16 [32, 8, 192, 1024], P(('groups', 'expert', 'inner')), parts along dimension 0, may hold values from -6 to 6
- parents: int32 [32, 8], P(('groups', 'expert', 'inner')), parts along dimension 0, may hold values from 0 to 7
- hidden: bfloat16 [256, 4096], P(('groups', 'expert', 'inner')), parts along dimension 0, may hold values from -6 to 6
- routes: int32 [256, 2], P(('groups', 'expert', 'inner')), parts along dimension 0, may hold values from 0 to 7, all different within a row; in each aligned block of 8 rows (0 to 7, 8 to 15, ...) at most 3 rows name the same one
- gate_values: bfloat16 [256, 2], P(('groups', 'expert', 'inner')), parts along dimension 0, may hold values from 0.19921875 to 1
- gate_up_weight: bfloat16 [8, 2, 4096, 1536], P('expert', None, 'inner'), may hold values from -0.09375 to 0.09375
- down_weight: bfloat16 [8, 1536, 4096], P('expert', None, 'inner'), may hold values from -0.15625 to 0.15625
Outputs:
- attended: bfloat16 [256, 8192], P(('groups', 'expert', 'inner')), parts along dimension 0
- expert_out: bfloat16 [256, 4096], P(('groups', 'expert', 'inner')), parts along dimension 0
The draws below stay inside these ranges and needn't reach their ends.
There are 2 independent parts, one for each index of `groups`. The reference program is written for one: setup_inputs(seed, part) draws one part's arguments, and reference() takes and returns one part's arrays. A program takes and returns all parts, laid end to end along the dimension named above; an argument that names none is the same for every part. Nothing has to cross between parts.
Inputs may be any that keep to these rules, and one draw needn't show every extreme that they name: `routes`: each row names 2 different experts; within the 8 rows of one device no expert is named by more than 3 rows, and in every draw some expert is named by exactly 3 rows of some device.
All inputs are finite; a program needn't handle non-finite values.
Results may differ from the reference program's by a relative error of at most 0.005.
Values may be sent and summed in bfloat16 or wider, within the bound.
No kernel may reach another device: no remote copies, remote signals or barrier semaphores. Data moves between devices by JAX's collectives and lax.ppermute only.
A program may use at most 128 MiB of HBM per device.

```python
import math
import jax
import jax.numpy as jnp
import numpy as np
from jax import lax

D = 4096
QUERY_HEADS = 64
KEY_HEADS = 4
HEAD_SIZE = 128
FF = 1536
BEAM_WIDTH = 8
CAP = 3
REQ_DEV = 1
CACHED_LENGTH = 192
EXPERTS = 8
TOP = 2
REQUEST_COUNT = 16
BEAM_ROWS = 128
N_EXPERT = 4
N_INNER = 4


def draw_queries(key, part):
    key = jax.random.fold_in(key, 11)
    value_rows = jnp.clip(jax.random.normal(key, (BEAM_ROWS, QUERY_HEADS * HEAD_SIZE), jnp.float32), -6.0, 6.0)
    return value_rows.astype(jnp.bfloat16)


def draw_cached_key_value(key, part):
    key = jax.random.fold_in(key, 23)
    value_rows = jnp.clip(jax.random.normal(key, (REQUEST_COUNT, BEAM_WIDTH, CACHED_LENGTH, 2 * KEY_HEADS * HEAD_SIZE), jnp.float32), -6.0, 6.0)
    return value_rows.astype(jnp.bfloat16)


def touch_ends(values, own_key, low, top_value):
    place = [jax.random.randint(jax.random.fold_in(own_key, axis), (), 0, length) for axis, length in enumerate(values.shape)]
    longest = values.shape.index(max(values.shape))
    next_to = place[:longest] + [(place[longest] + 1) % values.shape[longest]] + place[longest + 1:]
    return values.at[tuple(place)].set(low).at[tuple(next_to)].set(top_value)


def level_of(rng, shape, shards, smallest, top_value):
    gain, own = 1.0, jax.random.fold_in(rng, 6)
    for dim, shards_of in shards:
        steps = jnp.exp(jax.random.uniform(jax.random.fold_in(own, dim), (shards_of,), jnp.float32, smallest / len(shards), top_value / len(shards)))
        gain = gain * jnp.repeat(steps, shape[dim] // shards_of).reshape([-1 if axis == dim else 1 for axis in range(len(shape))])
    return gain


def shared_out(own_key, own, number, rows, amount, top, most, lean):
    sequence = jax.random.permutation(own_key, amount)
    crowded, ordinary = load_shares(amount, rows * top, most, lean, True), load_shares(amount, rows * top, most, lean, False)
    places = jnp.arange(amount)

    def named(lengths, offset_by):
        used = int((lengths > 0).sum())
        fixed = max(1, used // 4)
        moved = fixed + (places - fixed + offset_by * (used - fixed)) % max(1, amount - fixed)
        return jnp.zeros((amount,), jnp.int32).at[sequence[jnp.where(places < fixed, places, moved)]].set(jnp.asarray(lengths, jnp.int32))

    lengths = jnp.where(number % 4 == 0, named(crowded, number // 4), named(ordinary, number - number // 4 - 1))
    mixed = jax.random.permutation(jax.random.fold_in(own, 3), amount)
    giver, taker = mixed[0:amount // 2 * 2:2], mixed[1:amount // 2 * 2:2]
    room = jnp.minimum(lengths[giver] - 1, most - lengths[taker]) // 2
    room = jnp.where((giver == sequence[0]) | (taker == sequence[0]) | (lengths[taker] == 0), 0, jnp.maximum(room, 0))
    moved = jax.random.randint(jax.random.fold_in(own, 4), (amount // 2,), 0, 1 << 20) % (room + 1)
    lengths = lengths.at[giver].add(-moved).at[taker].add(moved)
    labels = jnp.searchsorted(jnp.cumsum(lengths), jnp.arange(rows * top), side="right").astype(jnp.int32)
    grid = labels.reshape(top, rows).T
    grid = grid[jax.random.permutation(jax.random.fold_in(own, 1), rows)]
    offset_by = jax.random.randint(jax.random.fold_in(own, 2), (rows, 1), 0, top)
    return jnp.take_along_axis(grid, (jnp.arange(top)[None, :] + offset_by) % top, axis=1)


def load_shares(count, total, bound, lean, full):
    weights = [(1 << 20) // math.isqrt(standing ** lean) + 1 for standing in range(1, count + 1)]
    largest = bound if full else min(bound, max(-(-total // count), total * weights[0] // sum(weights)))
    least = 1 if total - largest >= count - 1 else 0
    counts, spare = [largest] + [least] * (count - 1), total - largest - least * (count - 1)
    while spare > 0:
        candidates = [i for i in range(1, count) if counts[i] < largest] or [i for i in range(1, count) if counts[i] < bound]
        whole, remaining = sum([weights[i] for i in candidates]), spare
        for i in candidates:
            extra = min(bound - counts[i], max(1, remaining * weights[i] // whole), spare)
            counts[i] = counts[i] + extra
            spare = spare - extra
    return np.array(counts)


def centred(rng, extent, deviation, bound, pieces=(), kind=jnp.bfloat16):
    factor_of = level_of(rng, extent, pieces, -0.22, 0.18) if pieces else 1.0
    values = jax.random.normal(rng, extent, jnp.float32) * deviation * factor_of
    return jnp.minimum(jnp.maximum(values, -bound), bound).astype(kind)


def setup_inputs(seed: int = 0, part: int = 0) -> dict:
    splits = jax.random.split(jax.random.key(seed), 10)
    own_keys = jax.random.split(jax.random.fold_in(splits[9], part), 10)
    queries = draw_queries(jax.random.fold_in(jax.random.fold_in(splits[9], part), 71), part)
    new_key_value = centred(own_keys[1], (BEAM_ROWS, 2 * KEY_HEADS * HEAD_SIZE), 1.0, 6.0, ((0, 16),))
    cached_key_value = draw_cached_key_value(jax.random.fold_in(jax.random.fold_in(splits[9], part), 71), part)
    parents = touch_ends(jax.random.randint(own_keys[3], (REQUEST_COUNT, BEAM_WIDTH), 0, BEAM_WIDTH), jax.random.fold_in(own_keys[3], 1), 0, BEAM_WIDTH - 1).astype(jnp.int32)
    hidden = centred(own_keys[4], (BEAM_ROWS, D), 1.0, 6.0, ((0, 16),))
    routes_keys = jax.random.split(jax.random.fold_in(own_keys[5], 1), BEAM_ROWS // (BEAM_WIDTH * REQ_DEV))
    routes_turns = jax.random.permutation(jax.random.fold_in(own_keys[5], 3), BEAM_ROWS // (BEAM_WIDTH * REQ_DEV))
    routes = jax.vmap(lambda own, number: shared_out(jax.random.fold_in(own_keys[5], 2), own, number, BEAM_WIDTH * REQ_DEV, EXPERTS, TOP, CAP, 2))(routes_keys, routes_turns).reshape((BEAM_ROWS, TOP))
    gate_values = jnp.clip(0.19921875 + 0.80078125 * jax.random.uniform(own_keys[6], (BEAM_ROWS, TOP), jnp.float32) ** level_of(own_keys[6], (BEAM_ROWS, TOP), ((0, 16),), -0.2, 0.2), 0.19921875, 1.0).astype(jnp.bfloat16)
    gate_up_weight = centred(splits[7], (EXPERTS, 2, D, FF), D ** -0.5, 0.09375, ((0, 4), (2, 4)))
    down_weight = centred(splits[8], (EXPERTS, FF, D), FF ** -0.5, 0.15625, ((0, 4), (2, 4)))
    return dict(queries=queries, new_key_value=new_key_value, cached_key_value=cached_key_value, parents=parents, hidden=hidden, routes=routes, gate_values=gate_values, gate_up_weight=gate_up_weight, down_weight=down_weight)


def attend_request(query_matrix, new_token_pair, cache_rows, parent_ids):
    query_group = QUERY_HEADS // KEY_HEADS
    score_scale = 1.0 / math.sqrt(HEAD_SIZE)
    selected_parent = jnp.take(cache_rows, parent_ids.astype(jnp.int32), axis=0).astype(jnp.float32)
    selected_parent = selected_parent.reshape(BEAM_WIDTH, CACHED_LENGTH, 2, KEY_HEADS, HEAD_SIZE)
    keys = selected_parent[:, :, 0]
    value_rows = selected_parent[:, :, 1]
    new_token_pairs_all = new_token_pair.astype(jnp.float32).reshape(BEAM_WIDTH, 2, KEY_HEADS, HEAD_SIZE)
    query_vector = query_matrix.astype(jnp.float32).reshape(BEAM_WIDTH, KEY_HEADS, query_group, HEAD_SIZE)
    scores = jnp.einsum('bkgd,blkd->bkgl', query_vector, keys) * score_scale
    beam_private = jnp.einsum('wpaf,wpf->wpa', query_vector, new_token_pairs_all[:, 0]) * score_scale
    upper = jnp.maximum(lax.optimization_barrier(jnp.max(scores, axis=-1)), beam_private)
    expo = jnp.exp(scores - upper[..., None])
    own_expo = jnp.exp(beam_private - upper)
    total = lax.optimization_barrier(jnp.sum(expo, axis=-1)) + own_expo
    probs = lax.optimization_barrier((expo / total[..., None]).astype(jnp.bfloat16)).astype(jnp.float32)
    own_prob = lax.optimization_barrier((own_expo / total).astype(jnp.bfloat16)).astype(jnp.float32)
    result = jnp.einsum('bkgl,blkd->bkgd', probs, value_rows) + own_prob[..., None] * new_token_pairs_all[:, 1][:, :, None, :]
    return result.reshape(BEAM_WIDTH, QUERY_HEADS * HEAD_SIZE).astype(jnp.bfloat16)

def reference(queries, new_key_value, cached_key_value, parents, hidden, routes, gate_values, gate_up_weight, down_weight):

    def single_request(items):
        return attend_request(items[0], items[1], items[2], items[3])
    attended = lax.map(single_request, (queries.reshape(REQUEST_COUNT, BEAM_WIDTH, QUERY_HEADS * HEAD_SIZE), new_key_value.reshape(REQUEST_COUNT, BEAM_WIDTH, 2 * KEY_HEADS * HEAD_SIZE), cached_key_value, parents))
    attended = attended.reshape(BEAM_ROWS, QUERY_HEADS * HEAD_SIZE)
    gate_float = gate_values.astype(jnp.float32)
    most_rows = N_EXPERT * N_INNER * CAP

    def per_expert(total, item):
        index, gate_up, down = item
        named = routes == index
        selected_parent = lax.optimization_barrier(jnp.sum(named.astype(jnp.int32), axis=1)).astype(jnp.int32)
        share = lax.optimization_barrier(jnp.sum(jnp.where(named, gate_float, jnp.zeros_like(gate_float)), axis=1))
        order = jnp.argsort(-selected_parent, stable=True)[:most_rows].astype(jnp.int32)
        rows_in = jnp.take(hidden, order, axis=0)
        gate = jnp.dot(rows_in, gate_up[0], preferred_element_type=jnp.float32)
        upward = jnp.dot(rows_in, gate_up[1], preferred_element_type=jnp.float32)
        active = (jax.nn.silu(gate) * upward).astype(jnp.bfloat16)
        output = jnp.dot(active, down, preferred_element_type=jnp.float32)
        weight = jnp.take(share, order)
        return (total.at[order].add(weight[:, None] * output), None)
    start = jnp.zeros((BEAM_ROWS, D), jnp.float32)
    total, unused = lax.scan(per_expert, start, (jnp.arange(EXPERTS, dtype=jnp.int32), gate_up_weight, down_weight))
    return (attended, total.astype(jnp.bfloat16))
```

```python
import functools
import math

import jax
import jax.numpy as jnp
from jax import lax
from jax.experimental import pallas as pl
from jax.experimental.pallas import tpu as pltpu
from jax.sharding import PartitionSpec as P

QUERY_HEADS = 64
KEY_HEADS = 4
HEAD_SIZE = 128
CAP = 3
CAP_PAD = 4


def params(limit, *semantics):
    return pltpu.CompilerParams(
        dimension_semantics=semantics or None, vmem_limit_bytes=limit * 1024 * 1024
    )


def attend_kernel(parents, q_ref, new_ref, cache_ref, out_ref):
    del parents
    group = QUERY_HEADS // KEY_HEADS
    scale = 1.0 / math.sqrt(HEAD_SIZE)
    width = KEY_HEADS * HEAD_SIZE
    q = q_ref[0]
    fresh = new_ref[0].astype(jnp.float32)
    scores, own = [], []
    for k in range(KEY_HEADS):
        qk = q[k * group:(k + 1) * group]
        keys = cache_ref[0, 0, :, k * HEAD_SIZE:(k + 1) * HEAD_SIZE]
        scores.append(
            lax.dot_general(qk, keys, (((1,), (1,)), ((), ())), preferred_element_type=jnp.float32)
        )
        own.append(
            jnp.sum(qk.astype(jnp.float32) * fresh[k:k + 1], axis=-1, keepdims=True)
        )
    scores = jnp.concatenate(scores, axis=0) * scale
    own = jnp.concatenate(own, axis=0) * scale
    upper = jnp.maximum(jnp.max(scores, axis=-1, keepdims=True), own)
    expo = jnp.exp(scores - upper)
    own_expo = jnp.exp(own - upper)
    total = jnp.sum(expo, axis=-1, keepdims=True) + own_expo
    probs = (expo / total).astype(jnp.bfloat16)
    own_prob = (own_expo / total).astype(jnp.bfloat16).astype(jnp.float32)
    for k in range(KEY_HEADS):
        rows = slice(k * group, (k + 1) * group)
        values = cache_ref[0, 0, :, width + k * HEAD_SIZE:width + (k + 1) * HEAD_SIZE]
        result = jnp.dot(probs[rows], values, preferred_element_type=jnp.float32)
        result = result + own_prob[rows] * fresh[KEY_HEADS + k:KEY_HEADS + k + 1]
        out_ref[0, rows] = result.astype(out_ref.dtype)


def attend(queries, new_key_value, cached_key_value, parents):
    rows = queries.shape[0]
    _, beams, length, width = cached_key_value.shape
    out = pl.pallas_call(
        attend_kernel,
        grid_spec=pltpu.PrefetchScalarGridSpec(
            num_scalar_prefetch=1,
            grid=(rows,),
            in_specs=[
                pl.BlockSpec((1, QUERY_HEADS, HEAD_SIZE), lambda r, p: (r, 0, 0)),
                pl.BlockSpec((1, 2 * KEY_HEADS, HEAD_SIZE), lambda r, p: (r, 0, 0)),
                pl.BlockSpec((1, 1, length, width), lambda r, p: (r // beams, p[r], 0, 0)),
            ],
            out_specs=pl.BlockSpec((1, QUERY_HEADS, HEAD_SIZE), lambda r, p: (r, 0, 0)),
        ),
        out_shape=jax.ShapeDtypeStruct((rows, QUERY_HEADS, HEAD_SIZE), jnp.bfloat16),
        compiler_params=params(8),
        cost_estimate=pl.CostEstimate(
            flops=4 * rows * QUERY_HEADS * HEAD_SIZE * length,
            bytes_accessed=2 * rows * length * width,
            transcendentals=rows * QUERY_HEADS * length,
        ),
        name="attend",
    )(
        parents.reshape(rows),
        queries.reshape(rows, QUERY_HEADS, HEAD_SIZE),
        new_key_value.reshape(rows, 2 * KEY_HEADS, HEAD_SIZE),
        cached_key_value,
    )
    return out.reshape(rows, QUERY_HEADS * HEAD_SIZE)


def placing(turned_routes, slots):
    top, rows = turned_routes.shape
    slot = lax.broadcasted_iota(jnp.int32, (slots, rows), 0)
    expert, rank = slot // CAP_PAD, slot % CAP_PAD
    member = jnp.zeros((slots, rows), jnp.float32)
    for t in range(top):
        member = jnp.where(turned_routes[t:t + 1] == expert, 1.0, member)
    before = (
        lax.broadcasted_iota(jnp.int32, (rows, rows), 0)
        < lax.broadcasted_iota(jnp.int32, (rows, rows), 1)
    ).astype(jnp.float32)
    ranks = jnp.dot(member, before, preferred_element_type=jnp.float32)
    return jnp.where(ranks == rank.astype(jnp.float32), member, 0.0)


def dispatch_kernel(routes_ref, hidden_ref, out_ref):
    owners, inner, block, width = out_ref.shape
    place = placing(routes_ref[...], owners * block).astype(jnp.bfloat16)
    for i in range(inner):
        moved = jnp.dot(
            place, hidden_ref[:, i * width:(i + 1) * width], preferred_element_type=jnp.float32
        ).astype(jnp.bfloat16)
        for e in range(owners):
            out_ref[e, i] = moved[e * block:(e + 1) * block]


def combine_kernel(routes_ref, gates_ref, back_ref, out_ref):
    owners, inner, block, width = back_ref.shape
    slots = owners * block
    routes, gates = routes_ref[...], gates_ref[...].astype(jnp.float32)
    place = placing(routes, slots)
    expert = lax.broadcasted_iota(jnp.int32, place.shape, 0) // CAP_PAD
    weight = jnp.zeros_like(place)
    for t in range(routes.shape[0]):
        weight = weight + jnp.where(routes[t:t + 1] == expert, gates[t:t + 1], 0.0)
    weight = (weight * place).astype(jnp.bfloat16)
    for i in range(inner):
        rows = jnp.concatenate([back_ref[e, i] for e in range(owners)], axis=0)
        out_ref[:, i * width:(i + 1) * width] = lax.dot_general(
            weight, rows, (((0,), (0,)), ((), ())), preferred_element_type=jnp.float32
        ).astype(out_ref.dtype)


def picks(sources, block, expert):
    shape = (sources * CAP, sources * block)
    row = lax.broadcasted_iota(jnp.int32, shape, 0)
    slot = lax.broadcasted_iota(jnp.int32, shape, 1)
    wanted = (row % sources) * block + expert * CAP_PAD + row // sources
    return (slot == wanted).astype(jnp.bfloat16)


def select_kernel(slots_ref, out_ref):
    sources, block, width = slots_ref.shape
    slots = slots_ref[...].reshape(sources * block, width)
    for x in range(out_ref.shape[0]):
        out_ref[x] = jnp.dot(
            picks(sources, block, x), slots, preferred_element_type=jnp.float32
        ).astype(out_ref.dtype)


def gate_up_kernel(chunk, rows_ref, weight_ref, out_ref):
    del chunk
    ff = weight_ref.shape[3]
    rows = rows_ref[0]
    for k in range(2):
        out_ref[0, :, k * ff:(k + 1) * ff] = jnp.dot(
            rows, weight_ref[0, k], preferred_element_type=jnp.float32
        ).astype(out_ref.dtype)


def gate_up(chunk, chunks, rows, weight, dtype):
    experts, count, depth = rows.shape
    ff = weight.shape[3] // chunks
    return pl.pallas_call(
        gate_up_kernel,
        grid_spec=pltpu.PrefetchScalarGridSpec(
            num_scalar_prefetch=1,
            grid=(experts,),
            in_specs=[
                pl.BlockSpec((1, count, depth), lambda x, c: (x, 0, 0)),
                pl.BlockSpec((1, 2, depth, ff), lambda x, c: (x, 0, 0, c[0])),
            ],
            out_specs=pl.BlockSpec((1, count, 2 * ff), lambda x, c: (x, 0, 0)),
        ),
        out_shape=jax.ShapeDtypeStruct((experts, count, 2 * ff), dtype),
        compiler_params=params(16),
        cost_estimate=pl.CostEstimate(
            flops=4 * experts * count * depth * ff,
            bytes_accessed=4 * experts * depth * ff,
            transcendentals=0,
        ),
        name="gate_up",
    )(chunk, rows, weight)


def activate_kernel(*refs):
    own_ref, other_refs, out_ref = refs[0], refs[1:-1], refs[-1]
    ff = out_ref.shape[2]
    for x in range(out_ref.shape[0]):
        total = own_ref[x]
        for ref in other_refs:
            total = total + ref[x].astype(jnp.float32)
        gate, up = total[:, :ff], total[:, ff:]
        out_ref[x] = (gate / (1.0 + jnp.exp(-gate)) * up).astype(out_ref.dtype)


def down_kernel(inner, *refs):
    del inner
    weight_ref, out_ref, sum_ref = refs[-3], refs[-2], refs[-1]
    chunks = len(refs) - 3
    step, x = pl.program_id(0), pl.program_id(1)
    experts, count, _ = sum_ref.shape
    for s in range(chunks):
        @pl.when(step == s)
        def _():
            product = jnp.dot(refs[s][x], weight_ref[0], preferred_element_type=jnp.float32)
            sum_ref[x] = product if s == 0 else sum_ref[x] + product

    @pl.when((step == chunks - 1) & (x == experts - 1))
    def _():
        sources, block, width = out_ref.shape
        back = jnp.zeros((sources * block, width), jnp.float32)
        for y in range(experts):
            back = back + lax.dot_general(
                picks(sources, block, y),
                sum_ref[y].astype(jnp.bfloat16),
                (((0,), (0,)), ((), ())),
                preferred_element_type=jnp.float32,
            )
        out_ref[...] = back.astype(out_ref.dtype).reshape(sources, block, width)


def down(inner, parts, weight, sources, block):
    chunks = len(parts)
    experts, count, ff = parts[0].shape
    width = weight.shape[2]
    return pl.pallas_call(
        down_kernel,
        grid_spec=pltpu.PrefetchScalarGridSpec(
            num_scalar_prefetch=1,
            grid=(chunks, experts),
            in_specs=[pl.BlockSpec((experts, count, ff), lambda s, x, i: (0, 0, 0))] * chunks
            + [
                pl.BlockSpec(
                    (1, ff, width), lambda s, x, i: (x, lax.rem(i[0] + chunks - s, chunks), 0)
                )
            ],
            out_specs=pl.BlockSpec((sources, block, width), lambda s, x, i: (0, 0, 0)),
            scratch_shapes=[pltpu.VMEM((experts, count, width), jnp.float32)],
        ),
        out_shape=jax.ShapeDtypeStruct((sources, block, width), jnp.bfloat16),
        compiler_params=params(24),
        cost_estimate=pl.CostEstimate(
            flops=2 * experts * count * chunks * ff * width,
            bytes_accessed=2 * experts * chunks * ff * width,
            transcendentals=0,
        ),
        name="down",
    )(inner, *parts, weight)


def shifted(value, steps):
    size = lax.axis_size("inner")
    return lax.ppermute(value, "inner", [(i, (i + steps) % size) for i in range(size)])


def experts_by_columns(held, gate_up_weight, down_weight, sources, block):
    inner = lax.axis_size("inner")
    experts, count, _ = held.shape
    ff = gate_up_weight.shape[3]
    me = lax.axis_index("inner").astype(jnp.int32)
    order = [s for s in range(1, inner)]
    order.sort(key=lambda s: -min(s, inner - s))
    others = []
    for s in order:
        part = gate_up(((me + s) % inner).reshape(1), inner, held, gate_up_weight, jnp.bfloat16)
        others.append(shifted(part, s))
    own = gate_up(me.reshape(1), inner, held, gate_up_weight, jnp.float32)
    active = pl.pallas_call(
        activate_kernel,
        out_shape=jax.ShapeDtypeStruct((experts, count, ff // inner), jnp.bfloat16),
        compiler_params=params(32),
        name="activate",
    )(own, *others)
    parts = [active] + [shifted(active, s) for s in range(1, inner)]
    return down(me.reshape(1), parts, down_weight, sources, block)


def experts_by_rows(held, gate_up_weight, down_weight, sources, block):
    experts, count, _ = held.shape
    partial = jnp.einsum("xsd,xkdf->sxkf", held, gate_up_weight, preferred_element_type=jnp.float32)
    summed = lax.psum_scatter(partial, "inner", scatter_dimension=0, tiled=True)
    active = (jax.nn.silu(summed[:, :, 0]) * summed[:, :, 1]).astype(jnp.bfloat16)
    active = lax.all_gather(active, "inner", axis=0, tiled=True)
    outputs = jnp.einsum("sxf,xfd->xsd", active, down_weight, preferred_element_type=jnp.float32)
    outputs = outputs.astype(jnp.bfloat16).reshape(experts, CAP, sources, -1)
    outputs = jnp.pad(outputs, ((0, 0), (0, CAP_PAD - CAP), (0, 0), (0, 0)))
    return jnp.transpose(outputs, (2, 0, 1, 3)).reshape(sources, block, -1)


def body(
    queries,
    new_key_value,
    cached_key_value,
    parents,
    hidden,
    routes,
    gate_values,
    gate_up_weight,
    down_weight,
):
    owners, inner = lax.axis_size("expert"), lax.axis_size("inner")
    sources = owners * inner
    experts, _, depth, ff = gate_up_weight.shape
    rows, model = hidden.shape
    width = down_weight.shape[2]
    block = experts * CAP_PAD
    turned_routes, turned_gates = routes.T, gate_values.T
    both = ("expert", "inner")

    sent = pl.pallas_call(
        dispatch_kernel,
        out_shape=jax.ShapeDtypeStruct((owners, inner, block, depth), jnp.bfloat16),
        compiler_params=params(16),
        name="dispatch",
    )(turned_routes, hidden)
    slots = lax.all_to_all(
        sent.reshape(sources, block, depth), both, split_axis=0, concat_axis=0, tiled=True
    )
    attended = attend(queries, new_key_value, cached_key_value, parents)

    held = pl.pallas_call(
        select_kernel,
        out_shape=jax.ShapeDtypeStruct((experts, sources * CAP, depth), jnp.bfloat16),
        compiler_params=params(24),
        name="select",
    )(slots)
    even = ff % (inner * 128) == 0
    back = (experts_by_columns if even else experts_by_rows)(
        held, gate_up_weight, down_weight, sources, block
    )
    returned = lax.all_to_all(back, both, split_axis=0, concat_axis=0, tiled=True)
    expert_out = pl.pallas_call(
        combine_kernel,
        out_shape=jax.ShapeDtypeStruct((rows, model), jnp.bfloat16),
        compiler_params=params(16),
        name="combine",
    )(turned_routes, turned_gates, returned.reshape(owners, inner, block, width))
    return attended, expert_out


def solution(mesh):
    rows = ("groups", "expert", "inner")
    return jax.shard_map(
        body,
        mesh=mesh,
        in_specs=(
            P(rows, None),
            P(rows, None),
            P(rows, None, None, None),
            P(rows, None),
            P(rows, None),
            P(rows, None),
            P(rows, None),
            P("expert", None, "inner", None),
            P("expert", None, "inner"),
        ),
        out_specs=(P(rows, None), P(rows, None)),
        check_vma=False,
    )
```

```python
import functools
import math

import jax
import jax.numpy as jnp
from jax import lax
from jax.experimental import pallas as pl
from jax.experimental.pallas import tpu as pltpu
from jax.sharding import PartitionSpec as P

QUERY_HEADS = 64
KEY_HEADS = 4
HEAD_SIZE = 128
CAP = 3
LANES = 128


def params(limit, *semantics):
    return pltpu.CompilerParams(
        dimension_semantics=semantics or None, vmem_limit_bytes=limit * 1024 * 1024
    )


def attend_kernel(parents, q_ref, new_ref, cache_ref, after_ref, out_ref):
    del parents, after_ref
    group = QUERY_HEADS // KEY_HEADS
    scale = 1.0 / math.sqrt(HEAD_SIZE)
    width = KEY_HEADS * HEAD_SIZE
    q = q_ref[0]
    fresh = new_ref[0].astype(jnp.float32)
    scores, own = [], []
    for k in range(KEY_HEADS):
        qk = q[k * group:(k + 1) * group]
        keys = cache_ref[0, 0, :, k * HEAD_SIZE:(k + 1) * HEAD_SIZE]
        scores.append(
            lax.dot_general(qk, keys, (((1,), (1,)), ((), ())), preferred_element_type=jnp.float32)
        )
        own.append(
            jnp.sum(qk.astype(jnp.float32) * fresh[k:k + 1], axis=-1, keepdims=True)
        )
    scores = jnp.concatenate(scores, axis=0) * scale
    own = jnp.concatenate(own, axis=0) * scale
    upper = jnp.maximum(jnp.max(scores, axis=-1, keepdims=True), own)
    expo = jnp.exp(scores - upper)
    own_expo = jnp.exp(own - upper)
    total = jnp.sum(expo, axis=-1, keepdims=True) + own_expo
    probs = (expo / total).astype(jnp.bfloat16)
    own_prob = (own_expo / total).astype(jnp.bfloat16).astype(jnp.float32)
    for k in range(KEY_HEADS):
        rows = slice(k * group, (k + 1) * group)
        values = cache_ref[0, 0, :, width + k * HEAD_SIZE:width + (k + 1) * HEAD_SIZE]
        result = jnp.dot(probs[rows], values, preferred_element_type=jnp.float32)
        result = result + own_prob[rows] * fresh[KEY_HEADS + k:KEY_HEADS + k + 1]
        out_ref[0, rows] = result.astype(out_ref.dtype)


def attend(queries, new_key_value, cached_key_value, parents, after):
    rows = queries.shape[0]
    _, beams, length, width = cached_key_value.shape
    out = pl.pallas_call(
        attend_kernel,
        grid_spec=pltpu.PrefetchScalarGridSpec(
            num_scalar_prefetch=1,
            grid=(rows,),
            in_specs=[
                pl.BlockSpec((1, QUERY_HEADS, HEAD_SIZE), lambda r, p: (r, 0, 0)),
                pl.BlockSpec((1, 2 * KEY_HEADS, HEAD_SIZE), lambda r, p: (r, 0, 0)),
                pl.BlockSpec((1, 1, length, width), lambda r, p: (r // beams, p[r], 0, 0)),
                pl.BlockSpec(memory_space=pl.ANY),
            ],
            out_specs=pl.BlockSpec((1, QUERY_HEADS, HEAD_SIZE), lambda r, p: (r, 0, 0)),
        ),
        out_shape=jax.ShapeDtypeStruct((rows, QUERY_HEADS, HEAD_SIZE), jnp.bfloat16),
        compiler_params=params(50),
        cost_estimate=pl.CostEstimate(
            flops=4 * rows * QUERY_HEADS * HEAD_SIZE * length,
            bytes_accessed=2 * rows * length * width,
            transcendentals=rows * QUERY_HEADS * length,
        ),
        name="attend",
    )(
        parents.reshape(rows),
        queries.reshape(rows, QUERY_HEADS, HEAD_SIZE),
        new_key_value.reshape(rows, 2 * KEY_HEADS, HEAD_SIZE),
        cached_key_value,
        after,
    )
    return out.reshape(rows, QUERY_HEADS * HEAD_SIZE)


def spread(values, lanes, first):
    top = values.shape[0]
    shape = (top, lanes)
    chosen = (
        lax.broadcasted_iota(jnp.int32, shape, 1)
        == lax.broadcasted_iota(jnp.int32, shape, 0) + first
    ).astype(jnp.float32)
    return lax.dot_general(
        values.astype(jnp.float32), chosen, (((0,), (0,)), ((), ())), preferred_element_type=jnp.float32
    )


def prepare_kernel(me, routes_ref, gates_ref, hidden_ref, *out_refs):
    chunks = len(out_refs)
    width = hidden_ref.shape[1] // chunks
    top = routes_ref.shape[0]
    notes = spread(routes_ref[...], LANES, 0) + spread(gates_ref[...], LANES, top)
    notes = notes.astype(jnp.bfloat16)
    for s in range(chunks):
        start = pl.multiple_of(lax.rem(me[0] + s, chunks) * width, width)
        out_refs[s][:, :width] = hidden_ref[:, pl.ds(start, width)]
        out_refs[s][:, width:] = notes


def turned_notes(notes, top):
    shape = (max(8, 2 * top), LANES)
    chosen = (
        lax.broadcasted_iota(jnp.int32, shape, 0) == lax.broadcasted_iota(jnp.int32, shape, 1)
    ).astype(jnp.bfloat16)
    turned = lax.dot_general(
        chosen, notes, (((1,), (1,)), ((), ())), preferred_element_type=jnp.float32
    )
    return turned[:top], turned[top:2 * top]


def placing(routes, owner, level, experts, sources):
    top, rows = routes.shape
    count = CAP * sources
    shape = (experts * count, rows)
    slot = lax.broadcasted_iota(jnp.int32, shape, 0)
    row = lax.broadcasted_iota(jnp.int32, shape, 1)
    each = rows // sources
    local = jnp.zeros(shape, jnp.int32)
    for x in range(1, experts):
        local = local + (slot >= x * count).astype(jnp.int32)
    within = slot - local * count
    rank, source = within // sources, within % sources
    expert = (owner * experts + local).astype(jnp.float32)
    member = jnp.zeros(shape, jnp.float32)
    for t in range(top):
        member = jnp.where(routes[t:t + 1] == expert, 1.0, member)
    origin = level - row // each
    origin = jnp.where(origin < 0, origin + sources, origin)
    member = jnp.where(origin == source, member, 0.0)
    one = lax.broadcasted_iota(jnp.int32, (rows, rows), 0)
    other = lax.broadcasted_iota(jnp.int32, (rows, rows), 1)
    before = (one < other).astype(jnp.float32)
    ranks = jnp.dot(member, before, preferred_element_type=jnp.float32)
    return jnp.where(ranks == rank.astype(jnp.float32), member, 0.0), expert


def pack_kernel(top, experts, sources, column, level, *refs):
    owners = len(refs) - sources
    held, out_refs = refs[:sources], refs[sources:]
    width = out_refs[0].shape[1]
    rows = jnp.concatenate([ref[:, :width] for ref in held], axis=0)
    notes = jnp.concatenate([ref[:, width:] for ref in held], axis=0)
    routes, _ = turned_notes(notes, top)
    for t in range(owners):
        place, _ = placing(routes, lax.rem(column[0] + t, owners), level[0], experts, sources)
        out_refs[t][...] = jnp.dot(
            place.astype(jnp.bfloat16), rows, preferred_element_type=jnp.float32
        ).astype(out_refs[t].dtype)


def combine_kernel(top, experts, sources, column, level, *refs):
    owners = len(refs) - 2 * sources
    held, back, out_refs = refs[:sources], refs[sources:sources + owners], refs[sources + owners:]
    each, width = out_refs[0].shape
    notes = jnp.concatenate([ref[:, width:] for ref in held], axis=0)
    routes, gates = turned_notes(notes, top)
    total = jnp.zeros((sources * each, width), jnp.float32)
    for t in range(owners):
        place, expert = placing(routes, lax.rem(column[0] + t, owners), level[0], experts, sources)
        weight = jnp.zeros_like(place)
        for k in range(top):
            weight = weight + jnp.where(routes[k:k + 1] == expert, gates[k:k + 1], 0.0)
        total = total + lax.dot_general(
            (weight * place).astype(jnp.bfloat16),
            back[t][...],
            (((0,), (0,)), ((), ())),
            preferred_element_type=jnp.float32,
        )
    for s in range(sources):
        out_refs[s][...] = total[s * each:(s + 1) * each].astype(out_refs[s].dtype)


def assemble_kernel(me, *refs):
    chunks = len(refs) - 1
    out_ref = refs[-1]
    width = refs[0].shape[1]
    for s in range(chunks):
        start = pl.multiple_of(lax.rem(me[0] + s, chunks) * width, width)
        out_ref[:, pl.ds(start, width)] = refs[s][...]


def regroup(experts, owners, count):
    shape = (experts * owners * count, owners * experts * count)
    row = lax.broadcasted_iota(jnp.int32, shape, 0)
    other = lax.broadcasted_iota(jnp.int32, shape, 1)
    wanted = jnp.zeros(shape, jnp.int32) + row
    for x in range(experts):
        for t in range(owners):
            first = (x * owners + t) * count
            inside = (row >= first) & (row < first + count)
            wanted = jnp.where(inside, row - first + (t * experts + x) * count, wanted)
    return (other == wanted).astype(jnp.bfloat16)


def select_kernel(*refs):
    packs, out_ref = refs[:-1], refs[-1]
    experts, count, _ = out_ref.shape
    rows = jnp.concatenate([ref[...].astype(jnp.float32) for ref in packs], axis=0)
    moved = jnp.dot(
        regroup(experts, len(packs), count // len(packs)),
        rows.astype(jnp.bfloat16),
        preferred_element_type=jnp.float32,
    ).astype(out_ref.dtype)
    for x in range(experts):
        out_ref[x] = moved[x * count:(x + 1) * count]


def gate_up_kernel(chunk, rows_ref, weight_ref, out_ref, done_ref=None):
    del chunk
    if done_ref is not None:
        done_ref[...] = jnp.zeros_like(done_ref)
    ff = weight_ref.shape[3]
    rows = rows_ref[0]
    for k in range(2):
        out_ref[0, :, k * ff:(k + 1) * ff] = jnp.dot(
            rows, weight_ref[0, k], preferred_element_type=jnp.float32
        ).astype(out_ref.dtype)


def gate_up(chunk, chunks, rows, weight, dtype, done=False):
    experts, count, depth = rows.shape
    ff = weight.shape[3] // chunks
    return pl.pallas_call(
        gate_up_kernel,
        grid_spec=pltpu.PrefetchScalarGridSpec(
            num_scalar_prefetch=1,
            grid=(experts,),
            in_specs=[
                pl.BlockSpec((1, count, depth), lambda x, c: (x, 0, 0)),
                pl.BlockSpec((1, 2, depth, ff), lambda x, c: (x, 0, 0, c[0])),
            ],
            out_specs=[pl.BlockSpec((1, count, 2 * ff), lambda x, c: (x, 0, 0))]
            + [pl.BlockSpec((8, LANES), lambda x, c: (0, 0))] * done,
        ),
        out_shape=[jax.ShapeDtypeStruct((experts, count, 2 * ff), dtype)]
        + [jax.ShapeDtypeStruct((8, LANES), jnp.float32)] * done,
        compiler_params=params(52),
        cost_estimate=pl.CostEstimate(
            flops=4 * experts * count * depth * ff,
            bytes_accessed=4 * experts * depth * ff,
            transcendentals=0,
        ),
        name="gate_up",
    )(chunk, rows, weight)


def activate_kernel(own_ref, *refs):
    other_refs, out_ref = refs[:-2], refs[-1]
    ff = out_ref.shape[2]
    for x in range(out_ref.shape[0]):
        total = own_ref[x]
        for ref in other_refs:
            total = total + ref[x].astype(jnp.float32)
        gate, up = total[:, :ff], total[:, ff:]
        out_ref[x] = (gate / (1.0 + jnp.exp(-gate)) * up).astype(out_ref.dtype)


def down_own_kernel(me, part_ref, weight_ref, sum_ref):
    ff = part_ref.shape[2]
    chunk = pl.ds(pl.multiple_of(me[0] * ff, ff), ff)
    for x in range(part_ref.shape[0]):
        sum_ref[x] = jnp.dot(part_ref[x], weight_ref[x, chunk], preferred_element_type=jnp.float32)


def down_rest_kernel(chunks, me, sum_ref, *refs):
    parts, weight_ref, out_refs = refs[:chunks - 1], refs[chunks - 1], refs[chunks:]
    experts, count, width = sum_ref.shape
    ff = parts[0].shape[2]
    sums = []
    for x in range(experts):
        total = sum_ref[x]
        for s in range(1, chunks):
            chunk = lax.rem(me[0] + chunks - s, chunks)
            chunk = pl.ds(pl.multiple_of(chunk * ff, ff), ff)
            total = total + jnp.dot(
                parts[s - 1][x], weight_ref[x, chunk], preferred_element_type=jnp.float32
            )
        sums.append(total.astype(jnp.bfloat16))
    owners = len(out_refs)
    rows = experts * count // owners
    moved = lax.dot_general(
        regroup(experts, owners, count // owners),
        jnp.concatenate(sums, axis=0),
        (((0,), (0,)), ((), ())),
        preferred_element_type=jnp.float32,
    )
    for t in range(owners):
        out_refs[t][...] = moved[t * rows:(t + 1) * rows].astype(out_refs[t].dtype)


def shifted(value, axis, steps):
    size = lax.axis_size(axis)
    return lax.ppermute(value, axis, [(i, (i + steps) % size) for i in range(size)])


def farthest_first(size):
    return sorted(range(1, size), key=lambda s: -min(s, size - s))


def exchange(values, axis, back=False):
    out = [values[0]] + [None] * (len(values) - 1)
    for s in farthest_first(len(values)):
        out[s] = shifted(values[s], axis, -s if back else s)
    return out


def call(kernel, index, inputs, outputs, name, limit=16, after=()):
    single = not isinstance(outputs, list)
    return pl.pallas_call(
        kernel,
        in_specs=[pl.BlockSpec(memory_space=pltpu.SMEM)] * len(index)
        + [pl.BlockSpec(memory_space=pltpu.VMEM)] * len(inputs)
        + [pl.BlockSpec(memory_space=pl.ANY)] * len(after),
        out_specs=pl.BlockSpec(memory_space=pltpu.VMEM)
        if single
        else [pl.BlockSpec(memory_space=pltpu.VMEM)] * len(outputs),
        out_shape=outputs,
        compiler_params=params(limit),
        name=name,
    )(*index, *inputs, *after)


def experts_by_columns(held, gate_up_weight, down_weight, owners, attention):
    inner = lax.axis_size("inner")
    experts, count, _ = held.shape
    ff, width = down_weight.shape[1:]
    me = lax.axis_index("inner").astype(jnp.int32)
    level = me.reshape(1)
    others = []
    for s in farthest_first(inner):
        (part,) = gate_up(((me + s) % inner).reshape(1), inner, held, gate_up_weight, jnp.bfloat16)
        others.append(shifted(part, "inner", s))
    own, done = gate_up(level, inner, held, gate_up_weight, jnp.float32, True)
    attended = attention(done)
    active = call(
        activate_kernel,
        [],
        [own, *others],
        jax.ShapeDtypeStruct((experts, count, ff // inner), jnp.bfloat16),
        "activate",
        after=[attended],
    )
    parts = exchange([active] * inner, "inner")
    sums = call(
        down_own_kernel,
        [level],
        [parts[0], down_weight],
        jax.ShapeDtypeStruct((experts, count, width), jnp.float32),
        "down_own",
        24,
    )
    back = call(
        functools.partial(down_rest_kernel, inner),
        [level],
        [sums, *parts[1:], down_weight],
        [jax.ShapeDtypeStruct((experts * count // owners, width), jnp.bfloat16)] * owners,
        "down_rest",
        24,
    )
    return back, attended


def experts_by_rows(held, gate_up_weight, down_weight, owners, attention):
    experts, count, _ = held.shape
    partial = jnp.einsum("xsd,xkdf->sxkf", held, gate_up_weight, preferred_element_type=jnp.float32)
    summed = lax.psum_scatter(partial, "inner", scatter_dimension=0, tiled=True)
    active = (jax.nn.silu(summed[:, :, 0]) * summed[:, :, 1]).astype(jnp.bfloat16)
    active = lax.all_gather(active, "inner", axis=0, tiled=True)
    outputs = jnp.einsum("sxf,xfd->xsd", active, down_weight, preferred_element_type=jnp.float32)
    outputs = outputs.astype(jnp.bfloat16).reshape(experts, owners, count // owners, -1)
    back = [outputs[:, t].reshape(experts * count // owners, -1) for t in range(owners)]
    return back, attention(held)


def body(
    queries,
    new_key_value,
    cached_key_value,
    parents,
    hidden,
    routes,
    gate_values,
    gate_up_weight,
    down_weight,
):
    owners, inner = lax.axis_size("expert"), lax.axis_size("inner")
    experts, _, depth, ff = gate_up_weight.shape
    rows, model = hidden.shape
    width = down_weight.shape[2]
    top = routes.shape[1]
    column = lax.axis_index("expert").astype(jnp.int32).reshape(1)
    level = lax.axis_index("inner").astype(jnp.int32).reshape(1)
    slots = experts * CAP * inner

    attention = functools.partial(attend, queries, new_key_value, cached_key_value, parents)

    slices = call(
        prepare_kernel,
        [level],
        [routes.T, gate_values.T, hidden],
        [jax.ShapeDtypeStruct((rows, depth + LANES), jnp.bfloat16)] * inner,
        "prepare",
    )
    slices = exchange(slices, "inner")
    packs = call(
        functools.partial(pack_kernel, top, experts, inner),
        [column, level],
        slices,
        [jax.ShapeDtypeStruct((slots, depth), jnp.bfloat16)] * owners,
        "pack",
    )
    packs = exchange(packs, "expert")
    held = call(
        select_kernel,
        [],
        packs,
        jax.ShapeDtypeStruct((experts, owners * CAP * inner, depth), jnp.bfloat16),
        "select",
        24,
    )
    even = ff % (inner * LANES) == 0
    back, attended = (experts_by_columns if even else experts_by_rows)(
        held, gate_up_weight, down_weight, owners, attention
    )
    back = exchange(back, "expert", back=True)
    pieces = call(
        functools.partial(combine_kernel, top, experts, inner),
        [column, level],
        [*slices, *back],
        [jax.ShapeDtypeStruct((rows, width), jnp.bfloat16)] * inner,
        "combine",
    )
    pieces = exchange(pieces, "inner", back=True)
    expert_out = call(
        assemble_kernel,
        [level],
        pieces,
        jax.ShapeDtypeStruct((rows, model), jnp.bfloat16),
        "assemble",
    )
    return attended, expert_out


def solution(mesh):
    rows = ("groups", "expert", "inner")
    return jax.shard_map(
        body,
        mesh=mesh,
        in_specs=(
            P(rows, None),
            P(rows, None),
            P(rows, None, None, None),
            P(rows, None),
            P(rows, None),
            P(rows, None),
            P(rows, None),
            P("expert", None, "inner", None),
            P("expert", None, "inner"),
        ),
        out_specs=(P(rows, None), P(rows, None)),
        check_vma=False,
    )
```

```python
import functools
import math

import jax
import jax.numpy as jnp
from jax import lax
from jax.experimental import pallas as pl
from jax.experimental.pallas import tpu as pltpu
from jax.sharding import PartitionSpec as P

QUERY_HEADS = 64
KEY_HEADS = 4
HEAD_SIZE = 128
CAP = 3
LANES = 128


def params(limit, *semantics):
    return pltpu.CompilerParams(
        dimension_semantics=semantics or None, vmem_limit_bytes=limit * 1024 * 1024
    )


def attend_kernel(beams, parents, q_ref, new_ref, *refs):
    cache_refs, out_ref = refs[:beams], refs[-1]
    group = QUERY_HEADS // KEY_HEADS
    scale = 1.0 / math.sqrt(HEAD_SIZE)
    width = KEY_HEADS * HEAD_SIZE
    for b in range(beams):
        q, cache_ref = q_ref[b], cache_refs[b]
        fresh = new_ref[b].astype(jnp.float32)
        scores, own = [], []
        for k in range(KEY_HEADS):
            qk = q[k * group:(k + 1) * group]
            keys = cache_ref[0, 0, :, k * HEAD_SIZE:(k + 1) * HEAD_SIZE]
            scores.append(
                lax.dot_general(
                    qk, keys, (((1,), (1,)), ((), ())), preferred_element_type=jnp.float32
                )
            )
            own.append(
                jnp.sum(qk.astype(jnp.float32) * fresh[k:k + 1], axis=-1, keepdims=True)
            )
        scores = jnp.concatenate(scores, axis=0) * scale
        own = jnp.concatenate(own, axis=0) * scale
        upper = jnp.maximum(jnp.max(scores, axis=-1, keepdims=True), own)
        expo = jnp.exp(scores - upper)
        own_expo = jnp.exp(own - upper)
        total = jnp.sum(expo, axis=-1, keepdims=True) + own_expo
        probs = (expo / total).astype(jnp.bfloat16)
        own_prob = (own_expo / total).astype(jnp.bfloat16).astype(jnp.float32)
        for k in range(KEY_HEADS):
            rows = slice(k * group, (k + 1) * group)
            values = cache_ref[0, 0, :, width + k * HEAD_SIZE:width + (k + 1) * HEAD_SIZE]
            result = jnp.dot(probs[rows], values, preferred_element_type=jnp.float32)
            result = result + own_prob[rows] * fresh[KEY_HEADS + k:KEY_HEADS + k + 1]
            out_ref[b, rows] = result.astype(out_ref.dtype)


def attend(queries, new_key_value, cached_key_value, parents, after):
    rows = queries.shape[0]
    _, beams, length, width = cached_key_value.shape
    step = 4

    def parent_of(b):
        return lambda r, p: ((r * step + b) // beams, p[r * step + b], 0, 0)

    out = pl.pallas_call(
        functools.partial(attend_kernel, step),
        grid_spec=pltpu.PrefetchScalarGridSpec(
            num_scalar_prefetch=1,
            grid=(rows // step,),
            in_specs=[
                pl.BlockSpec((step, QUERY_HEADS, HEAD_SIZE), lambda r, p: (r, 0, 0)),
                pl.BlockSpec((step, 2 * KEY_HEADS, HEAD_SIZE), lambda r, p: (r, 0, 0)),
            ]
            + [pl.BlockSpec((1, 1, length, width), parent_of(b)) for b in range(step)]
            + [pl.BlockSpec(memory_space=pl.ANY)],
            out_specs=pl.BlockSpec((step, QUERY_HEADS, HEAD_SIZE), lambda r, p: (r, 0, 0)),
        ),
        out_shape=jax.ShapeDtypeStruct((rows, QUERY_HEADS, HEAD_SIZE), jnp.bfloat16),
        compiler_params=params(40),
        cost_estimate=pl.CostEstimate(
            flops=4 * rows * QUERY_HEADS * HEAD_SIZE * length,
            bytes_accessed=2 * rows * length * width,
            transcendentals=rows * QUERY_HEADS * length,
        ),
        name="attend",
    )(
        parents.reshape(rows),
        queries.reshape(rows, QUERY_HEADS, HEAD_SIZE),
        new_key_value.reshape(rows, 2 * KEY_HEADS, HEAD_SIZE),
        *[cached_key_value] * step,
        after,
    )
    return out.reshape(rows, QUERY_HEADS * HEAD_SIZE)


def spread(values, lanes, first):
    top = values.shape[0]
    shape = (top, lanes)
    chosen = (
        lax.broadcasted_iota(jnp.int32, shape, 1)
        == lax.broadcasted_iota(jnp.int32, shape, 0) + first
    ).astype(jnp.float32)
    return lax.dot_general(
        values.astype(jnp.float32), chosen, (((0,), (0,)), ((), ())), preferred_element_type=jnp.float32
    )


def prepare_kernel(me, routes_ref, gates_ref, hidden_ref, *out_refs):
    chunks = len(out_refs)
    width = hidden_ref.shape[1] // chunks
    top = routes_ref.shape[0]
    notes = spread(routes_ref[...], LANES, 0) + spread(gates_ref[...], LANES, top)
    notes = notes.astype(jnp.bfloat16)
    for s in range(chunks):
        start = pl.multiple_of(lax.rem(me[0] + s, chunks) * width, width)
        out_refs[s][:, :width] = hidden_ref[:, pl.ds(start, width)]
        out_refs[s][:, width:] = notes


def turned_notes(notes, top):
    shape = (max(8, 2 * top), LANES)
    chosen = (
        lax.broadcasted_iota(jnp.int32, shape, 0) == lax.broadcasted_iota(jnp.int32, shape, 1)
    ).astype(jnp.bfloat16)
    turned = lax.dot_general(
        chosen, notes, (((1,), (1,)), ((), ())), preferred_element_type=jnp.float32
    )
    return turned[:top], turned[top:2 * top]


def placing(routes, owner, level, experts, sources):
    top, rows = routes.shape
    count = CAP * sources
    shape = (experts * count, rows)
    slot = lax.broadcasted_iota(jnp.int32, shape, 0)
    row = lax.broadcasted_iota(jnp.int32, shape, 1)
    each = rows // sources
    local = jnp.zeros(shape, jnp.int32)
    for x in range(1, experts):
        local = local + (slot >= x * count).astype(jnp.int32)
    within = slot - local * count
    rank, source = within // sources, within % sources
    expert = (owner * experts + local).astype(jnp.float32)
    member = jnp.zeros(shape, jnp.float32)
    for t in range(top):
        member = jnp.where(routes[t:t + 1] == expert, 1.0, member)
    origin = level - row // each
    origin = jnp.where(origin < 0, origin + sources, origin)
    member = jnp.where(origin == source, member, 0.0)
    one = lax.broadcasted_iota(jnp.int32, (rows, rows), 0)
    other = lax.broadcasted_iota(jnp.int32, (rows, rows), 1)
    before = (one < other).astype(jnp.float32)
    ranks = jnp.dot(member, before, preferred_element_type=jnp.float32)
    return jnp.where(ranks == rank.astype(jnp.float32), member, 0.0), expert


def pack_kernel(top, experts, sources, column, level, *refs):
    owners = len(refs) - sources
    held, out_refs = refs[:sources], refs[sources:]
    width = out_refs[0].shape[1]
    rows = jnp.concatenate([ref[:, :width] for ref in held], axis=0)
    notes = jnp.concatenate([ref[:, width:] for ref in held], axis=0)
    routes, _ = turned_notes(notes, top)
    for t in range(owners):
        place, _ = placing(routes, lax.rem(column[0] + t, owners), level[0], experts, sources)
        out_refs[t][...] = jnp.dot(
            place.astype(jnp.bfloat16), rows, preferred_element_type=jnp.float32
        ).astype(out_refs[t].dtype)


def combine_kernel(top, experts, sources, column, level, *refs):
    held, back_ref, out_ref = refs[:sources], refs[sources], refs[sources + 1]
    owners = back_ref.shape[0]
    _, each, width = out_ref.shape
    notes = jnp.concatenate([ref[:, width:] for ref in held], axis=0)
    routes, gates = turned_notes(notes, top)
    total = jnp.zeros((sources * each, width), jnp.float32)
    for t in range(owners):
        place, expert = placing(routes, t, level[0], experts, sources)
        weight = jnp.zeros_like(place)
        for k in range(top):
            weight = weight + jnp.where(routes[k:k + 1] == expert, gates[k:k + 1], 0.0)
        total = total + lax.dot_general(
            (weight * place).astype(jnp.bfloat16),
            back_ref[t],
            (((0,), (0,)), ((), ())),
            preferred_element_type=jnp.float32,
        )
    for s in range(sources):
        out_ref[lax.rem(level[0] + sources - s, sources)] = total[
            s * each:(s + 1) * each
        ].astype(out_ref.dtype)


def assemble_kernel(pieces_ref, out_ref):
    chunks, _, width = pieces_ref.shape
    for k in range(chunks):
        out_ref[:, k * width:(k + 1) * width] = pieces_ref[k]


def regroup(experts, owners, count):
    shape = (experts * owners * count, owners * experts * count)
    row = lax.broadcasted_iota(jnp.int32, shape, 0)
    other = lax.broadcasted_iota(jnp.int32, shape, 1)
    wanted = jnp.zeros(shape, jnp.int32) + row
    for x in range(experts):
        for t in range(owners):
            first = (x * owners + t) * count
            inside = (row >= first) & (row < first + count)
            wanted = jnp.where(inside, row - first + (t * experts + x) * count, wanted)
    return (other == wanted).astype(jnp.bfloat16)


def select_kernel(*refs):
    packs, out_ref = refs[:-1], refs[-1]
    experts, count, _ = out_ref.shape
    rows = jnp.concatenate([ref[...].astype(jnp.float32) for ref in packs], axis=0)
    moved = jnp.dot(
        regroup(experts, len(packs), count // len(packs)),
        rows.astype(jnp.bfloat16),
        preferred_element_type=jnp.float32,
    ).astype(out_ref.dtype)
    for x in range(experts):
        out_ref[x] = moved[x * count:(x + 1) * count]


def gate_up_kernel(chunk, rows_ref, weight_ref, out_ref, done_ref=None):
    if done_ref is not None:
        done_ref[...] = jnp.zeros_like(done_ref)
    ff = out_ref.shape[2] // 2
    columns = pl.ds(pl.multiple_of(chunk[0] * ff, ff), ff)
    for x in range(out_ref.shape[0]):
        for k in range(2):
            out_ref[x, :, k * ff:(k + 1) * ff] = jnp.dot(
                rows_ref[x], weight_ref[x, k, :, columns], preferred_element_type=jnp.float32
            ).astype(out_ref.dtype)


def gate_up(chunk, chunks, rows, weight, dtype, done=False):
    experts, count, depth = rows.shape
    ff = weight.shape[3] // chunks
    return call(
        gate_up_kernel,
        [chunk],
        [rows, weight],
        [jax.ShapeDtypeStruct((experts, count, 2 * ff), dtype)]
        + [jax.ShapeDtypeStruct((8, LANES), jnp.float32)] * done,
        "gate_up",
        24,
        cost=1,
    )


def activate_kernel(own_ref, *refs):
    other_refs, out_ref = refs[:-2], refs[-1]
    ff = out_ref.shape[2]
    for x in range(out_ref.shape[0]):
        total = own_ref[x]
        for ref in other_refs:
            total = total + ref[x].astype(jnp.float32)
        gate, up = total[:, :ff], total[:, ff:]
        out_ref[x] = (gate / (1.0 + jnp.exp(-gate)) * up).astype(out_ref.dtype)


def down_own_kernel(me, part_ref, weight_ref, sum_ref):
    ff = part_ref.shape[2]
    chunk = pl.ds(pl.multiple_of(me[0] * ff, ff), ff)
    for x in range(part_ref.shape[0]):
        sum_ref[x] = jnp.dot(part_ref[x], weight_ref[x, chunk], preferred_element_type=jnp.float32)


def down_rest_kernel(chunks, me, column, sum_ref, *refs):
    parts, weight_ref, out_ref = refs[:chunks - 1], refs[chunks - 1], refs[chunks]
    experts, count, width = sum_ref.shape
    ff = parts[0].shape[2]
    sums = []
    for x in range(experts):
        total = sum_ref[x]
        for s in range(1, chunks):
            chunk = lax.rem(me[0] + chunks - s, chunks)
            chunk = pl.ds(pl.multiple_of(chunk * ff, ff), ff)
            total = total + jnp.dot(
                parts[s - 1][x], weight_ref[x, chunk], preferred_element_type=jnp.float32
            )
        sums.append(total.astype(jnp.bfloat16))
    owners, rows, _ = out_ref.shape
    moved = lax.dot_general(
        regroup(experts, owners, count // owners),
        jnp.concatenate(sums, axis=0),
        (((0,), (0,)), ((), ())),
        preferred_element_type=jnp.float32,
    )
    for t in range(owners):
        out_ref[lax.rem(column[0] + owners - t, owners)] = moved[
            t * rows:(t + 1) * rows
        ].astype(out_ref.dtype)


def shifted(value, axis, steps):
    size = lax.axis_size(axis)
    return lax.ppermute(value, axis, [(i, (i + steps) % size) for i in range(size)])


def farthest_first(size):
    return sorted(range(1, size), key=lambda s: -min(s, size - s))


def exchange(values, axis):
    out = [values[0]] + [None] * (len(values) - 1)
    for s in farthest_first(len(values)):
        out[s] = shifted(values[s], axis, s)
    return out


def call(kernel, index, inputs, outputs, name, limit=16, after=(), cost=0):
    single = not isinstance(outputs, list)
    return pl.pallas_call(
        kernel,
        in_specs=[pl.BlockSpec(memory_space=pltpu.SMEM)] * len(index)
        + [pl.BlockSpec(memory_space=pltpu.VMEM)] * len(inputs)
        + [pl.BlockSpec(memory_space=pl.ANY)] * len(after),
        out_specs=pl.BlockSpec(memory_space=pltpu.VMEM)
        if single
        else [pl.BlockSpec(memory_space=pltpu.VMEM)] * len(outputs),
        out_shape=outputs,
        compiler_params=params(limit),
        cost_estimate=pl.CostEstimate(
            flops=cost * 10**9, bytes_accessed=cost * 3 * 10**6, transcendentals=0
        ),
        name=name,
    )(*index, *inputs, *after)


def experts_by_columns(held, gate_up_weight, down_weight, owners, attention):
    inner = lax.axis_size("inner")
    experts, count, _ = held.shape
    ff, width = down_weight.shape[1:]
    me = lax.axis_index("inner").astype(jnp.int32)
    level = me.reshape(1)
    others = []
    for s in farthest_first(inner):
        (part,) = gate_up(((me + s) % inner).reshape(1), inner, held, gate_up_weight, jnp.bfloat16)
        others.append(shifted(part, "inner", s))
    own, done = gate_up(level, inner, held, gate_up_weight, jnp.float32, True)
    attended = attention(done)
    active = call(
        activate_kernel,
        [],
        [own, *others],
        jax.ShapeDtypeStruct((experts, count, ff // inner), jnp.bfloat16),
        "activate",
        after=[attended],
    )
    parts = exchange([active] * inner, "inner")
    sums = call(
        down_own_kernel,
        [level],
        [parts[0], down_weight],
        jax.ShapeDtypeStruct((experts, count, width), jnp.float32),
        "down_own",
        24,
    )
    back = call(
        functools.partial(down_rest_kernel, inner),
        [level, lax.axis_index("expert").astype(jnp.int32).reshape(1)],
        [sums, *parts[1:], down_weight],
        jax.ShapeDtypeStruct((owners, experts * count // owners, width), jnp.bfloat16),
        "down_rest",
        24,
    )
    return back, attended


def experts_by_rows(held, gate_up_weight, down_weight, owners, attention):
    experts, count, _ = held.shape
    partial = jnp.einsum("xsd,xkdf->sxkf", held, gate_up_weight, preferred_element_type=jnp.float32)
    summed = lax.psum_scatter(partial, "inner", scatter_dimension=0, tiled=True)
    active = (jax.nn.silu(summed[:, :, 0]) * summed[:, :, 1]).astype(jnp.bfloat16)
    active = lax.all_gather(active, "inner", axis=0, tiled=True)
    outputs = jnp.einsum("sxf,xfd->xsd", active, down_weight, preferred_element_type=jnp.float32)
    outputs = outputs.astype(jnp.bfloat16).reshape(experts, owners, count // owners, -1)
    back = jnp.transpose(outputs, (1, 0, 2, 3)).reshape(owners, experts * count // owners, -1)
    origin = (lax.axis_index("expert") - jnp.arange(owners)) % owners
    return back[origin], attention(held)


def body(
    queries,
    new_key_value,
    cached_key_value,
    parents,
    hidden,
    routes,
    gate_values,
    gate_up_weight,
    down_weight,
):
    owners, inner = lax.axis_size("expert"), lax.axis_size("inner")
    experts, _, depth, ff = gate_up_weight.shape
    rows, model = hidden.shape
    width = down_weight.shape[2]
    top = routes.shape[1]
    column = lax.axis_index("expert").astype(jnp.int32).reshape(1)
    level = lax.axis_index("inner").astype(jnp.int32).reshape(1)
    slots = experts * CAP * inner

    attention = functools.partial(attend, queries, new_key_value, cached_key_value, parents)

    slices = call(
        prepare_kernel,
        [level],
        [routes.T, gate_values.T, hidden],
        [jax.ShapeDtypeStruct((rows, depth + LANES), jnp.bfloat16)] * inner,
        "prepare",
        cost=2,
    )
    slices = exchange(slices, "inner")
    packs = call(
        functools.partial(pack_kernel, top, experts, inner),
        [column, level],
        slices,
        [jax.ShapeDtypeStruct((slots, depth), jnp.bfloat16)] * owners,
        "pack",
        cost=3,
    )
    packs = exchange(packs, "expert")
    held = call(
        select_kernel,
        [],
        packs,
        jax.ShapeDtypeStruct((experts, owners * CAP * inner, depth), jnp.bfloat16),
        "select",
        24,
        cost=1,
    )
    even = ff % (inner * LANES) == 0
    back, attended = (experts_by_columns if even else experts_by_rows)(
        held, gate_up_weight, down_weight, owners, attention
    )
    back = lax.all_to_all(back, "expert", split_axis=0, concat_axis=0, tiled=True)
    pieces = call(
        functools.partial(combine_kernel, top, experts, inner),
        [column, level],
        [*slices, back],
        jax.ShapeDtypeStruct((inner, rows, width), jnp.bfloat16),
        "combine",
    )
    pieces = lax.all_to_all(pieces, "inner", split_axis=0, concat_axis=0, tiled=True)
    expert_out = call(
        assemble_kernel,
        [],
        [pieces],
        jax.ShapeDtypeStruct((rows, model), jnp.bfloat16),
        "assemble",
    )
    return attended, expert_out


def solution(mesh):
    rows = ("groups", "expert", "inner")
    return jax.shard_map(
        body,
        mesh=mesh,
        in_specs=(
            P(rows, None),
            P(rows, None),
            P(rows, None, None, None),
            P(rows, None),
            P(rows, None),
            P(rows, None),
            P(rows, None),
            P("expert", None, "inner", None),
            P("expert", None, "inner"),
        ),
        out_specs=(P(rows, None), P(rows, None)),
        check_vma=False,
    )
```

```python
import functools
import math

import jax
import jax.numpy as jnp
from jax import lax
from jax.experimental import pallas as pl
from jax.experimental.pallas import tpu as pltpu
from jax.sharding import PartitionSpec as P

QUERY_HEADS = 64
KEY_HEADS = 4
HEAD_SIZE = 128
CAP = 3
LANES = 128


def params(limit, *semantics):
    return pltpu.CompilerParams(
        dimension_semantics=semantics or None, vmem_limit_bytes=limit * 1024 * 1024
    )


def attend_kernel(beams, parents, q_ref, new_ref, *refs):
    cache_refs, out_ref = refs[:beams], refs[-1]
    group = QUERY_HEADS // KEY_HEADS
    scale = 1.0 / math.sqrt(HEAD_SIZE)
    width = KEY_HEADS * HEAD_SIZE
    for b in range(beams):
        q, cache_ref = q_ref[b], cache_refs[b]
        fresh = new_ref[b].astype(jnp.float32)
        scores, own = [], []
        for k in range(KEY_HEADS):
            qk = q[k * group:(k + 1) * group]
            keys = cache_ref[0, 0, :, k * HEAD_SIZE:(k + 1) * HEAD_SIZE]
            scores.append(
                lax.dot_general(
                    qk, keys, (((1,), (1,)), ((), ())), preferred_element_type=jnp.float32
                )
            )
            own.append(
                jnp.sum(qk.astype(jnp.float32) * fresh[k:k + 1], axis=-1, keepdims=True)
            )
        scores = jnp.concatenate(scores, axis=0) * scale
        own = jnp.concatenate(own, axis=0) * scale
        upper = jnp.maximum(jnp.max(scores, axis=-1, keepdims=True), own)
        expo = jnp.exp(scores - upper)
        own_expo = jnp.exp(own - upper)
        total = jnp.sum(expo, axis=-1, keepdims=True) + own_expo
        probs = (expo / total).astype(jnp.bfloat16)
        own_prob = (own_expo / total).astype(jnp.bfloat16).astype(jnp.float32)
        for k in range(KEY_HEADS):
            rows = slice(k * group, (k + 1) * group)
            values = cache_ref[0, 0, :, width + k * HEAD_SIZE:width + (k + 1) * HEAD_SIZE]
            result = jnp.dot(probs[rows], values, preferred_element_type=jnp.float32)
            result = result + own_prob[rows] * fresh[KEY_HEADS + k:KEY_HEADS + k + 1]
            out_ref[b, rows] = result.astype(out_ref.dtype)


def attend(queries, new_key_value, cached_key_value, parents, after, part, parts):
    rows = queries.shape[0] // parts
    first = part * rows
    _, beams, length, width = cached_key_value.shape
    step = 4

    def parent_of(b):
        return lambda r, p: ((first + r * step + b) // beams, p[first + r * step + b], 0, 0)

    out = pl.pallas_call(
        functools.partial(attend_kernel, step),
        grid_spec=pltpu.PrefetchScalarGridSpec(
            num_scalar_prefetch=1,
            grid=(rows // step,),
            in_specs=[
                pl.BlockSpec(
                    (step, QUERY_HEADS, HEAD_SIZE), lambda r, p: (first // step + r, 0, 0)
                ),
                pl.BlockSpec(
                    (step, 2 * KEY_HEADS, HEAD_SIZE), lambda r, p: (first // step + r, 0, 0)
                ),
            ]
            + [pl.BlockSpec((1, 1, length, width), parent_of(b)) for b in range(step)]
            + [pl.BlockSpec(memory_space=pl.ANY)],
            out_specs=pl.BlockSpec((step, QUERY_HEADS, HEAD_SIZE), lambda r, p: (r, 0, 0)),
        ),
        out_shape=jax.ShapeDtypeStruct((rows, QUERY_HEADS, HEAD_SIZE), jnp.bfloat16),
        compiler_params=params(40),
        cost_estimate=pl.CostEstimate(
            flops=4 * rows * QUERY_HEADS * HEAD_SIZE * length,
            bytes_accessed=2 * rows * length * width,
            transcendentals=rows * QUERY_HEADS * length,
        ),
        name="attend",
    )(
        parents.reshape(-1),
        queries.reshape(-1, QUERY_HEADS, HEAD_SIZE),
        new_key_value.reshape(-1, 2 * KEY_HEADS, HEAD_SIZE),
        *[cached_key_value] * step,
        after,
    )
    return out


def spread(values, lanes, first):
    top = values.shape[0]
    shape = (top, lanes)
    chosen = (
        lax.broadcasted_iota(jnp.int32, shape, 1)
        == lax.broadcasted_iota(jnp.int32, shape, 0) + first
    ).astype(jnp.float32)
    return lax.dot_general(
        values.astype(jnp.float32), chosen, (((0,), (0,)), ((), ())), preferred_element_type=jnp.float32
    )


def prepare_kernel(me, routes_ref, gates_ref, hidden_ref, *out_refs):
    _, _, padded = out_refs[0].shape
    width = padded - LANES
    top = routes_ref.shape[0]
    notes = spread(routes_ref[...], LANES, 0) + spread(gates_ref[...], LANES, top)
    notes = notes.astype(jnp.bfloat16)
    for s in range(hidden_ref.shape[1] // width):
        start = pl.multiple_of((me[0] ^ s) * width, width)
        out_refs[s % 2][s // 2, :, :width] = hidden_ref[:, pl.ds(start, width)]
        out_refs[s % 2][s // 2, :, width:] = notes


def turned_notes(notes, top):
    shape = (max(8, 2 * top), LANES)
    chosen = (
        lax.broadcasted_iota(jnp.int32, shape, 0) == lax.broadcasted_iota(jnp.int32, shape, 1)
    ).astype(jnp.bfloat16)
    turned = lax.dot_general(
        chosen, notes, (((1,), (1,)), ((), ())), preferred_element_type=jnp.float32
    )
    return turned[:top], turned[top:2 * top]


def placing(routes, owner, level, experts, sources):
    top, rows = routes.shape
    count = CAP * sources
    shape = (experts * count, rows)
    slot = lax.broadcasted_iota(jnp.int32, shape, 0)
    row = lax.broadcasted_iota(jnp.int32, shape, 1)
    each = rows // sources
    local = jnp.zeros(shape, jnp.int32)
    for x in range(1, experts):
        local = local + (slot >= x * count).astype(jnp.int32)
    within = slot - local * count
    rank, source = within // sources, within % sources
    expert = (owner * experts + local).astype(jnp.float32)
    member = jnp.zeros(shape, jnp.float32)
    for t in range(top):
        member = jnp.where(routes[t:t + 1] == expert, 1.0, member)
    origin = level ^ (row // each)
    member = jnp.where(origin == source, member, 0.0)
    one = lax.broadcasted_iota(jnp.int32, (rows, rows), 0)
    other = lax.broadcasted_iota(jnp.int32, (rows, rows), 1)
    before = (one < other).astype(jnp.float32)
    ranks = jnp.dot(member, before, preferred_element_type=jnp.float32)
    return jnp.where(ranks == rank.astype(jnp.float32), member, 0.0), expert


def pack_kernel(top, experts, places, column, level, *refs):
    held, out_refs = refs[:-2], refs[-2:]
    half, _, width = out_refs[0].shape
    rows = jnp.concatenate([held[a][i, :, :width] for a, i in places], axis=0)
    notes = jnp.concatenate([held[a][i, :, width:] for a, i in places], axis=0)
    routes, _ = turned_notes(notes, top)
    for t in range(2 * half):
        place, _ = placing(routes, column[0] ^ t, level[0], experts, len(places))
        out_refs[t % 2][t // 2] = jnp.dot(
            place.astype(jnp.bfloat16), rows, preferred_element_type=jnp.float32
        ).astype(out_refs[t % 2].dtype)


def combine_kernel(top, experts, places, back_places, column, level, *refs):
    count = 1 + max(a for a, _ in places)
    held, back, out_refs = refs[:count], refs[count:-2], refs[-2:]
    _, each, width = out_refs[0].shape
    notes = jnp.concatenate([held[a][i, :, width:] for a, i in places], axis=0)
    routes, gates = turned_notes(notes, top)
    total = jnp.zeros((len(places) * each, width), jnp.float32)
    for t, (a, i) in enumerate(back_places):
        place, expert = placing(routes, column[0] ^ t, level[0], experts, len(places))
        weight = jnp.zeros_like(place)
        for k in range(top):
            weight = weight + jnp.where(routes[k:k + 1] == expert, gates[k:k + 1], 0.0)
        total = total + lax.dot_general(
            (weight * place).astype(jnp.bfloat16),
            back[a][i],
            (((0,), (0,)), ((), ())),
            preferred_element_type=jnp.float32,
        )
    for s in range(len(places)):
        out_refs[s % 2][s // 2] = total[s * each:(s + 1) * each].astype(out_refs[s % 2].dtype)


def assemble_kernel(places, me, *refs):
    pieces, out_ref = refs[:-1], refs[-1]
    width = pieces[0].shape[2]
    for s, (a, i) in enumerate(places):
        start = pl.multiple_of((me[0] ^ s) * width, width)
        out_ref[:, pl.ds(start, width)] = pieces[a][i]


def regroup(experts, owners, count):
    shape = (experts * owners * count, owners * experts * count)
    row = lax.broadcasted_iota(jnp.int32, shape, 0)
    other = lax.broadcasted_iota(jnp.int32, shape, 1)
    wanted = jnp.zeros(shape, jnp.int32) + row
    for x in range(experts):
        for t in range(owners):
            first = (x * owners + t) * count
            inside = (row >= first) & (row < first + count)
            wanted = jnp.where(inside, row - first + (t * experts + x) * count, wanted)
    return (other == wanted).astype(jnp.bfloat16)


def select_kernel(places, *refs):
    packs, out_ref = refs[:-1], refs[-1]
    experts, count, _ = out_ref.shape
    rows = jnp.concatenate([packs[a][i].astype(jnp.float32) for a, i in places], axis=0)
    moved = jnp.dot(
        regroup(experts, len(places), count // len(places)),
        rows.astype(jnp.bfloat16),
        preferred_element_type=jnp.float32,
    ).astype(out_ref.dtype)
    for x in range(experts):
        out_ref[x] = moved[x * count:(x + 1) * count]


def gate_up_kernel(chunk, rows_ref, weight_ref, out_ref, done_ref=None):
    if done_ref is not None:
        done_ref[...] = jnp.zeros_like(done_ref)
    ff = out_ref.shape[2] // 2
    columns = pl.ds(pl.multiple_of(chunk[0] * ff, ff), ff)
    for x in range(out_ref.shape[0]):
        for k in range(2):
            out_ref[x, :, k * ff:(k + 1) * ff] = jnp.dot(
                rows_ref[x], weight_ref[x, k, :, columns], preferred_element_type=jnp.float32
            ).astype(out_ref.dtype)


def gate_up(chunk, chunks, rows, weight, dtype, done=False):
    experts, count, depth = rows.shape
    ff = weight.shape[3] // chunks
    return call(
        gate_up_kernel,
        [chunk],
        [rows, weight],
        [jax.ShapeDtypeStruct((experts, count, 2 * ff), dtype)]
        + [jax.ShapeDtypeStruct((8, LANES), jnp.float32)] * done,
        "gate_up",
        24,
        cost=1,
    )


def activate_kernel(own_ref, *refs):
    other_refs, out_ref = refs[:-2], refs[-1]
    ff = out_ref.shape[2]
    for x in range(out_ref.shape[0]):
        total = own_ref[x]
        for ref in other_refs:
            total = total + ref[x].astype(jnp.float32)
        gate, up = total[:, :ff], total[:, ff:]
        out_ref[x] = (gate / (1.0 + jnp.exp(-gate)) * up).astype(out_ref.dtype)


def down_own_kernel(me, part_ref, weight_ref, sum_ref):
    ff = part_ref.shape[2]
    chunk = pl.ds(pl.multiple_of(me[0] * ff, ff), ff)
    for x in range(part_ref.shape[0]):
        sum_ref[x] = jnp.dot(part_ref[x], weight_ref[x, chunk], preferred_element_type=jnp.float32)


def down_rest_kernel(chunks, me, sum_ref, *refs):
    parts, weight_ref, out_refs = refs[:chunks - 1], refs[chunks - 1], refs[chunks + 1:]
    experts, count, width = sum_ref.shape
    ff = parts[0].shape[2]
    sums = []
    for x in range(experts):
        total = sum_ref[x]
        for s in range(1, chunks):
            chunk = lax.rem(me[0] + chunks - s, chunks)
            chunk = pl.ds(pl.multiple_of(chunk * ff, ff), ff)
            total = total + jnp.dot(
                parts[s - 1][x], weight_ref[x, chunk], preferred_element_type=jnp.float32
            )
        sums.append(total.astype(jnp.bfloat16))
    half, rows, _ = out_refs[0].shape
    owners = 2 * half
    moved = lax.dot_general(
        regroup(experts, owners, count // owners),
        jnp.concatenate(sums, axis=0),
        (((0,), (0,)), ((), ())),
        preferred_element_type=jnp.float32,
    )
    for t in range(owners):
        out_refs[t % 2][t // 2] = moved[t * rows:(t + 1) * rows].astype(out_refs[t % 2].dtype)


def shifted(value, axis, steps):
    size = lax.axis_size(axis)
    return lax.ppermute(value, axis, [(i, (i + steps) % size) for i in range(size)])


def farthest_first(size):
    return sorted(range(1, size), key=lambda s: -min(s, size - s))


def exchange(values, axis):
    out = [values[0]] + [None] * (len(values) - 1)
    for s in farthest_first(len(values)):
        out[s] = shifted(values[s], axis, s)
    return out


def take_kernel(places, *refs):
    for n, (a, i) in enumerate(places):
        refs[-1][n] = refs[a][i]


def trade(kept, sent, axis):
    size = lax.axis_size(axis)
    arrays = [kept]
    where = {(r, 0): (0, r // 2) for r in range(0, size, 2)}
    bit = 1
    while bit < size:
        moving = sorted(key for key in where if key[0] & bit)
        if bit > 1:
            sent = call(
                functools.partial(take_kernel, [where.pop(key) for key in moving]),
                [],
                arrays,
                jax.ShapeDtypeStruct((len(moving),) + kept.shape[1:], kept.dtype),
                "take",
            )
        else:
            moving = [(r, 0) for r in range(1, size, 2)]
        got = lax.ppermute(sent, axis, [(i, i ^ bit) for i in range(size)])
        for n, (r, s) in enumerate(moving):
            where[r ^ bit, s | bit] = (len(arrays), n)
        arrays.append(got)
        bit *= 2
    return arrays, [where[0, s] for s in range(size)]


def call(kernel, index, inputs, outputs, name, limit=16, after=(), cost=0):
    single = not isinstance(outputs, list)
    return pl.pallas_call(
        kernel,
        in_specs=[pl.BlockSpec(memory_space=pltpu.SMEM)] * len(index)
        + [pl.BlockSpec(memory_space=pltpu.VMEM)] * len(inputs)
        + [pl.BlockSpec(memory_space=pl.ANY)] * len(after),
        out_specs=pl.BlockSpec(memory_space=pltpu.VMEM)
        if single
        else [pl.BlockSpec(memory_space=pltpu.VMEM)] * len(outputs),
        out_shape=outputs,
        compiler_params=params(limit),
        cost_estimate=pl.CostEstimate(
            flops=cost * 10**9, bytes_accessed=cost * 3 * 10**6, transcendentals=0
        ),
        name=name,
    )(*index, *inputs, *after)


def experts_by_columns(held, gate_up_weight, down_weight, owners, attention):
    inner = lax.axis_size("inner")
    experts, count, _ = held.shape
    ff, width = down_weight.shape[1:]
    me = lax.axis_index("inner").astype(jnp.int32)
    level = me.reshape(1)
    others = []
    for s in farthest_first(inner):
        (part,) = gate_up(((me + s) % inner).reshape(1), inner, held, gate_up_weight, jnp.bfloat16)
        others.append(shifted(part, "inner", s))
    own, done = gate_up(level, inner, held, gate_up_weight, jnp.float32, True)
    first = attention(done, 0, 2)
    active = call(
        activate_kernel,
        [],
        [own, *others],
        jax.ShapeDtypeStruct((experts, count, ff // inner), jnp.bfloat16),
        "activate",
        after=[first],
    )
    parts = exchange([active] * inner, "inner")
    sums = call(
        down_own_kernel,
        [level],
        [parts[0], down_weight],
        jax.ShapeDtypeStruct((experts, count, width), jnp.float32),
        "down_own",
        24,
    )
    second = attention(sums, 1, 2)
    back = call(
        functools.partial(down_rest_kernel, inner),
        [level],
        [sums, *parts[1:], down_weight],
        [jax.ShapeDtypeStruct((owners // 2, experts * count // owners, width), jnp.bfloat16)] * 2,
        "down_rest",
        24,
        after=[second],
    )
    return back, jnp.concatenate([first, second], axis=0)


def experts_by_rows(held, gate_up_weight, down_weight, owners, attention):
    experts, count, _ = held.shape
    partial = jnp.einsum("xsd,xkdf->sxkf", held, gate_up_weight, preferred_element_type=jnp.float32)
    summed = lax.psum_scatter(partial, "inner", scatter_dimension=0, tiled=True)
    active = (jax.nn.silu(summed[:, :, 0]) * summed[:, :, 1]).astype(jnp.bfloat16)
    active = lax.all_gather(active, "inner", axis=0, tiled=True)
    outputs = jnp.einsum("sxf,xfd->xsd", active, down_weight, preferred_element_type=jnp.float32)
    outputs = outputs.astype(jnp.bfloat16).reshape(experts, owners, count // owners, -1)
    back = jnp.transpose(outputs, (1, 0, 2, 3)).reshape(owners, experts * count // owners, -1)
    return [back[0::2], back[1::2]], attention(held, 0, 1)


def body(
    queries,
    new_key_value,
    cached_key_value,
    parents,
    hidden,
    routes,
    gate_values,
    gate_up_weight,
    down_weight,
):
    owners, inner = lax.axis_size("expert"), lax.axis_size("inner")
    experts, _, depth, ff = gate_up_weight.shape
    rows, model = hidden.shape
    width = down_weight.shape[2]
    top = routes.shape[1]
    column = lax.axis_index("expert").astype(jnp.int32).reshape(1)
    level = lax.axis_index("inner").astype(jnp.int32).reshape(1)
    slots = experts * CAP * inner

    def attention(after, part, parts):
        return attend(queries, new_key_value, cached_key_value, parents, after, part, parts)

    kept, sent = call(
        prepare_kernel,
        [level],
        [routes.T, gate_values.T, hidden],
        [jax.ShapeDtypeStruct((inner // 2, rows, depth + LANES), jnp.bfloat16)] * 2,
        "prepare",
        cost=10,
    )
    slices, places = trade(kept, sent, "inner")
    kept, sent = call(
        functools.partial(pack_kernel, top, experts, places),
        [column, level],
        slices,
        [jax.ShapeDtypeStruct((owners // 2, slots, depth), jnp.bfloat16)] * 2,
        "pack",
        cost=20,
    )
    packs, pack_places = trade(kept, sent, "expert")
    held = call(
        functools.partial(select_kernel, pack_places),
        [],
        packs,
        jax.ShapeDtypeStruct((experts, owners * CAP * inner, depth), jnp.bfloat16),
        "select",
        24,
        cost=10,
    )
    even = ff % (inner * LANES) == 0
    (kept, sent), attended = (experts_by_columns if even else experts_by_rows)(
        held, gate_up_weight, down_weight, owners, attention
    )
    back, back_places = trade(kept, sent, "expert")
    kept, sent = call(
        functools.partial(combine_kernel, top, experts, places, back_places),
        [column, level],
        [*slices, *back],
        [jax.ShapeDtypeStruct((inner // 2, rows, width), jnp.bfloat16)] * 2,
        "combine",
    )
    pieces, piece_places = trade(kept, sent, "inner")
    expert_out = call(
        functools.partial(assemble_kernel, piece_places),
        [level],
        pieces,
        jax.ShapeDtypeStruct((rows, model), jnp.bfloat16),
        "assemble",
    )
    return attended.reshape(rows, QUERY_HEADS * HEAD_SIZE), expert_out


def solution(mesh):
    rows = ("groups", "expert", "inner")
    return jax.shard_map(
        body,
        mesh=mesh,
        in_specs=(
            P(rows, None),
            P(rows, None),
            P(rows, None, None, None),
            P(rows, None),
            P(rows, None),
            P(rows, None),
            P(rows, None),
            P("expert", None, "inner", None),
            P("expert", None, "inner"),
        ),
        out_specs=(P(rows, None), P(rows, None)),
        check_vma=False,
    )
```

```python
import functools
import math

import jax
import jax.numpy as jnp
from jax import lax
from jax.experimental import pallas as pl
from jax.experimental.pallas import tpu as pltpu
from jax.sharding import PartitionSpec as P

QUERY_HEADS = 64
KEY_HEADS = 4
HEAD_SIZE = 128
CAP = 3
LANES = 128


def params(limit, *semantics):
    return pltpu.CompilerParams(
        dimension_semantics=semantics or None, vmem_limit_bytes=limit * 1024 * 1024
    )


def attend_kernel(beams, parents, q_ref, new_ref, *refs):
    cache_refs, out_ref = refs[:beams], refs[-1]
    group = QUERY_HEADS // KEY_HEADS
    scale = 1.0 / math.sqrt(HEAD_SIZE)
    width = KEY_HEADS * HEAD_SIZE
    for b in range(beams):
        q, cache_ref = q_ref[b], cache_refs[b]
        fresh = new_ref[b].astype(jnp.float32)
        scores, own = [], []
        for k in range(KEY_HEADS):
            qk = q[k * group:(k + 1) * group]
            keys = cache_ref[0, 0, :, k * HEAD_SIZE:(k + 1) * HEAD_SIZE]
            scores.append(
                lax.dot_general(
                    qk, keys, (((1,), (1,)), ((), ())), preferred_element_type=jnp.float32
                )
            )
            own.append(
                jnp.sum(qk.astype(jnp.float32) * fresh[k:k + 1], axis=-1, keepdims=True)
            )
        scores = jnp.concatenate(scores, axis=0) * scale
        own = jnp.concatenate(own, axis=0) * scale
        upper = jnp.maximum(jnp.max(scores, axis=-1, keepdims=True), own)
        expo = jnp.exp(scores - upper)
        own_expo = jnp.exp(own - upper)
        total = jnp.sum(expo, axis=-1, keepdims=True) + own_expo
        probs = (expo / total).astype(jnp.bfloat16)
        own_prob = (own_expo / total).astype(jnp.bfloat16).astype(jnp.float32)
        for k in range(KEY_HEADS):
            rows = slice(k * group, (k + 1) * group)
            values = cache_ref[0, 0, :, width + k * HEAD_SIZE:width + (k + 1) * HEAD_SIZE]
            result = jnp.dot(probs[rows], values, preferred_element_type=jnp.float32)
            result = result + own_prob[rows] * fresh[KEY_HEADS + k:KEY_HEADS + k + 1]
            out_ref[b, rows] = result.astype(out_ref.dtype)


def attend(queries, new_key_value, cached_key_value, parents, after, part, parts):
    rows = queries.shape[0] // parts
    first = part * rows
    _, beams, length, width = cached_key_value.shape
    step = 4

    def parent_of(b):
        return lambda r, p: ((first + r * step + b) // beams, p[first + r * step + b], 0, 0)

    out = pl.pallas_call(
        functools.partial(attend_kernel, step),
        grid_spec=pltpu.PrefetchScalarGridSpec(
            num_scalar_prefetch=1,
            grid=(rows // step,),
            in_specs=[
                pl.BlockSpec(
                    (step, QUERY_HEADS, HEAD_SIZE), lambda r, p: (first // step + r, 0, 0)
                ),
                pl.BlockSpec(
                    (step, 2 * KEY_HEADS, HEAD_SIZE), lambda r, p: (first // step + r, 0, 0)
                ),
            ]
            + [pl.BlockSpec((1, 1, length, width), parent_of(b)) for b in range(step)]
            + [pl.BlockSpec(memory_space=pl.ANY)],
            out_specs=pl.BlockSpec((step, QUERY_HEADS, HEAD_SIZE), lambda r, p: (r, 0, 0)),
        ),
        out_shape=jax.ShapeDtypeStruct((rows, QUERY_HEADS, HEAD_SIZE), jnp.bfloat16),
        compiler_params=params(40),
        cost_estimate=pl.CostEstimate(
            flops=4 * rows * QUERY_HEADS * HEAD_SIZE * length,
            bytes_accessed=2 * rows * length * width,
            transcendentals=rows * QUERY_HEADS * length,
        ),
        name="attend",
    )(
        parents.reshape(-1),
        queries.reshape(-1, QUERY_HEADS, HEAD_SIZE),
        new_key_value.reshape(-1, 2 * KEY_HEADS, HEAD_SIZE),
        *[cached_key_value] * step,
        after,
    )
    return out


def spread(values, lanes, first):
    top = values.shape[0]
    shape = (top, lanes)
    chosen = (
        lax.broadcasted_iota(jnp.int32, shape, 1)
        == lax.broadcasted_iota(jnp.int32, shape, 0) + first
    ).astype(jnp.float32)
    return lax.dot_general(
        values.astype(jnp.float32), chosen, (((0,), (0,)), ((), ())), preferred_element_type=jnp.float32
    )


def prepare_kernel(me, routes_ref, gates_ref, hidden_ref, *out_refs):
    width = hidden_ref.shape[1] // len(out_refs)
    top = routes_ref.shape[0]
    notes = spread(routes_ref[...], LANES, 0) + spread(gates_ref[...], LANES, top)
    notes = notes.astype(jnp.bfloat16)
    for s, out_ref in enumerate(out_refs):
        start = pl.multiple_of((me[0] ^ s) * width, width)
        out_ref[:, :width] = hidden_ref[:, pl.ds(start, width)]
        out_ref[:, width:] = notes


def turned_notes(notes, top):
    shape = (max(8, 2 * top), LANES)
    chosen = (
        lax.broadcasted_iota(jnp.int32, shape, 0) == lax.broadcasted_iota(jnp.int32, shape, 1)
    ).astype(jnp.bfloat16)
    turned = lax.dot_general(
        chosen, notes, (((1,), (1,)), ((), ())), preferred_element_type=jnp.float32
    )
    return turned[:top], turned[top:2 * top]


def placing(routes, owner, level, experts, sources):
    top, rows = routes.shape
    count = CAP * sources
    shape = (experts * count, rows)
    slot = lax.broadcasted_iota(jnp.int32, shape, 0)
    row = lax.broadcasted_iota(jnp.int32, shape, 1)
    each = rows // sources
    local = jnp.zeros(shape, jnp.int32)
    for x in range(1, experts):
        local = local + (slot >= x * count).astype(jnp.int32)
    within = slot - local * count
    rank, source = within // sources, within % sources
    expert = (owner * experts + local).astype(jnp.float32)
    member = jnp.zeros(shape, jnp.float32)
    for t in range(top):
        member = jnp.where(routes[t:t + 1] == expert, 1.0, member)
    origin = level ^ (row // each)
    member = jnp.where(origin == source, member, 0.0)
    one = lax.broadcasted_iota(jnp.int32, (rows, rows), 0)
    other = lax.broadcasted_iota(jnp.int32, (rows, rows), 1)
    before = (one < other).astype(jnp.float32)
    ranks = jnp.dot(member, before, preferred_element_type=jnp.float32)
    return jnp.where(ranks == rank.astype(jnp.float32), member, 0.0), expert


def pack_kernel(top, experts, sources, column, level, *refs):
    held, out_refs = refs[:sources], refs[sources:]
    width = out_refs[0].shape[1]
    rows = jnp.concatenate([ref[:, :width] for ref in held], axis=0)
    notes = jnp.concatenate([ref[:, width:] for ref in held], axis=0)
    routes, _ = turned_notes(notes, top)
    for t, out_ref in enumerate(out_refs):
        place, _ = placing(routes, column[0] ^ t, level[0], experts, sources)
        out_ref[...] = jnp.dot(
            place.astype(jnp.bfloat16), rows, preferred_element_type=jnp.float32
        ).astype(out_ref.dtype)


def weigh_kernel(top, experts, column, level, *refs):
    held, out_ref = refs[:-1], refs[-1]
    notes = jnp.concatenate([ref[:, -LANES:] for ref in held], axis=0)
    routes, gates = turned_notes(notes, top)
    for t in range(out_ref.shape[0]):
        place, expert = placing(routes, column[0] ^ t, level[0], experts, len(held))
        weight = jnp.zeros_like(place)
        for k in range(top):
            weight = weight + jnp.where(routes[k:k + 1] == expert, gates[k:k + 1], 0.0)
        out_ref[t] = (weight * place).astype(out_ref.dtype)


def combine_kernel(weight_ref, *refs):
    owners = weight_ref.shape[0]
    back, out_refs = refs[:owners], refs[owners:]
    each = out_refs[0].shape[0]
    total = 0.0
    for t in range(owners):
        total = total + lax.dot_general(
            weight_ref[t],
            back[t][...],
            (((0,), (0,)), ((), ())),
            preferred_element_type=jnp.float32,
        )
    for s, out_ref in enumerate(out_refs):
        out_ref[...] = total[s * each:(s + 1) * each].astype(out_ref.dtype)


def assemble_kernel(me, *refs):
    pieces, out_ref = refs[:-1], refs[-1]
    width = pieces[0].shape[1]
    for s, piece in enumerate(pieces):
        start = pl.multiple_of((me[0] ^ s) * width, width)
        out_ref[:, pl.ds(start, width)] = piece[...]


def regroup(experts, owners, count):
    shape = (experts * owners * count, owners * experts * count)
    row = lax.broadcasted_iota(jnp.int32, shape, 0)
    other = lax.broadcasted_iota(jnp.int32, shape, 1)
    wanted = jnp.zeros(shape, jnp.int32) + row
    for x in range(experts):
        for t in range(owners):
            first = (x * owners + t) * count
            inside = (row >= first) & (row < first + count)
            wanted = jnp.where(inside, row - first + (t * experts + x) * count, wanted)
    return (other == wanted).astype(jnp.bfloat16)


def select_kernel(*refs):
    packs, out_ref = refs[:-1], refs[-1]
    experts, count, _ = out_ref.shape
    rows = jnp.concatenate([ref[...].astype(jnp.float32) for ref in packs], axis=0)
    moved = jnp.dot(
        regroup(experts, len(packs), count // len(packs)),
        rows.astype(jnp.bfloat16),
        preferred_element_type=jnp.float32,
    ).astype(out_ref.dtype)
    for x in range(experts):
        out_ref[x] = moved[x * count:(x + 1) * count]


def gate_up_kernel(pieces, afters, chunk, rows_ref, weight_hbm, *refs):
    refs = refs[afters:]
    out_ref, held, sems = refs[0], refs[-2], refs[-1]
    experts, _, depth, ff = held.shape
    columns = pl.ds(pl.multiple_of(chunk[0] * ff, ff), ff)
    step = depth // pieces
    copies = {}
    for x in range(experts):
        for k in range(2):
            for n in range(pieces):
                part = pl.ds(n * step, step)
                copies[x, k, n] = pltpu.make_async_copy(
                    weight_hbm.at[x, k, part, columns],
                    held.at[x, k, part],
                    sems.at[(x * 2 + k) * pieces + n],
                )
                copies[x, k, n].start()
    if len(refs) > 3:
        refs[1][...] = jnp.zeros_like(refs[1])
    for x in range(experts):
        for k in range(2):
            total = 0.0
            for n in range(pieces):
                part = slice(n * step, (n + 1) * step)
                copies[x, k, n].wait()
                total = total + jnp.dot(
                    rows_ref[x, :, part], held[x, k, part], preferred_element_type=jnp.float32
                )
            out_ref[x, :, k * ff:(k + 1) * ff] = total.astype(out_ref.dtype)


def gate_up(chunk, chunks, rows, weight, dtype, done=False, after=()):
    experts, count, depth = rows.shape
    ff = weight.shape[3] // chunks
    pieces = 2
    return pl.pallas_call(
        functools.partial(gate_up_kernel, pieces, len(after)),
        in_specs=[
            pl.BlockSpec(memory_space=pltpu.SMEM),
            pl.BlockSpec(memory_space=pltpu.VMEM),
            pl.BlockSpec(memory_space=pl.ANY),
        ]
        + [pl.BlockSpec(memory_space=pl.ANY)] * len(after),
        out_specs=[pl.BlockSpec(memory_space=pltpu.VMEM)] * (1 + done),
        out_shape=[jax.ShapeDtypeStruct((experts, count, 2 * ff), dtype)]
        + [jax.ShapeDtypeStruct((8, LANES), jnp.float32)] * done,
        scratch_shapes=[
            pltpu.VMEM((experts, 2, depth, ff), weight.dtype),
            pltpu.SemaphoreType.DMA((experts * 2 * pieces,)),
        ],
        compiler_params=params(52),
        cost_estimate=pl.CostEstimate(
            flops=4 * experts * count * depth * ff,
            bytes_accessed=4 * experts * depth * ff,
            transcendentals=0,
        ),
        name="gate_up",
    )(chunk, rows, weight, *after)


def activate_kernel(own_ref, *refs):
    other_refs, out_ref = refs[:-2], refs[-1]
    ff = out_ref.shape[2]
    for x in range(out_ref.shape[0]):
        total = own_ref[x]
        for ref in other_refs:
            total = total + ref[x].astype(jnp.float32)
        gate, up = total[:, :ff], total[:, ff:]
        out_ref[x] = (gate / (1.0 + jnp.exp(-gate)) * up).astype(out_ref.dtype)


def down_product(part_ref, weight_ref, x, chunk):
    ff = part_ref.shape[2]
    rows = pl.ds(pl.multiple_of(chunk * ff, ff), ff)
    return jnp.dot(part_ref[x], weight_ref[x, rows], preferred_element_type=jnp.float32)


def down_first_kernel(me, part_ref, weight_ref, sum_ref):
    for x in range(part_ref.shape[0]):
        sum_ref[x] = down_product(part_ref, weight_ref, x, me[0])


def down_more_kernel(index, me, before_ref, part_ref, weight_ref, sum_ref):
    for x in range(part_ref.shape[0]):
        sum_ref[x] = before_ref[x] + down_product(part_ref, weight_ref, x, me[0] ^ index)


def down_rest_kernel(indices, me, sum_ref, *refs):
    count = len(indices)
    parts, weight_ref, out_refs = refs[:count], refs[count], refs[count + 2:]
    experts, slots, _ = sum_ref.shape
    sums = []
    for x in range(experts):
        total = sum_ref[x]
        for part_ref, index in zip(parts, indices):
            total = total + down_product(part_ref, weight_ref, x, me[0] ^ index)
        sums.append(total.astype(jnp.bfloat16))
    owners = len(out_refs)
    rows = experts * slots // owners
    moved = lax.dot_general(
        regroup(experts, owners, slots // owners),
        jnp.concatenate(sums, axis=0),
        (((0,), (0,)), ((), ())),
        preferred_element_type=jnp.float32,
    )
    for t, out_ref in enumerate(out_refs):
        out_ref[...] = moved[t * rows:(t + 1) * rows].astype(out_ref.dtype)


def traded(value, axis, index):
    return lax.ppermute(value, axis, [(i, i ^ index) for i in range(lax.axis_size(axis))])


def trade(values, axis):
    out = [values[0]] + [None] * (len(values) - 1)
    for s in reversed(range(1, len(values))):
        out[s] = traded(values[s], axis, s)
    return out


def call(kernel, index, inputs, outputs, name, limit=16, after=(), cost=0):
    single = not isinstance(outputs, list)
    return pl.pallas_call(
        kernel,
        in_specs=[pl.BlockSpec(memory_space=pltpu.SMEM)] * len(index)
        + [pl.BlockSpec(memory_space=pltpu.VMEM)] * len(inputs)
        + [pl.BlockSpec(memory_space=pl.ANY)] * len(after),
        out_specs=pl.BlockSpec(memory_space=pltpu.VMEM)
        if single
        else [pl.BlockSpec(memory_space=pltpu.VMEM)] * len(outputs),
        out_shape=outputs,
        compiler_params=params(limit),
        cost_estimate=pl.CostEstimate(
            flops=cost * 10**9, bytes_accessed=cost * 3 * 10**6, transcendentals=0
        ),
        name=name,
    )(*index, *inputs, *after)


def experts_by_columns(held, gate_up_weight, down_weight, owners, attention):
    inner = lax.axis_size("inner")
    experts, count, _ = held.shape
    ff, width = down_weight.shape[1:]
    me = lax.axis_index("inner").astype(jnp.int32)
    level = me.reshape(1)
    others, last = [], []
    for s in reversed(range(1, inner)):
        last = gate_up(
            (me ^ s).reshape(1), inner, held, gate_up_weight, jnp.bfloat16, after=last
        )
        others.append(traded(last[0], "inner", s))
    own, done = gate_up(level, inner, held, gate_up_weight, jnp.float32, True, last)
    first = attention(done, 0, 2)
    active = call(
        activate_kernel,
        [],
        [own, *others],
        jax.ShapeDtypeStruct((experts, count, ff // inner), jnp.bfloat16),
        "activate",
        after=[first],
    )
    parts = trade([active] * inner, "inner")
    sums_shape = jax.ShapeDtypeStruct((experts, count, width), jnp.float32)
    sums = call(down_first_kernel, [level], [active, down_weight], sums_shape, "down_first", 24)
    second = attention(sums, 1, 2)
    sums = call(
        functools.partial(down_more_kernel, 1),
        [level],
        [sums, parts[1], down_weight],
        sums_shape,
        "down_more",
        24,
    )
    back = call(
        functools.partial(down_rest_kernel, list(range(2, inner))),
        [level],
        [sums, *parts[2:], down_weight],
        [jax.ShapeDtypeStruct((experts * count // owners, width), jnp.bfloat16)] * owners,
        "down_rest",
        24,
        after=[second],
    )
    return back, jnp.concatenate([first, second], axis=0)


def experts_by_rows(held, gate_up_weight, down_weight, owners, attention):
    experts, count, _ = held.shape
    partial = jnp.einsum("xsd,xkdf->sxkf", held, gate_up_weight, preferred_element_type=jnp.float32)
    summed = lax.psum_scatter(partial, "inner", scatter_dimension=0, tiled=True)
    active = (jax.nn.silu(summed[:, :, 0]) * summed[:, :, 1]).astype(jnp.bfloat16)
    active = lax.all_gather(active, "inner", axis=0, tiled=True)
    outputs = jnp.einsum("sxf,xfd->xsd", active, down_weight, preferred_element_type=jnp.float32)
    outputs = outputs.astype(jnp.bfloat16).reshape(experts, owners, count // owners, -1)
    back = [outputs[:, t].reshape(experts * count // owners, -1) for t in range(owners)]
    return back, attention(held, 0, 1)


def body(
    queries,
    new_key_value,
    cached_key_value,
    parents,
    hidden,
    routes,
    gate_values,
    gate_up_weight,
    down_weight,
):
    owners, inner = lax.axis_size("expert"), lax.axis_size("inner")
    experts, _, depth, ff = gate_up_weight.shape
    rows, model = hidden.shape
    width = down_weight.shape[2]
    top = routes.shape[1]
    column = lax.axis_index("expert").astype(jnp.int32).reshape(1)
    level = lax.axis_index("inner").astype(jnp.int32).reshape(1)
    slots = experts * CAP * inner

    def attention(after, part, parts):
        return attend(queries, new_key_value, cached_key_value, parents, after, part, parts)

    slices = call(
        prepare_kernel,
        [level],
        [routes.T, gate_values.T, hidden],
        [jax.ShapeDtypeStruct((rows, depth + LANES), jnp.bfloat16)] * inner,
        "prepare",
    )
    slices = trade(slices, "inner")
    packs = call(
        functools.partial(pack_kernel, top, experts, inner),
        [column, level],
        slices,
        [jax.ShapeDtypeStruct((slots, depth), jnp.bfloat16)] * owners,
        "pack",
    )
    packs = trade(packs, "expert")
    held = call(
        select_kernel,
        [],
        packs,
        jax.ShapeDtypeStruct((experts, owners * CAP * inner, depth), jnp.bfloat16),
        "select",
        24,
    )
    even = ff % (inner * LANES) == 0
    back, attended = (experts_by_columns if even else experts_by_rows)(
        held, gate_up_weight, down_weight, owners, attention
    )
    back = trade(back, "expert")
    weights = call(
        functools.partial(weigh_kernel, top, experts),
        [column, level],
        slices,
        jax.ShapeDtypeStruct((owners, slots, inner * rows), jnp.bfloat16),
        "weigh",
        cost=1,
    )
    pieces = call(
        combine_kernel,
        [],
        [weights, *back],
        [jax.ShapeDtypeStruct((rows, width), jnp.bfloat16)] * inner,
        "combine",
    )
    pieces = trade(pieces, "inner")
    expert_out = call(
        assemble_kernel,
        [level],
        pieces,
        jax.ShapeDtypeStruct((rows, model), jnp.bfloat16),
        "assemble",
    )
    return attended.reshape(rows, QUERY_HEADS * HEAD_SIZE), expert_out


def solution(mesh):
    rows = ("groups", "expert", "inner")
    return jax.shard_map(
        body,
        mesh=mesh,
        in_specs=(
            P(rows, None),
            P(rows, None),
            P(rows, None, None, None),
            P(rows, None),
            P(rows, None),
            P(rows, None),
            P(rows, None),
            P("expert", None, "inner", None),
            P("expert", None, "inner"),
        ),
        out_specs=(P(rows, None), P(rows, None)),
        check_vma=False,
    )
```

```python
import functools
import math

import jax
import jax.numpy as jnp
from jax import lax
from jax.experimental import pallas as pl
from jax.experimental.pallas import tpu as pltpu
from jax.sharding import PartitionSpec as P

QUERY_HEADS = 64
KEY_HEADS = 4
HEAD_SIZE = 128
CAP = 3
LANES = 128


def params(limit, *semantics):
    return pltpu.CompilerParams(
        dimension_semantics=semantics or None, vmem_limit_bytes=limit * 1024 * 1024
    )


def attend_kernel(beams, parents, q_ref, new_ref, *refs):
    cache_refs, out_ref = refs[:beams], refs[-1]
    group = QUERY_HEADS // KEY_HEADS
    scale = 1.0 / math.sqrt(HEAD_SIZE)
    width = KEY_HEADS * HEAD_SIZE
    for b in range(beams):
        q, cache_ref = q_ref[b], cache_refs[b]
        fresh = new_ref[b].astype(jnp.float32)
        scores, own = [], []
        for k in range(KEY_HEADS):
            qk = q[k * group:(k + 1) * group]
            keys = cache_ref[0, 0, :, k * HEAD_SIZE:(k + 1) * HEAD_SIZE]
            scores.append(
                lax.dot_general(
                    qk, keys, (((1,), (1,)), ((), ())), preferred_element_type=jnp.float32
                )
            )
            own.append(
                jnp.sum(qk.astype(jnp.float32) * fresh[k:k + 1], axis=-1, keepdims=True)
            )
        scores = jnp.concatenate(scores, axis=0) * scale
        own = jnp.concatenate(own, axis=0) * scale
        upper = jnp.maximum(jnp.max(scores, axis=-1, keepdims=True), own)
        expo = jnp.exp(scores - upper)
        own_expo = jnp.exp(own - upper)
        total = jnp.sum(expo, axis=-1, keepdims=True) + own_expo
        probs = (expo / total).astype(jnp.bfloat16)
        own_prob = (own_expo / total).astype(jnp.bfloat16).astype(jnp.float32)
        for k in range(KEY_HEADS):
            rows = slice(k * group, (k + 1) * group)
            values = cache_ref[0, 0, :, width + k * HEAD_SIZE:width + (k + 1) * HEAD_SIZE]
            result = jnp.dot(probs[rows], values, preferred_element_type=jnp.float32)
            result = result + own_prob[rows] * fresh[KEY_HEADS + k:KEY_HEADS + k + 1]
            out_ref[b, rows] = result.astype(out_ref.dtype)


def attend(queries, new_key_value, cached_key_value, parents, after, part, parts):
    rows = queries.shape[0] // parts
    first = part * rows
    _, beams, length, width = cached_key_value.shape
    step = 4

    def parent_of(b):
        return lambda r, p: ((first + r * step + b) // beams, p[first + r * step + b], 0, 0)

    out = pl.pallas_call(
        functools.partial(attend_kernel, step),
        grid_spec=pltpu.PrefetchScalarGridSpec(
            num_scalar_prefetch=1,
            grid=(rows // step,),
            in_specs=[
                pl.BlockSpec(
                    (step, QUERY_HEADS, HEAD_SIZE), lambda r, p: (first // step + r, 0, 0)
                ),
                pl.BlockSpec(
                    (step, 2 * KEY_HEADS, HEAD_SIZE), lambda r, p: (first // step + r, 0, 0)
                ),
            ]
            + [pl.BlockSpec((1, 1, length, width), parent_of(b)) for b in range(step)]
            + [pl.BlockSpec(memory_space=pl.ANY)],
            out_specs=pl.BlockSpec((step, QUERY_HEADS, HEAD_SIZE), lambda r, p: (r, 0, 0)),
        ),
        out_shape=jax.ShapeDtypeStruct((rows, QUERY_HEADS, HEAD_SIZE), jnp.bfloat16),
        compiler_params=params(40),
        cost_estimate=pl.CostEstimate(
            flops=4 * rows * QUERY_HEADS * HEAD_SIZE * length,
            bytes_accessed=2 * rows * length * width,
            transcendentals=rows * QUERY_HEADS * length,
        ),
        name="attend",
    )(
        parents.reshape(-1),
        queries.reshape(-1, QUERY_HEADS, HEAD_SIZE),
        new_key_value.reshape(-1, 2 * KEY_HEADS, HEAD_SIZE),
        *[cached_key_value] * step,
        after,
    )
    return out


def spread(values, lanes, first):
    top = values.shape[0]
    shape = (top, lanes)
    chosen = (
        lax.broadcasted_iota(jnp.int32, shape, 1)
        == lax.broadcasted_iota(jnp.int32, shape, 0) + first
    ).astype(jnp.float32)
    return lax.dot_general(
        values.astype(jnp.float32), chosen, (((0,), (0,)), ((), ())), preferred_element_type=jnp.float32
    )


def prepare_kernel(me, routes_ref, gates_ref, hidden_ref, *out_refs):
    width = hidden_ref.shape[1] // len(out_refs)
    top = routes_ref.shape[0]
    notes = spread(routes_ref[...], LANES, 0) + spread(gates_ref[...], LANES, top)
    notes = notes.astype(jnp.bfloat16)
    for s, out_ref in enumerate(out_refs):
        start = pl.multiple_of((me[0] ^ s) * width, width)
        out_ref[:, :width] = hidden_ref[:, pl.ds(start, width)]
        out_ref[:, width:] = notes


def turned_notes(notes, top):
    shape = (max(8, 2 * top), LANES)
    chosen = (
        lax.broadcasted_iota(jnp.int32, shape, 0) == lax.broadcasted_iota(jnp.int32, shape, 1)
    ).astype(jnp.bfloat16)
    turned = lax.dot_general(
        chosen, notes, (((1,), (1,)), ((), ())), preferred_element_type=jnp.float32
    )
    return turned[:top], turned[top:2 * top]


def placing(routes, owner, level, experts, sources):
    top, rows = routes.shape
    count = CAP * sources
    shape = (experts * count, rows)
    slot = lax.broadcasted_iota(jnp.int32, shape, 0)
    row = lax.broadcasted_iota(jnp.int32, shape, 1)
    each = rows // sources
    local = jnp.zeros(shape, jnp.int32)
    for x in range(1, experts):
        local = local + (slot >= x * count).astype(jnp.int32)
    within = slot - local * count
    rank, source = within // sources, within % sources
    expert = (owner * experts + local).astype(jnp.float32)
    member = jnp.zeros(shape, jnp.float32)
    for t in range(top):
        member = jnp.where(routes[t:t + 1] == expert, 1.0, member)
    origin = level ^ (row // each)
    member = jnp.where(origin == source, member, 0.0)
    one = lax.broadcasted_iota(jnp.int32, (rows, rows), 0)
    other = lax.broadcasted_iota(jnp.int32, (rows, rows), 1)
    before = (one < other).astype(jnp.float32)
    ranks = jnp.dot(member, before, preferred_element_type=jnp.float32)
    return jnp.where(ranks == rank.astype(jnp.float32), member, 0.0), expert


def pack_kernel(top, experts, sources, afters, column, level, *refs):
    held, out_refs = refs[:sources], refs[sources + afters:]
    width = out_refs[0].shape[1]
    rows = jnp.concatenate([ref[:, :width] for ref in held], axis=0)
    notes = jnp.concatenate([ref[:, width:] for ref in held], axis=0)
    routes, _ = turned_notes(notes, top)
    for t, out_ref in enumerate(out_refs):
        place, _ = placing(routes, column[0] ^ t, level[0], experts, sources)
        out_ref[...] = jnp.dot(
            place.astype(jnp.bfloat16), rows, preferred_element_type=jnp.float32
        ).astype(out_ref.dtype)


def weigh_kernel(top, experts, column, level, *refs):
    held, out_ref = refs[:-1], refs[-1]
    notes = jnp.concatenate([ref[:, -LANES:] for ref in held], axis=0)
    routes, gates = turned_notes(notes, top)
    for t in range(out_ref.shape[0]):
        place, expert = placing(routes, column[0] ^ t, level[0], experts, len(held))
        weight = jnp.zeros_like(place)
        for k in range(top):
            weight = weight + jnp.where(routes[k:k + 1] == expert, gates[k:k + 1], 0.0)
        out_ref[t] = (weight * place).astype(out_ref.dtype)


def combine_kernel(weight_ref, *refs):
    owners = weight_ref.shape[0]
    back, out_refs = refs[:owners], refs[owners:]
    each = out_refs[0].shape[0]
    total = 0.0
    for t in range(owners):
        total = total + lax.dot_general(
            weight_ref[t],
            back[t][...],
            (((0,), (0,)), ((), ())),
            preferred_element_type=jnp.float32,
        )
    for s, out_ref in enumerate(out_refs):
        out_ref[...] = total[s * each:(s + 1) * each].astype(out_ref.dtype)


def assemble_kernel(me, *refs):
    pieces, out_ref = refs[:-1], refs[-1]
    width = pieces[0].shape[1]
    for s, piece in enumerate(pieces):
        start = pl.multiple_of((me[0] ^ s) * width, width)
        out_ref[:, pl.ds(start, width)] = piece[...]


def regroup(experts, owners, count):
    shape = (experts * owners * count, owners * experts * count)
    row = lax.broadcasted_iota(jnp.int32, shape, 0)
    other = lax.broadcasted_iota(jnp.int32, shape, 1)
    wanted = jnp.zeros(shape, jnp.int32) + row
    for x in range(experts):
        for t in range(owners):
            first = (x * owners + t) * count
            inside = (row >= first) & (row < first + count)
            wanted = jnp.where(inside, row - first + (t * experts + x) * count, wanted)
    return (other == wanted).astype(jnp.bfloat16)


def select_kernel(owners, *refs):
    packs, out_ref = refs[:owners], refs[-1]
    experts, count, _ = out_ref.shape
    rows = jnp.concatenate([ref[...].astype(jnp.float32) for ref in packs], axis=0)
    moved = jnp.dot(
        regroup(experts, len(packs), count // len(packs)),
        rows.astype(jnp.bfloat16),
        preferred_element_type=jnp.float32,
    ).astype(out_ref.dtype)
    for x in range(experts):
        out_ref[x] = moved[x * count:(x + 1) * count]


def load_kernel(expert, pieces, weight_hbm, after_ref, out_ref, done_ref, sems):
    del after_ref
    step = out_ref.shape[1] // pieces
    copies = [
        pltpu.make_async_copy(
            weight_hbm.at[expert, k, pl.ds(n * step, step)],
            out_ref.at[k, pl.ds(n * step, step)],
            sems.at[k * pieces + n],
        )
        for k in range(2)
        for n in range(pieces)
    ]
    for copy in copies:
        copy.start()
    done_ref[...] = jnp.zeros_like(done_ref)
    for copy in copies:
        copy.wait()


def load(weight, expert, after, limit):
    pieces = 2
    return pl.pallas_call(
        functools.partial(load_kernel, expert, pieces),
        in_specs=[pl.BlockSpec(memory_space=pl.ANY)] * 2,
        out_specs=[pl.BlockSpec(memory_space=pltpu.VMEM)] * 2,
        out_shape=[
            jax.ShapeDtypeStruct(weight.shape[1:], weight.dtype),
            jax.ShapeDtypeStruct((8, LANES), jnp.float32),
        ],
        scratch_shapes=[pltpu.SemaphoreType.DMA((2 * pieces,))],
        compiler_params=params(limit),
        cost_estimate=pl.CostEstimate(flops=2 * 10**9, bytes_accessed=0, transcendentals=0),
        name="load",
    )(weight, after)


def gate_up_kernel(experts, afters, chunk, rows_ref, *refs):
    weight_refs, out_refs = refs[:experts], refs[experts + afters:]
    out_ref = out_refs[0]
    if len(out_refs) > 1:
        out_refs[1][...] = jnp.zeros_like(out_refs[1])
    ff = out_ref.shape[2] // 2
    columns = pl.ds(pl.multiple_of(chunk[0] * ff, ff), ff)
    for x in range(experts):
        for k in range(2):
            out_ref[x, :, k * ff:(k + 1) * ff] = jnp.dot(
                rows_ref[x], weight_refs[x][k, :, columns], preferred_element_type=jnp.float32
            ).astype(out_ref.dtype)


def gate_up(chunk, chunks, rows, weights, dtype, done=False, after=()):
    experts, count, _ = rows.shape
    ff = weights[0].shape[2] // chunks
    return call(
        functools.partial(gate_up_kernel, experts, len(after)),
        [chunk],
        [rows, *weights],
        [jax.ShapeDtypeStruct((experts, count, 2 * ff), dtype)]
        + [jax.ShapeDtypeStruct((8, LANES), jnp.float32)] * done,
        "gate_up",
        24,
        after=after,
        cost=2,
    )


def activate_kernel(own_ref, *refs):
    other_refs, out_ref = refs[:-2], refs[-1]
    ff = out_ref.shape[2]
    for x in range(out_ref.shape[0]):
        total = own_ref[x]
        for ref in other_refs:
            total = total + ref[x].astype(jnp.float32)
        gate, up = total[:, :ff], total[:, ff:]
        out_ref[x] = (gate / (1.0 + jnp.exp(-gate)) * up).astype(out_ref.dtype)


def down_product(part_ref, weight_ref, x, chunk):
    ff = part_ref.shape[2]
    rows = pl.ds(pl.multiple_of(chunk * ff, ff), ff)
    return jnp.dot(part_ref[x], weight_ref[x, rows], preferred_element_type=jnp.float32)


def down_first_kernel(me, part_ref, weight_ref, sum_ref):
    for x in range(part_ref.shape[0]):
        sum_ref[x] = down_product(part_ref, weight_ref, x, me[0])


def down_more_kernel(index, me, before_ref, part_ref, weight_ref, sum_ref):
    for x in range(part_ref.shape[0]):
        sum_ref[x] = before_ref[x] + down_product(part_ref, weight_ref, x, me[0] ^ index)


def down_rest_kernel(indices, me, sum_ref, *refs):
    count = len(indices)
    parts, weight_ref, out_refs = refs[:count], refs[count], refs[count + 2:]
    experts, slots, _ = sum_ref.shape
    sums = []
    for x in range(experts):
        total = sum_ref[x]
        for part_ref, index in zip(parts, indices):
            total = total + down_product(part_ref, weight_ref, x, me[0] ^ index)
        sums.append(total.astype(jnp.bfloat16))
    owners = len(out_refs)
    rows = experts * slots // owners
    moved = lax.dot_general(
        regroup(experts, owners, slots // owners),
        jnp.concatenate(sums, axis=0),
        (((0,), (0,)), ((), ())),
        preferred_element_type=jnp.float32,
    )
    for t, out_ref in enumerate(out_refs):
        out_ref[...] = moved[t * rows:(t + 1) * rows].astype(out_ref.dtype)


def traded(value, axis, index):
    return lax.ppermute(value, axis, [(i, i ^ index) for i in range(lax.axis_size(axis))])


def trade(values, axis):
    out = [values[0]] + [None] * (len(values) - 1)
    for s in reversed(range(1, len(values))):
        out[s] = traded(values[s], axis, s)
    return out


def call(kernel, index, inputs, outputs, name, limit=16, after=(), cost=0):
    single = not isinstance(outputs, list)
    return pl.pallas_call(
        kernel,
        in_specs=[pl.BlockSpec(memory_space=pltpu.SMEM)] * len(index)
        + [pl.BlockSpec(memory_space=pltpu.VMEM)] * len(inputs)
        + [pl.BlockSpec(memory_space=pl.ANY)] * len(after),
        out_specs=pl.BlockSpec(memory_space=pltpu.VMEM)
        if single
        else [pl.BlockSpec(memory_space=pltpu.VMEM)] * len(outputs),
        out_shape=outputs,
        compiler_params=params(limit),
        cost_estimate=pl.CostEstimate(
            flops=cost * 10**9, bytes_accessed=0, transcendentals=0
        ),
        name=name,
    )(*index, *inputs, *after)


def experts_by_columns(held, loaded, down_weight, owners, attention):
    inner = lax.axis_size("inner")
    experts, count, _ = held.shape
    ff, width = down_weight.shape[1:]
    me = lax.axis_index("inner").astype(jnp.int32)
    level = me.reshape(1)
    others, last = [], []
    for s in reversed(range(1, inner)):
        last = gate_up(
            (me ^ s).reshape(1), inner, held, loaded, jnp.bfloat16, after=last
        )
        others.append(traded(last[0], "inner", s))
    own, done = gate_up(level, inner, held, loaded, jnp.float32, True, last)
    first = attention(done, 0, 2)
    active = call(
        activate_kernel,
        [],
        [own, *others],
        jax.ShapeDtypeStruct((experts, count, ff // inner), jnp.bfloat16),
        "activate",
        after=[first],
    )
    parts = trade([active] * inner, "inner")
    sums_shape = jax.ShapeDtypeStruct((experts, count, width), jnp.float32)
    sums = call(down_first_kernel, [level], [active, down_weight], sums_shape, "down_first", 24)
    second = attention(sums, 1, 2)
    sums = call(
        functools.partial(down_more_kernel, 1),
        [level],
        [sums, parts[1], down_weight],
        sums_shape,
        "down_more",
        24,
    )
    back = call(
        functools.partial(down_rest_kernel, list(range(2, inner))),
        [level],
        [sums, *parts[2:], down_weight],
        [jax.ShapeDtypeStruct((experts * count // owners, width), jnp.bfloat16)] * owners,
        "down_rest",
        24,
        after=[second],
    )
    return back, jnp.concatenate([first, second], axis=0)


def experts_by_rows(held, gate_up_weight, down_weight, owners, attention):
    experts, count, _ = held.shape
    partial = jnp.einsum("xsd,xkdf->sxkf", held, gate_up_weight, preferred_element_type=jnp.float32)
    summed = lax.psum_scatter(partial, "inner", scatter_dimension=0, tiled=True)
    active = (jax.nn.silu(summed[:, :, 0]) * summed[:, :, 1]).astype(jnp.bfloat16)
    active = lax.all_gather(active, "inner", axis=0, tiled=True)
    outputs = jnp.einsum("sxf,xfd->xsd", active, down_weight, preferred_element_type=jnp.float32)
    outputs = outputs.astype(jnp.bfloat16).reshape(experts, owners, count // owners, -1)
    back = [outputs[:, t].reshape(experts * count // owners, -1) for t in range(owners)]
    return back, attention(held, 0, 1)


def body(
    queries,
    new_key_value,
    cached_key_value,
    parents,
    hidden,
    routes,
    gate_values,
    gate_up_weight,
    down_weight,
):
    owners, inner = lax.axis_size("expert"), lax.axis_size("inner")
    experts, _, depth, ff = gate_up_weight.shape
    rows, model = hidden.shape
    width = down_weight.shape[2]
    top = routes.shape[1]
    column = lax.axis_index("expert").astype(jnp.int32).reshape(1)
    level = lax.axis_index("inner").astype(jnp.int32).reshape(1)
    slots = experts * CAP * inner

    def attention(after, part, parts):
        return attend(queries, new_key_value, cached_key_value, parents, after, part, parts)

    slices = call(
        prepare_kernel,
        [level],
        [routes.T, gate_values.T, hidden],
        [jax.ShapeDtypeStruct((rows, depth + LANES), jnp.bfloat16)] * inner,
        "prepare",
    )
    even = ff % (inner * LANES) == 0
    loaded = [load(gate_up_weight, 0, slices[0], 45)] if even else []
    slices = trade(slices, "inner")
    packs = call(
        functools.partial(pack_kernel, top, experts, inner, len(loaded)),
        [column, level],
        slices,
        [jax.ShapeDtypeStruct((slots, depth), jnp.bfloat16)] * owners,
        "pack",
        after=[done for _, done in loaded],
    )
    if even:
        loaded += [load(gate_up_weight, x, packs[0], 40) for x in range(1, experts)]
    packs = trade(packs, "expert")
    held = call(
        functools.partial(select_kernel, owners),
        [],
        packs,
        jax.ShapeDtypeStruct((experts, owners * CAP * inner, depth), jnp.bfloat16),
        "select",
        24,
        after=[done for _, done in loaded[1:]],
    )
    back, attended = (experts_by_columns if even else experts_by_rows)(
        held, [part for part, _ in loaded] or gate_up_weight, down_weight, owners, attention
    )
    back = trade(back, "expert")
    weights = call(
        functools.partial(weigh_kernel, top, experts),
        [column, level],
        slices,
        jax.ShapeDtypeStruct((owners, slots, inner * rows), jnp.bfloat16),
        "weigh",
        cost=1,
    )
    pieces = call(
        combine_kernel,
        [],
        [weights, *back],
        [jax.ShapeDtypeStruct((rows, width), jnp.bfloat16)] * inner,
        "combine",
    )
    pieces = trade(pieces, "inner")
    expert_out = call(
        assemble_kernel,
        [level],
        pieces,
        jax.ShapeDtypeStruct((rows, model), jnp.bfloat16),
        "assemble",
    )
    return attended.reshape(rows, QUERY_HEADS * HEAD_SIZE), expert_out


def solution(mesh):
    rows = ("groups", "expert", "inner")
    return jax.shard_map(
        body,
        mesh=mesh,
        in_specs=(
            P(rows, None),
            P(rows, None),
            P(rows, None, None, None),
            P(rows, None),
            P(rows, None),
            P(rows, None),
            P(rows, None),
            P("expert", None, "inner", None),
            P("expert", None, "inner"),
        ),
        out_specs=(P(rows, None), P(rows, None)),
        check_vma=False,
    )
```

```python
import functools
import math

import jax
import jax.numpy as jnp
from jax import lax
from jax.experimental import pallas as pl
from jax.experimental.pallas import tpu as pltpu
from jax.sharding import PartitionSpec as P

QUERY_HEADS = 64
KEY_HEADS = 4
HEAD_SIZE = 128
CAP = 3
LANES = 128


def params(limit, *semantics):
    return pltpu.CompilerParams(
        dimension_semantics=semantics or None, vmem_limit_bytes=limit * 1024 * 1024
    )


def attend_kernel(beams, parents, q_ref, new_ref, *refs):
    cache_refs, out_ref = refs[:beams], refs[-1]
    group = QUERY_HEADS // KEY_HEADS
    scale = 1.0 / math.sqrt(HEAD_SIZE)
    width = KEY_HEADS * HEAD_SIZE
    for b in range(beams):
        q, cache_ref = q_ref[b], cache_refs[b]
        fresh = new_ref[b].astype(jnp.float32)
        scores, own = [], []
        for k in range(KEY_HEADS):
            qk = q[k * group:(k + 1) * group]
            keys = cache_ref[0, 0, :, k * HEAD_SIZE:(k + 1) * HEAD_SIZE]
            scores.append(
                lax.dot_general(
                    qk, keys, (((1,), (1,)), ((), ())), preferred_element_type=jnp.float32
                )
            )
            own.append(
                jnp.sum(qk.astype(jnp.float32) * fresh[k:k + 1], axis=-1, keepdims=True)
            )
        scores = jnp.concatenate(scores, axis=0) * scale
        own = jnp.concatenate(own, axis=0) * scale
        upper = jnp.maximum(jnp.max(scores, axis=-1, keepdims=True), own)
        expo = jnp.exp(scores - upper)
        own_expo = jnp.exp(own - upper)
        total = jnp.sum(expo, axis=-1, keepdims=True) + own_expo
        probs = (expo / total).astype(jnp.bfloat16)
        own_prob = (own_expo / total).astype(jnp.bfloat16).astype(jnp.float32)
        for k in range(KEY_HEADS):
            rows = slice(k * group, (k + 1) * group)
            values = cache_ref[0, 0, :, width + k * HEAD_SIZE:width + (k + 1) * HEAD_SIZE]
            result = jnp.dot(probs[rows], values, preferred_element_type=jnp.float32)
            result = result + own_prob[rows] * fresh[KEY_HEADS + k:KEY_HEADS + k + 1]
            out_ref[b, rows] = result.astype(out_ref.dtype)


def attend(queries, new_key_value, cached_key_value, parents, after):
    rows = queries.shape[0]
    _, beams, length, width = cached_key_value.shape
    step = 4

    def parent_of(b):
        return lambda r, p: ((r * step + b) // beams, p[r * step + b], 0, 0)

    out = pl.pallas_call(
        functools.partial(attend_kernel, step),
        grid_spec=pltpu.PrefetchScalarGridSpec(
            num_scalar_prefetch=1,
            grid=(rows // step,),
            in_specs=[
                pl.BlockSpec((step, QUERY_HEADS, HEAD_SIZE), lambda r, p: (r, 0, 0)),
                pl.BlockSpec((step, 2 * KEY_HEADS, HEAD_SIZE), lambda r, p: (r, 0, 0)),
            ]
            + [pl.BlockSpec((1, 1, length, width), parent_of(b)) for b in range(step)]
            + [pl.BlockSpec(memory_space=pl.ANY)],
            out_specs=pl.BlockSpec((step, QUERY_HEADS, HEAD_SIZE), lambda r, p: (r, 0, 0)),
        ),
        out_shape=jax.ShapeDtypeStruct((rows, QUERY_HEADS, HEAD_SIZE), jnp.bfloat16),
        compiler_params=params(40),
        cost_estimate=pl.CostEstimate(
            flops=4 * rows * QUERY_HEADS * HEAD_SIZE * length,
            bytes_accessed=2 * rows * length * width,
            transcendentals=rows * QUERY_HEADS * length,
        ),
        name="attend",
    )(
        parents.reshape(-1),
        queries.reshape(-1, QUERY_HEADS, HEAD_SIZE),
        new_key_value.reshape(-1, 2 * KEY_HEADS, HEAD_SIZE),
        *[cached_key_value] * step,
        after,
    )
    return out


def spread(values, lanes, first):
    top = values.shape[0]
    shape = (top, lanes)
    chosen = (
        lax.broadcasted_iota(jnp.int32, shape, 1)
        == lax.broadcasted_iota(jnp.int32, shape, 0) + first
    ).astype(jnp.float32)
    return lax.dot_general(
        values.astype(jnp.float32), chosen, (((0,), (0,)), ((), ())), preferred_element_type=jnp.float32
    )


def prepare_kernel(me, routes_ref, gates_ref, hidden_ref, *out_refs):
    width = hidden_ref.shape[1] // len(out_refs)
    top = routes_ref.shape[0]
    notes = spread(routes_ref[...], LANES, 0) + spread(gates_ref[...], LANES, top)
    notes = notes.astype(jnp.bfloat16)
    for s, out_ref in enumerate(out_refs):
        start = pl.multiple_of((me[0] ^ s) * width, width)
        out_ref[:, :width] = hidden_ref[:, pl.ds(start, width)]
        out_ref[:, width:] = notes


def turned_notes(notes, top):
    shape = (max(8, 2 * top), LANES)
    chosen = (
        lax.broadcasted_iota(jnp.int32, shape, 0) == lax.broadcasted_iota(jnp.int32, shape, 1)
    ).astype(jnp.bfloat16)
    turned = lax.dot_general(
        chosen, notes, (((1,), (1,)), ((), ())), preferred_element_type=jnp.float32
    )
    return turned[:top], turned[top:2 * top]


def placing(routes, column, level, owners, experts, sources):
    top, rows = routes.shape
    count = CAP * sources
    shape = (owners * experts * count, rows)
    slot = lax.broadcasted_iota(jnp.int32, shape, 0)
    row = lax.broadcasted_iota(jnp.int32, shape, 1)
    each = rows // sources
    block = jnp.zeros(shape, jnp.int32)
    for n in range(1, owners * experts):
        block = block + (slot >= n * count).astype(jnp.int32)
    within = slot - block * count
    rank, source = within // sources, within % sources
    expert = ((column ^ (block // experts)) * experts + block % experts).astype(jnp.float32)
    member = jnp.zeros(shape, jnp.float32)
    for t in range(top):
        member = jnp.where(routes[t:t + 1] == expert, 1.0, member)
    origin = level ^ (row // each)
    member = jnp.where(origin == source, member, 0.0)
    one = lax.broadcasted_iota(jnp.int32, (rows, rows), 0)
    other = lax.broadcasted_iota(jnp.int32, (rows, rows), 1)
    before = (one < other).astype(jnp.float32)
    ranks = jnp.dot(member, before, preferred_element_type=jnp.float32)
    return jnp.where(ranks == rank.astype(jnp.float32), member, 0.0), expert


def pack_kernel(top, experts, sources, afters, column, level, *refs):
    held, out_refs = refs[:sources], refs[sources + afters:]
    slots, width = out_refs[0].shape
    rows = jnp.concatenate([ref[:, :width] for ref in held], axis=0)
    notes = jnp.concatenate([ref[:, width:] for ref in held], axis=0)
    routes, _ = turned_notes(notes, top)
    place, _ = placing(routes, column[0], level[0], len(out_refs), experts, sources)
    moved = jnp.dot(place.astype(jnp.bfloat16), rows, preferred_element_type=jnp.float32)
    for t, out_ref in enumerate(out_refs):
        out_ref[...] = moved[t * slots:(t + 1) * slots].astype(out_ref.dtype)


def weigh_kernel(top, experts, column, level, *refs):
    held, out_ref = refs[:-1], refs[-1]
    owners, slots, _ = out_ref.shape
    notes = jnp.concatenate([ref[:, -LANES:] for ref in held], axis=0)
    routes, gates = turned_notes(notes, top)
    place, expert = placing(routes, column[0], level[0], owners, experts, len(held))
    weight = jnp.zeros_like(place)
    for k in range(top):
        weight = weight + jnp.where(routes[k:k + 1] == expert, gates[k:k + 1], 0.0)
    weight = weight * place
    for t in range(owners):
        out_ref[t] = weight[t * slots:(t + 1) * slots].astype(out_ref.dtype)


def combine_kernel(weight_ref, *refs):
    owners = weight_ref.shape[0]
    back, out_refs = refs[:owners], refs[owners:]
    each = out_refs[0].shape[0]
    total = 0.0
    for t in range(owners):
        total = total + lax.dot_general(
            weight_ref[t],
            back[t][...],
            (((0,), (0,)), ((), ())),
            preferred_element_type=jnp.float32,
        )
    for s, out_ref in enumerate(out_refs):
        out_ref[...] = total[s * each:(s + 1) * each].astype(out_ref.dtype)


def assemble_kernel(me, *refs):
    pieces, out_ref = refs[:-1], refs[-1]
    width = pieces[0].shape[1]
    for s, piece in enumerate(pieces):
        start = pl.multiple_of((me[0] ^ s) * width, width)
        out_ref[:, pl.ds(start, width)] = piece[...]


def regroup(experts, owners, count):
    shape = (experts * owners * count, owners * experts * count)
    row = lax.broadcasted_iota(jnp.int32, shape, 0)
    other = lax.broadcasted_iota(jnp.int32, shape, 1)
    wanted = jnp.zeros(shape, jnp.int32) + row
    for x in range(experts):
        for t in range(owners):
            first = (x * owners + t) * count
            inside = (row >= first) & (row < first + count)
            wanted = jnp.where(inside, row - first + (t * experts + x) * count, wanted)
    return (other == wanted).astype(jnp.bfloat16)


def select_kernel(owners, *refs):
    packs, out_ref = refs[:owners], refs[-1]
    experts, count, _ = out_ref.shape
    rows = jnp.concatenate([ref[...].astype(jnp.float32) for ref in packs], axis=0)
    moved = jnp.dot(
        regroup(experts, len(packs), count // len(packs)),
        rows.astype(jnp.bfloat16),
        preferred_element_type=jnp.float32,
    ).astype(out_ref.dtype)
    for x in range(experts):
        out_ref[x] = moved[x * count:(x + 1) * count]


def load_kernel(expert, pieces, weight_hbm, after_ref, out_ref, done_ref, sems):
    del after_ref
    step = out_ref.shape[1] // pieces
    copies = [
        pltpu.make_async_copy(
            weight_hbm.at[expert, k, pl.ds(n * step, step)],
            out_ref.at[k, pl.ds(n * step, step)],
            sems.at[k * pieces + n],
        )
        for k in range(2)
        for n in range(pieces)
    ]
    for copy in copies:
        copy.start()
    done_ref[...] = jnp.zeros_like(done_ref)
    for copy in copies:
        copy.wait()


def load(weight, expert, after, limit):
    pieces = 8
    return pl.pallas_call(
        functools.partial(load_kernel, expert, pieces),
        in_specs=[pl.BlockSpec(memory_space=pl.ANY)] * 2,
        out_specs=[pl.BlockSpec(memory_space=pltpu.VMEM)] * 2,
        out_shape=[
            jax.ShapeDtypeStruct(weight.shape[1:], weight.dtype),
            jax.ShapeDtypeStruct((8, LANES), jnp.float32),
        ],
        scratch_shapes=[pltpu.SemaphoreType.DMA((2 * pieces,))],
        compiler_params=params(limit),
        cost_estimate=pl.CostEstimate(flops=10**8, bytes_accessed=0, transcendentals=0),
        name="load",
    )(weight, after)


def gate_up_kernel(experts, afters, chunk, rows_ref, *refs):
    weight_refs, out_refs = refs[:experts], refs[experts + afters:]
    out_ref = out_refs[0]
    if len(out_refs) > 1:
        out_refs[1][...] = jnp.zeros_like(out_refs[1])
    ff = out_ref.shape[2] // 2
    columns = pl.ds(pl.multiple_of(chunk[0] * ff, ff), ff)
    for x in range(experts):
        for k in range(2):
            out_ref[x, :, k * ff:(k + 1) * ff] = jnp.dot(
                rows_ref[x], weight_refs[x][k, :, columns], preferred_element_type=jnp.float32
            ).astype(out_ref.dtype)


def gate_up(chunk, chunks, rows, weights, dtype, done=False, after=()):
    experts, count, _ = rows.shape
    ff = weights[0].shape[2] // chunks
    return call(
        functools.partial(gate_up_kernel, experts, len(after)),
        [chunk],
        [rows, *weights],
        [jax.ShapeDtypeStruct((experts, count, 2 * ff), dtype)]
        + [jax.ShapeDtypeStruct((8, LANES), jnp.float32)] * done,
        "gate_up",
        24,
        after=after,
        cost=2,
    )


def activate_kernel(own_ref, *refs):
    other_refs, out_ref = refs[:-2], refs[-1]
    ff = out_ref.shape[2]
    for x in range(out_ref.shape[0]):
        total = own_ref[x]
        for ref in other_refs:
            total = total + ref[x].astype(jnp.float32)
        gate, up = total[:, :ff], total[:, ff:]
        out_ref[x] = (gate / (1.0 + jnp.exp(-gate)) * up).astype(out_ref.dtype)


def down_product(part_ref, weight_ref, x, chunk):
    ff = part_ref.shape[2]
    rows = pl.ds(pl.multiple_of(chunk * ff, ff), ff)
    return jnp.dot(part_ref[x], weight_ref[x, rows], preferred_element_type=jnp.float32)


def down_first_kernel(me, part_ref, weight_ref, sum_ref):
    for x in range(part_ref.shape[0]):
        sum_ref[x] = down_product(part_ref, weight_ref, x, me[0])


def down_more_kernel(index, me, before_ref, part_ref, weight_ref, sum_ref):
    for x in range(part_ref.shape[0]):
        sum_ref[x] = before_ref[x] + down_product(part_ref, weight_ref, x, me[0] ^ index)


def down_rest_kernel(indices, me, sum_ref, *refs):
    count = len(indices)
    parts, weight_ref, out_refs = refs[:count], refs[count], refs[count + 1:]
    experts, slots, _ = sum_ref.shape
    sums = []
    for x in range(experts):
        total = sum_ref[x]
        for part_ref, index in zip(parts, indices):
            total = total + down_product(part_ref, weight_ref, x, me[0] ^ index)
        sums.append(total.astype(jnp.bfloat16))
    owners = len(out_refs)
    rows = experts * slots // owners
    moved = lax.dot_general(
        regroup(experts, owners, slots // owners),
        jnp.concatenate(sums, axis=0),
        (((0,), (0,)), ((), ())),
        preferred_element_type=jnp.float32,
    )
    for t, out_ref in enumerate(out_refs):
        out_ref[...] = moved[t * rows:(t + 1) * rows].astype(out_ref.dtype)


def traded(value, axis, index):
    return lax.ppermute(value, axis, [(i, i ^ index) for i in range(lax.axis_size(axis))])


def trade(values, axis):
    out = [values[0]] + [None] * (len(values) - 1)
    for s in reversed(range(1, len(values))):
        out[s] = traded(values[s], axis, s)
    return out


def call(kernel, index, inputs, outputs, name, limit=16, after=(), cost=0):
    single = not isinstance(outputs, list)
    return pl.pallas_call(
        kernel,
        in_specs=[pl.BlockSpec(memory_space=pltpu.SMEM)] * len(index)
        + [pl.BlockSpec(memory_space=pltpu.VMEM)] * len(inputs)
        + [pl.BlockSpec(memory_space=pl.ANY)] * len(after),
        out_specs=pl.BlockSpec(memory_space=pltpu.VMEM)
        if single
        else [pl.BlockSpec(memory_space=pltpu.VMEM)] * len(outputs),
        out_shape=outputs,
        compiler_params=params(limit),
        cost_estimate=pl.CostEstimate(
            flops=cost * 10**9, bytes_accessed=0, transcendentals=0
        ),
        name=name,
    )(*index, *inputs, *after)


def experts_by_columns(held, loaded, down_weight, owners, attention):
    inner = lax.axis_size("inner")
    experts, count, _ = held.shape
    ff, width = down_weight.shape[1:]
    me = lax.axis_index("inner").astype(jnp.int32)
    level = me.reshape(1)
    others, last = [], []
    for s in reversed(range(1, inner)):
        last = gate_up(
            (me ^ s).reshape(1), inner, held, loaded, jnp.bfloat16, after=last
        )
        others.append(traded(last[0], "inner", s))
    own, done = gate_up(level, inner, held, loaded, jnp.float32, True, last)
    attended = attention(done)
    active = call(
        activate_kernel,
        [],
        [own, *others],
        jax.ShapeDtypeStruct((experts, count, ff // inner), jnp.bfloat16),
        "activate",
        after=[attended],
    )
    parts = trade([active] * inner, "inner")
    sums_shape = jax.ShapeDtypeStruct((experts, count, width), jnp.float32)
    sums = call(down_first_kernel, [level], [active, down_weight], sums_shape, "down_first", 24)
    sums = call(
        functools.partial(down_more_kernel, 1),
        [level],
        [sums, parts[1], down_weight],
        sums_shape,
        "down_more",
        24,
    )
    back = call(
        functools.partial(down_rest_kernel, list(range(2, inner))),
        [level],
        [sums, *parts[2:], down_weight],
        [jax.ShapeDtypeStruct((experts * count // owners, width), jnp.bfloat16)] * owners,
        "down_rest",
        24,
    )
    return back, attended


def experts_by_rows(held, gate_up_weight, down_weight, owners, attention):
    experts, count, _ = held.shape
    partial = jnp.einsum("xsd,xkdf->sxkf", held, gate_up_weight, preferred_element_type=jnp.float32)
    summed = lax.psum_scatter(partial, "inner", scatter_dimension=0, tiled=True)
    active = (jax.nn.silu(summed[:, :, 0]) * summed[:, :, 1]).astype(jnp.bfloat16)
    active = lax.all_gather(active, "inner", axis=0, tiled=True)
    outputs = jnp.einsum("sxf,xfd->xsd", active, down_weight, preferred_element_type=jnp.float32)
    outputs = outputs.astype(jnp.bfloat16).reshape(experts, owners, count // owners, -1)
    back = [outputs[:, t].reshape(experts * count // owners, -1) for t in range(owners)]
    return back, attention(held)


def body(
    queries,
    new_key_value,
    cached_key_value,
    parents,
    hidden,
    routes,
    gate_values,
    gate_up_weight,
    down_weight,
):
    owners, inner = lax.axis_size("expert"), lax.axis_size("inner")
    experts, _, depth, ff = gate_up_weight.shape
    rows, model = hidden.shape
    width = down_weight.shape[2]
    top = routes.shape[1]
    column = lax.axis_index("expert").astype(jnp.int32).reshape(1)
    level = lax.axis_index("inner").astype(jnp.int32).reshape(1)
    slots = experts * CAP * inner

    attention = functools.partial(attend, queries, new_key_value, cached_key_value, parents)

    slices = call(
        prepare_kernel,
        [level],
        [routes.T, gate_values.T, hidden],
        [jax.ShapeDtypeStruct((rows, depth + LANES), jnp.bfloat16)] * inner,
        "prepare",
    )
    even = ff % (inner * LANES) == 0
    loaded = [load(gate_up_weight, 0, slices[0], 45)] if even else []
    slices = trade(slices, "inner")
    packs = call(
        functools.partial(pack_kernel, top, experts, inner, len(loaded)),
        [column, level],
        slices,
        [jax.ShapeDtypeStruct((slots, depth), jnp.bfloat16)] * owners,
        "pack",
        after=[done for _, done in loaded],
    )
    if even:
        loaded += [load(gate_up_weight, x, packs[0], 40) for x in range(1, experts)]
    packs = trade(packs, "expert")
    held = call(
        functools.partial(select_kernel, owners),
        [],
        packs,
        jax.ShapeDtypeStruct((experts, owners * CAP * inner, depth), jnp.bfloat16),
        "select",
        24,
        after=[done for _, done in loaded[1:]],
    )
    back, attended = (experts_by_columns if even else experts_by_rows)(
        held, [part for part, _ in loaded] or gate_up_weight, down_weight, owners, attention
    )
    back = trade(back, "expert")
    weights = call(
        functools.partial(weigh_kernel, top, experts),
        [column, level],
        slices,
        jax.ShapeDtypeStruct((owners, slots, inner * rows), jnp.bfloat16),
        "weigh",
        cost=1,
    )
    pieces = call(
        combine_kernel,
        [],
        [weights, *back],
        [jax.ShapeDtypeStruct((rows, width), jnp.bfloat16)] * inner,
        "combine",
    )
    pieces = trade(pieces, "inner")
    expert_out = call(
        assemble_kernel,
        [level],
        pieces,
        jax.ShapeDtypeStruct((rows, model), jnp.bfloat16),
        "assemble",
    )
    return attended.reshape(rows, QUERY_HEADS * HEAD_SIZE), expert_out


def solution(mesh):
    rows = ("groups", "expert", "inner")
    return jax.shard_map(
        body,
        mesh=mesh,
        in_specs=(
            P(rows, None),
            P(rows, None),
            P(rows, None, None, None),
            P(rows, None),
            P(rows, None),
            P(rows, None),
            P(rows, None),
            P("expert", None, "inner", None),
            P("expert", None, "inner"),
        ),
        out_specs=(P(rows, None), P(rows, None)),
        check_vma=False,
    )
```

```python
import functools
import math

import jax
import jax.numpy as jnp
from jax import lax
from jax.experimental import pallas as pl
from jax.experimental.pallas import tpu as pltpu
from jax.sharding import PartitionSpec as P

QUERY_HEADS = 64
KEY_HEADS = 4
HEAD_SIZE = 128
CAP = 3
LANES = 128


def params(limit, *semantics):
    return pltpu.CompilerParams(
        dimension_semantics=semantics or None, vmem_limit_bytes=limit * 1024 * 1024
    )


def attend_kernel(beams, parents, q_ref, new_ref, *refs):
    cache_refs, out_ref = refs[:beams], refs[-1]
    group = QUERY_HEADS // KEY_HEADS
    scale = 1.0 / math.sqrt(HEAD_SIZE)
    width = KEY_HEADS * HEAD_SIZE
    for b in range(beams):
        q, cache_ref = q_ref[b], cache_refs[b]
        fresh = new_ref[b].astype(jnp.float32)
        scores, own = [], []
        for k in range(KEY_HEADS):
            qk = q[k * group:(k + 1) * group]
            keys = cache_ref[0, 0, :, k * HEAD_SIZE:(k + 1) * HEAD_SIZE]
            scores.append(
                lax.dot_general(
                    qk, keys, (((1,), (1,)), ((), ())), preferred_element_type=jnp.float32
                )
            )
            own.append(
                jnp.sum(qk.astype(jnp.float32) * fresh[k:k + 1], axis=-1, keepdims=True)
            )
        scores = jnp.concatenate(scores, axis=0) * scale
        own = jnp.concatenate(own, axis=0) * scale
        upper = jnp.maximum(jnp.max(scores, axis=-1, keepdims=True), own)
        expo = jnp.exp(scores - upper)
        own_expo = jnp.exp(own - upper)
        total = jnp.sum(expo, axis=-1, keepdims=True) + own_expo
        probs = (expo / total).astype(jnp.bfloat16)
        own_prob = (own_expo / total).astype(jnp.bfloat16).astype(jnp.float32)
        for k in range(KEY_HEADS):
            rows = slice(k * group, (k + 1) * group)
            values = cache_ref[0, 0, :, width + k * HEAD_SIZE:width + (k + 1) * HEAD_SIZE]
            result = jnp.dot(probs[rows], values, preferred_element_type=jnp.float32)
            result = result + own_prob[rows] * fresh[KEY_HEADS + k:KEY_HEADS + k + 1]
            out_ref[b, rows] = result.astype(out_ref.dtype)


def attend(queries, new_key_value, cached_key_value, parents, after):
    rows = queries.shape[0]
    _, beams, length, width = cached_key_value.shape
    step = 4

    def parent_of(b):
        return lambda r, p: ((r * step + b) // beams, p[r * step + b], 0, 0)

    out = pl.pallas_call(
        functools.partial(attend_kernel, step),
        grid_spec=pltpu.PrefetchScalarGridSpec(
            num_scalar_prefetch=1,
            grid=(rows // step,),
            in_specs=[
                pl.BlockSpec((step, QUERY_HEADS, HEAD_SIZE), lambda r, p: (r, 0, 0)),
                pl.BlockSpec((step, 2 * KEY_HEADS, HEAD_SIZE), lambda r, p: (r, 0, 0)),
            ]
            + [pl.BlockSpec((1, 1, length, width), parent_of(b)) for b in range(step)]
            + [pl.BlockSpec(memory_space=pl.ANY)],
            out_specs=pl.BlockSpec((step, QUERY_HEADS, HEAD_SIZE), lambda r, p: (r, 0, 0)),
        ),
        out_shape=jax.ShapeDtypeStruct((rows, QUERY_HEADS, HEAD_SIZE), jnp.bfloat16),
        compiler_params=params(40),
        cost_estimate=pl.CostEstimate(
            flops=4 * rows * QUERY_HEADS * HEAD_SIZE * length,
            bytes_accessed=2 * rows * length * width,
            transcendentals=rows * QUERY_HEADS * length,
        ),
        name="attend",
    )(
        parents.reshape(-1),
        queries.reshape(-1, QUERY_HEADS, HEAD_SIZE),
        new_key_value.reshape(-1, 2 * KEY_HEADS, HEAD_SIZE),
        *[cached_key_value] * step,
        after,
    )
    return out


def spread(values, lanes, first):
    top = values.shape[0]
    shape = (top, lanes)
    chosen = (
        lax.broadcasted_iota(jnp.int32, shape, 1)
        == lax.broadcasted_iota(jnp.int32, shape, 0) + first
    ).astype(jnp.float32)
    return lax.dot_general(
        values.astype(jnp.float32), chosen, (((0,), (0,)), ((), ())), preferred_element_type=jnp.float32
    )


def prepare_kernel(me, routes_ref, gates_ref, hidden_ref, *out_refs):
    width = hidden_ref.shape[1] // len(out_refs)
    top = routes_ref.shape[0]
    notes = spread(routes_ref[...], LANES, 0) + spread(gates_ref[...], LANES, top)
    notes = notes.astype(jnp.bfloat16)
    for s, out_ref in enumerate(out_refs):
        start = pl.multiple_of((me[0] ^ s) * width, width)
        out_ref[:, :width] = hidden_ref[:, pl.ds(start, width)]
        out_ref[:, width:] = notes


def turned_notes(notes, top):
    shape = (max(8, 2 * top), LANES)
    chosen = (
        lax.broadcasted_iota(jnp.int32, shape, 0) == lax.broadcasted_iota(jnp.int32, shape, 1)
    ).astype(jnp.bfloat16)
    turned = lax.dot_general(
        chosen, notes, (((1,), (1,)), ((), ())), preferred_element_type=jnp.float32
    )
    return turned[:top], turned[top:2 * top]


def placing(routes, column, level, owners, experts, sources):
    top, rows = routes.shape
    count = CAP * sources
    shape = (owners * experts * count, rows)
    slot = lax.broadcasted_iota(jnp.int32, shape, 0)
    row = lax.broadcasted_iota(jnp.int32, shape, 1)
    each = rows // sources
    block = jnp.zeros(shape, jnp.int32)
    for n in range(1, owners * experts):
        block = block + (slot >= n * count).astype(jnp.int32)
    within = slot - block * count
    rank, source = within // sources, within % sources
    expert = ((column ^ (block // experts)) * experts + block % experts).astype(jnp.float32)
    member = jnp.zeros(shape, jnp.float32)
    for t in range(top):
        member = jnp.where(routes[t:t + 1] == expert, 1.0, member)
    origin = level ^ (row // each)
    member = jnp.where(origin == source, member, 0.0)
    one = lax.broadcasted_iota(jnp.int32, (rows, rows), 0)
    other = lax.broadcasted_iota(jnp.int32, (rows, rows), 1)
    before = (one < other).astype(jnp.float32)
    ranks = jnp.dot(member, before, preferred_element_type=jnp.float32)
    return jnp.where(ranks == rank.astype(jnp.float32), member, 0.0), expert


def pack_kernel(top, experts, sources, afters, column, level, *refs):
    held, out_refs = refs[:sources], refs[sources + afters:]
    slots, width = out_refs[0].shape
    rows = jnp.concatenate([ref[:, :width] for ref in held], axis=0)
    notes = jnp.concatenate([ref[:, width:] for ref in held], axis=0)
    routes, _ = turned_notes(notes, top)
    place, _ = placing(routes, column[0], level[0], len(out_refs), experts, sources)
    moved = jnp.dot(place.astype(jnp.bfloat16), rows, preferred_element_type=jnp.float32)
    for t, out_ref in enumerate(out_refs):
        out_ref[...] = moved[t * slots:(t + 1) * slots].astype(out_ref.dtype)


def weigh_kernel(top, experts, column, level, *refs):
    held, out_ref = refs[:-1], refs[-1]
    owners, slots, _ = out_ref.shape
    notes = jnp.concatenate([ref[:, -LANES:] for ref in held], axis=0)
    routes, gates = turned_notes(notes, top)
    place, expert = placing(routes, column[0], level[0], owners, experts, len(held))
    weight = jnp.zeros_like(place)
    for k in range(top):
        weight = weight + jnp.where(routes[k:k + 1] == expert, gates[k:k + 1], 0.0)
    weight = weight * place
    for t in range(owners):
        out_ref[t] = weight[t * slots:(t + 1) * slots].astype(out_ref.dtype)


def combine_kernel(weight_ref, *refs):
    owners = weight_ref.shape[0]
    back, out_refs = refs[:owners], refs[owners:]
    each = out_refs[0].shape[0]
    total = 0.0
    for t in range(owners):
        total = total + lax.dot_general(
            weight_ref[t],
            back[t][...],
            (((0,), (0,)), ((), ())),
            preferred_element_type=jnp.float32,
        )
    for s, out_ref in enumerate(out_refs):
        out_ref[...] = total[s * each:(s + 1) * each].astype(out_ref.dtype)


def assemble_kernel(me, *refs):
    pieces, out_ref = refs[:-1], refs[-1]
    width = pieces[0].shape[1]
    for s, piece in enumerate(pieces):
        start = pl.multiple_of((me[0] ^ s) * width, width)
        out_ref[:, pl.ds(start, width)] = piece[...]


def regroup(experts, owners, count):
    shape = (experts * owners * count, owners * experts * count)
    row = lax.broadcasted_iota(jnp.int32, shape, 0)
    other = lax.broadcasted_iota(jnp.int32, shape, 1)
    wanted = jnp.zeros(shape, jnp.int32) + row
    for x in range(experts):
        for t in range(owners):
            first = (x * owners + t) * count
            inside = (row >= first) & (row < first + count)
            wanted = jnp.where(inside, row - first + (t * experts + x) * count, wanted)
    return (other == wanted).astype(jnp.bfloat16)


def select_kernel(owners, *refs):
    packs, out_ref = refs[:owners], refs[-1]
    experts, count, _ = out_ref.shape
    rows = jnp.concatenate([ref[...].astype(jnp.float32) for ref in packs], axis=0)
    moved = jnp.dot(
        regroup(experts, len(packs), count // len(packs)),
        rows.astype(jnp.bfloat16),
        preferred_element_type=jnp.float32,
    ).astype(out_ref.dtype)
    for x in range(experts):
        out_ref[x] = moved[x * count:(x + 1) * count]


def load_kernel(expert, pieces, weight_hbm, *refs):
    out_ref, sems = refs[-2:]
    step = out_ref.shape[1] // pieces
    copies = [
        pltpu.make_async_copy(
            weight_hbm.at[expert, k, pl.ds(n * step, step)],
            out_ref.at[k, pl.ds(n * step, step)],
            sems.at[k * pieces + n],
        )
        for k in range(2)
        for n in range(pieces)
    ]
    for copy in copies:
        copy.start()
    for copy in copies:
        copy.wait()


def load(weight, expert, after, limit):
    pieces = 8
    return pl.pallas_call(
        functools.partial(load_kernel, expert, pieces),
        in_specs=[pl.BlockSpec(memory_space=pl.ANY)] * (1 + len(after)),
        out_specs=pl.BlockSpec(memory_space=pltpu.VMEM),
        out_shape=jax.ShapeDtypeStruct(weight.shape[1:], weight.dtype),
        scratch_shapes=[pltpu.SemaphoreType.DMA((2 * pieces,))],
        compiler_params=params(limit),
        cost_estimate=pl.CostEstimate(flops=10**8, bytes_accessed=0, transcendentals=0),
        name="load",
    )(weight, *after)


def gate_up_kernel(experts, afters, chunk, rows_ref, *refs):
    weight_refs, out_refs = refs[:experts], refs[experts + afters:]
    out_ref = out_refs[0]
    if len(out_refs) > 1:
        out_refs[1][...] = jnp.zeros_like(out_refs[1])
    ff = out_ref.shape[2] // 2
    columns = pl.ds(pl.multiple_of(chunk[0] * ff, ff), ff)
    for x in range(experts):
        for k in range(2):
            out_ref[x, :, k * ff:(k + 1) * ff] = jnp.dot(
                rows_ref[x], weight_refs[x][k, :, columns], preferred_element_type=jnp.float32
            ).astype(out_ref.dtype)


def gate_up(chunk, chunks, rows, weights, dtype, done=False, after=()):
    experts, count, _ = rows.shape
    ff = weights[0].shape[2] // chunks
    return call(
        functools.partial(gate_up_kernel, experts, len(after)),
        [chunk],
        [rows, *weights],
        [jax.ShapeDtypeStruct((experts, count, 2 * ff), dtype)]
        + [jax.ShapeDtypeStruct((8, LANES), jnp.float32)] * done,
        "gate_up",
        24,
        after=after,
        cost=2,
    )


def activate_kernel(own_ref, *refs):
    other_refs, out_ref = refs[:-2], refs[-1]
    ff = out_ref.shape[2]
    for x in range(out_ref.shape[0]):
        total = own_ref[x]
        for ref in other_refs:
            total = total + ref[x].astype(jnp.float32)
        gate, up = total[:, :ff], total[:, ff:]
        out_ref[x] = (gate / (1.0 + jnp.exp(-gate)) * up).astype(out_ref.dtype)


def down_product(part_ref, weight_ref, x, chunk):
    ff = part_ref.shape[2]
    rows = pl.ds(pl.multiple_of(chunk * ff, ff), ff)
    return jnp.dot(part_ref[x], weight_ref[x, rows], preferred_element_type=jnp.float32)


def down_first_kernel(me, part_ref, weight_ref, sum_ref):
    for x in range(part_ref.shape[0]):
        sum_ref[x] = down_product(part_ref, weight_ref, x, me[0])


def down_more_kernel(index, me, before_ref, part_ref, weight_ref, sum_ref):
    for x in range(part_ref.shape[0]):
        sum_ref[x] = before_ref[x] + down_product(part_ref, weight_ref, x, me[0] ^ index)


def down_rest_kernel(indices, me, sum_ref, *refs):
    count = len(indices)
    parts, weight_ref, out_refs = refs[:count], refs[count], refs[count + 1:]
    experts, slots, _ = sum_ref.shape
    sums = []
    for x in range(experts):
        total = sum_ref[x]
        for part_ref, index in zip(parts, indices):
            total = total + down_product(part_ref, weight_ref, x, me[0] ^ index)
        sums.append(total.astype(jnp.bfloat16))
    owners = len(out_refs)
    rows = experts * slots // owners
    moved = lax.dot_general(
        regroup(experts, owners, slots // owners),
        jnp.concatenate(sums, axis=0),
        (((0,), (0,)), ((), ())),
        preferred_element_type=jnp.float32,
    )
    for t, out_ref in enumerate(out_refs):
        out_ref[...] = moved[t * rows:(t + 1) * rows].astype(out_ref.dtype)


def traded(value, axis, index):
    return lax.ppermute(value, axis, [(i, i ^ index) for i in range(lax.axis_size(axis))])


def trade(values, axis):
    out = [values[0]] + [None] * (len(values) - 1)
    for s in reversed(range(1, len(values))):
        out[s] = traded(values[s], axis, s)
    return out


def call(kernel, index, inputs, outputs, name, limit=16, after=(), cost=0):
    single = not isinstance(outputs, list)
    return pl.pallas_call(
        kernel,
        in_specs=[pl.BlockSpec(memory_space=pltpu.SMEM)] * len(index)
        + [pl.BlockSpec(memory_space=pltpu.VMEM)] * len(inputs)
        + [pl.BlockSpec(memory_space=pl.ANY)] * len(after),
        out_specs=pl.BlockSpec(memory_space=pltpu.VMEM)
        if single
        else [pl.BlockSpec(memory_space=pltpu.VMEM)] * len(outputs),
        out_shape=outputs,
        compiler_params=params(limit),
        cost_estimate=pl.CostEstimate(
            flops=cost * 10**9, bytes_accessed=0, transcendentals=0
        ),
        name=name,
    )(*index, *inputs, *after)


def experts_by_columns(held, loaded, down_weight, owners, attention):
    inner = lax.axis_size("inner")
    experts, count, _ = held.shape
    ff, width = down_weight.shape[1:]
    me = lax.axis_index("inner").astype(jnp.int32)
    level = me.reshape(1)
    others, last = [], []
    for s in reversed(range(1, inner)):
        last = gate_up(
            (me ^ s).reshape(1), inner, held, loaded, jnp.bfloat16, after=last
        )
        others.append(traded(last[0], "inner", s))
    own, done = gate_up(level, inner, held, loaded, jnp.float32, True, last)
    attended = attention(done)
    active = call(
        activate_kernel,
        [],
        [own, *others],
        jax.ShapeDtypeStruct((experts, count, ff // inner), jnp.bfloat16),
        "activate",
        after=[attended],
    )
    parts = trade([active] * inner, "inner")
    sums_shape = jax.ShapeDtypeStruct((experts, count, width), jnp.float32)
    sums = call(down_first_kernel, [level], [active, down_weight], sums_shape, "down_first", 24)
    sums = call(
        functools.partial(down_more_kernel, 1),
        [level],
        [sums, parts[1], down_weight],
        sums_shape,
        "down_more",
        24,
    )
    back = call(
        functools.partial(down_rest_kernel, list(range(2, inner))),
        [level],
        [sums, *parts[2:], down_weight],
        [jax.ShapeDtypeStruct((experts * count // owners, width), jnp.bfloat16)] * owners,
        "down_rest",
        24,
    )
    return back, attended


def experts_by_rows(held, gate_up_weight, down_weight, owners, attention):
    experts, count, _ = held.shape
    partial = jnp.einsum("xsd,xkdf->sxkf", held, gate_up_weight, preferred_element_type=jnp.float32)
    summed = lax.psum_scatter(partial, "inner", scatter_dimension=0, tiled=True)
    active = (jax.nn.silu(summed[:, :, 0]) * summed[:, :, 1]).astype(jnp.bfloat16)
    active = lax.all_gather(active, "inner", axis=0, tiled=True)
    outputs = jnp.einsum("sxf,xfd->xsd", active, down_weight, preferred_element_type=jnp.float32)
    outputs = outputs.astype(jnp.bfloat16).reshape(experts, owners, count // owners, -1)
    back = [outputs[:, t].reshape(experts * count // owners, -1) for t in range(owners)]
    return back, attention(held)


def body(
    queries,
    new_key_value,
    cached_key_value,
    parents,
    hidden,
    routes,
    gate_values,
    gate_up_weight,
    down_weight,
):
    owners, inner = lax.axis_size("expert"), lax.axis_size("inner")
    experts, _, depth, ff = gate_up_weight.shape
    rows, model = hidden.shape
    width = down_weight.shape[2]
    top = routes.shape[1]
    column = lax.axis_index("expert").astype(jnp.int32).reshape(1)
    level = lax.axis_index("inner").astype(jnp.int32).reshape(1)
    slots = experts * CAP * inner

    attention = functools.partial(attend, queries, new_key_value, cached_key_value, parents)

    slices = call(
        prepare_kernel,
        [level],
        [routes.T, gate_values.T, hidden],
        [jax.ShapeDtypeStruct((rows, depth + LANES), jnp.bfloat16)] * inner,
        "prepare",
    )
    even = ff % (inner * LANES) == 0
    loaded = [load(gate_up_weight, 0, slices[:1], 45)] if even else []
    slices = trade(slices, "inner")
    packs = call(
        functools.partial(pack_kernel, top, experts, inner, len(loaded)),
        [column, level],
        slices,
        [jax.ShapeDtypeStruct((slots, depth), jnp.bfloat16)] * owners,
        "pack",
        after=loaded,
    )
    if even:
        for x in range(1, experts):
            loaded = loaded + [load(gate_up_weight, x, [packs[0], *loaded], 40)]
    packs = trade(packs, "expert")
    held = call(
        functools.partial(select_kernel, owners),
        [],
        packs,
        jax.ShapeDtypeStruct((experts, owners * CAP * inner, depth), jnp.bfloat16),
        "select",
        24,
        after=loaded,
    )
    back, attended = (experts_by_columns if even else experts_by_rows)(
        held, loaded or gate_up_weight, down_weight, owners, attention
    )
    back = trade(back, "expert")
    weights = call(
        functools.partial(weigh_kernel, top, experts),
        [column, level],
        slices,
        jax.ShapeDtypeStruct((owners, slots, inner * rows), jnp.bfloat16),
        "weigh",
        cost=1,
    )
    pieces = call(
        combine_kernel,
        [],
        [weights, *back],
        [jax.ShapeDtypeStruct((rows, width), jnp.bfloat16)] * inner,
        "combine",
    )
    pieces = trade(pieces, "inner")
    expert_out = call(
        assemble_kernel,
        [level],
        pieces,
        jax.ShapeDtypeStruct((rows, model), jnp.bfloat16),
        "assemble",
    )
    return attended.reshape(rows, QUERY_HEADS * HEAD_SIZE), expert_out


def solution(mesh):
    rows = ("groups", "expert", "inner")
    return jax.shard_map(
        body,
        mesh=mesh,
        in_specs=(
            P(rows, None),
            P(rows, None),
            P(rows, None, None, None),
            P(rows, None),
            P(rows, None),
            P(rows, None),
            P(rows, None),
            P("expert", None, "inner", None),
            P("expert", None, "inner"),
        ),
        out_specs=(P(rows, None), P(rows, None)),
        check_vma=False,
    )
```

```python
import functools
import math

import jax
import jax.numpy as jnp
from jax import lax
from jax.experimental import pallas as pl
from jax.experimental.pallas import tpu as pltpu
from jax.sharding import PartitionSpec as P

QUERY_HEADS = 64
KEY_HEADS = 4
HEAD_SIZE = 128
CAP = 3
LANES = 128


def params(limit, *semantics):
    return pltpu.CompilerParams(
        dimension_semantics=semantics or None, vmem_limit_bytes=limit * 1024 * 1024
    )


def attend_kernel(
    parents, q_ref, new_ref, cache_ref, after_ref, out_ref, done_ref, q_rows, new_rows, out_rows
):
    del after_ref
    done_ref[...] = jnp.zeros_like(done_ref)
    group = QUERY_HEADS // KEY_HEADS
    scale = 1.0 / math.sqrt(HEAD_SIZE)
    width = KEY_HEADS * HEAD_SIZE
    count, beams = q_ref.shape[0], cache_ref.shape[1]
    for h in range(QUERY_HEADS):
        q_rows[h * count:(h + 1) * count] = q_ref[
            :, h * HEAD_SIZE:(h + 1) * HEAD_SIZE
        ].astype(jnp.float32)
    for h in range(2 * KEY_HEADS):
        new_rows[h * count:(h + 1) * count] = new_ref[
            :, h * HEAD_SIZE:(h + 1) * HEAD_SIZE
        ].astype(jnp.float32)
    for r in range(count):
        request, parent = r // beams, parents[r]
        q = q_rows[pl.ds(r, QUERY_HEADS, stride=count), :]
        fresh = new_rows[pl.ds(r, 2 * KEY_HEADS, stride=count), :]
        scores, own = [], []
        for k in range(KEY_HEADS):
            qk = q[k * group:(k + 1) * group]
            keys = cache_ref[request, parent, :, k * HEAD_SIZE:(k + 1) * HEAD_SIZE]
            scores.append(
                lax.dot_general(
                    qk.astype(jnp.bfloat16),
                    keys,
                    (((1,), (1,)), ((), ())),
                    preferred_element_type=jnp.float32,
                )
            )
            own.append(jnp.sum(qk * fresh[k:k + 1], axis=-1, keepdims=True))
        scores = jnp.concatenate(scores, axis=0) * scale
        own = jnp.concatenate(own, axis=0) * scale
        upper = jnp.maximum(jnp.max(scores, axis=-1, keepdims=True), own)
        expo = jnp.exp(scores - upper)
        own_expo = jnp.exp(own - upper)
        total = jnp.sum(expo, axis=-1, keepdims=True) + own_expo
        probs = (expo / total).astype(jnp.bfloat16)
        own_prob = (own_expo / total).astype(jnp.bfloat16).astype(jnp.float32)
        for k in range(KEY_HEADS):
            heads = slice(k * group, (k + 1) * group)
            columns = slice(width + k * HEAD_SIZE, width + (k + 1) * HEAD_SIZE)
            result = jnp.dot(
                probs[heads], cache_ref[request, parent, :, columns], preferred_element_type=jnp.float32
            )
            out_rows[pl.ds(k * group * count + r, group, stride=count), :] = (
                result + own_prob[heads] * fresh[KEY_HEADS + k:KEY_HEADS + k + 1]
            )
    for h in range(QUERY_HEADS):
        out_ref[:, h * HEAD_SIZE:(h + 1) * HEAD_SIZE] = out_rows[
            h * count:(h + 1) * count
        ].astype(out_ref.dtype)


def attend(queries, new_key_value, cached_key_value, parents, after):
    rows = queries.shape[0]
    _, _, length, width = cached_key_value.shape
    vmem = pl.BlockSpec(memory_space=pltpu.VMEM)
    return pl.pallas_call(
        attend_kernel,
        in_specs=[pl.BlockSpec(memory_space=pltpu.SMEM), vmem, vmem, vmem]
        + [pl.BlockSpec(memory_space=pl.ANY)],
        out_specs=[vmem, vmem],
        out_shape=[
            jax.ShapeDtypeStruct(queries.shape, queries.dtype),
            jax.ShapeDtypeStruct((8, LANES), jnp.float32),
        ],
        scratch_shapes=[
            pltpu.VMEM((QUERY_HEADS * rows, HEAD_SIZE), jnp.float32),
            pltpu.VMEM((2 * KEY_HEADS * rows, HEAD_SIZE), jnp.float32),
            pltpu.VMEM((QUERY_HEADS * rows, HEAD_SIZE), jnp.float32),
        ],
        compiler_params=params(32),
        cost_estimate=pl.CostEstimate(
            flops=4 * rows * QUERY_HEADS * HEAD_SIZE * length,
            bytes_accessed=2 * rows * length * width,
            transcendentals=rows * QUERY_HEADS * length,
        ),
        name="attend",
    )(parents.reshape(rows), queries, new_key_value, cached_key_value, after)


def spread(values, lanes, first):
    top = values.shape[0]
    shape = (top, lanes)
    chosen = (
        lax.broadcasted_iota(jnp.int32, shape, 1)
        == lax.broadcasted_iota(jnp.int32, shape, 0) + first
    ).astype(jnp.float32)
    return lax.dot_general(
        values.astype(jnp.float32), chosen, (((0,), (0,)), ((), ())), preferred_element_type=jnp.float32
    )


def prepare_kernel(me, routes_ref, gates_ref, hidden_ref, *out_refs):
    width = hidden_ref.shape[1] // len(out_refs)
    top = routes_ref.shape[0]
    notes = spread(routes_ref[...], LANES, 0) + spread(gates_ref[...], LANES, top)
    notes = notes.astype(jnp.bfloat16)
    for s, out_ref in enumerate(out_refs):
        start = pl.multiple_of((me[0] ^ s) * width, width)
        out_ref[:, :width] = hidden_ref[:, pl.ds(start, width)]
        out_ref[:, width:] = notes


def turned_notes(notes, top):
    shape = (max(8, 2 * top), LANES)
    chosen = (
        lax.broadcasted_iota(jnp.int32, shape, 0) == lax.broadcasted_iota(jnp.int32, shape, 1)
    ).astype(jnp.bfloat16)
    turned = lax.dot_general(
        chosen, notes, (((1,), (1,)), ((), ())), preferred_element_type=jnp.float32
    )
    return turned[:top], turned[top:2 * top]


def placing(routes, column, level, owners, experts, sources):
    top, rows = routes.shape
    count = CAP * sources
    shape = (owners * experts * count, rows)
    slot = lax.broadcasted_iota(jnp.int32, shape, 0)
    row = lax.broadcasted_iota(jnp.int32, shape, 1)
    each = rows // sources
    block = jnp.zeros(shape, jnp.int32)
    for n in range(1, owners * experts):
        block = block + (slot >= n * count).astype(jnp.int32)
    within = slot - block * count
    rank, source = within // sources, within % sources
    expert = ((column ^ (block // experts)) * experts + block % experts).astype(jnp.float32)
    member = jnp.zeros(shape, jnp.float32)
    for t in range(top):
        member = jnp.where(routes[t:t + 1] == expert, 1.0, member)
    origin = level ^ (row // each)
    member = jnp.where(origin == source, member, 0.0)
    one = lax.broadcasted_iota(jnp.int32, (rows, rows), 0)
    other = lax.broadcasted_iota(jnp.int32, (rows, rows), 1)
    before = (one < other).astype(jnp.float32)
    ranks = jnp.dot(member, before, preferred_element_type=jnp.float32)
    return jnp.where(ranks == rank.astype(jnp.float32), member, 0.0), expert


def pack_kernel(top, experts, sources, afters, column, level, *refs):
    held, out_refs = refs[:sources], refs[sources + afters:]
    slots, width = out_refs[0].shape
    rows = jnp.concatenate([ref[:, :width] for ref in held], axis=0)
    notes = jnp.concatenate([ref[:, width:] for ref in held], axis=0)
    routes, _ = turned_notes(notes, top)
    place, _ = placing(routes, column[0], level[0], len(out_refs), experts, sources)
    moved = jnp.dot(place.astype(jnp.bfloat16), rows, preferred_element_type=jnp.float32)
    for t, out_ref in enumerate(out_refs):
        out_ref[...] = moved[t * slots:(t + 1) * slots].astype(out_ref.dtype)


def weigh_kernel(top, experts, column, level, *refs):
    held, out_ref = refs[:-1], refs[-1]
    owners, slots, _ = out_ref.shape
    notes = jnp.concatenate([ref[:, -LANES:] for ref in held], axis=0)
    routes, gates = turned_notes(notes, top)
    place, expert = placing(routes, column[0], level[0], owners, experts, len(held))
    weight = jnp.zeros_like(place)
    for k in range(top):
        weight = weight + jnp.where(routes[k:k + 1] == expert, gates[k:k + 1], 0.0)
    weight = weight * place
    for t in range(owners):
        out_ref[t] = weight[t * slots:(t + 1) * slots].astype(out_ref.dtype)


def combine_kernel(weight_ref, *refs):
    owners = weight_ref.shape[0]
    back, out_refs = refs[:owners], refs[owners:]
    each = out_refs[0].shape[0]
    total = 0.0
    for t in range(owners):
        total = total + lax.dot_general(
            weight_ref[t],
            back[t][...],
            (((0,), (0,)), ((), ())),
            preferred_element_type=jnp.float32,
        )
    for s, out_ref in enumerate(out_refs):
        out_ref[...] = total[s * each:(s + 1) * each].astype(out_ref.dtype)


def assemble_kernel(me, *refs):
    pieces, out_ref = refs[:-1], refs[-1]
    width = pieces[0].shape[1]
    for s, piece in enumerate(pieces):
        start = pl.multiple_of((me[0] ^ s) * width, width)
        out_ref[:, pl.ds(start, width)] = piece[...]


def regroup(experts, owners, count):
    shape = (experts * owners * count, owners * experts * count)
    row = lax.broadcasted_iota(jnp.int32, shape, 0)
    other = lax.broadcasted_iota(jnp.int32, shape, 1)
    wanted = jnp.zeros(shape, jnp.int32) + row
    for x in range(experts):
        for t in range(owners):
            first = (x * owners + t) * count
            inside = (row >= first) & (row < first + count)
            wanted = jnp.where(inside, row - first + (t * experts + x) * count, wanted)
    return (other == wanted).astype(jnp.bfloat16)


def select_kernel(owners, *refs):
    packs, out_ref = refs[:owners], refs[-1]
    experts, count, _ = out_ref.shape
    rows = jnp.concatenate([ref[...].astype(jnp.float32) for ref in packs], axis=0)
    moved = jnp.dot(
        regroup(experts, len(packs), count // len(packs)),
        rows.astype(jnp.bfloat16),
        preferred_element_type=jnp.float32,
    ).astype(out_ref.dtype)
    for x in range(experts):
        out_ref[x] = moved[x * count:(x + 1) * count]


def load_kernel(expert, pieces, weight_hbm, *refs):
    out_ref, sems = refs[-2:]
    step = out_ref.shape[1] // pieces
    copies = [
        pltpu.make_async_copy(
            weight_hbm.at[expert, k, pl.ds(n * step, step)],
            out_ref.at[k, pl.ds(n * step, step)],
            sems.at[k * pieces + n],
        )
        for k in range(2)
        for n in range(pieces)
    ]
    for copy in copies:
        copy.start()
    for copy in copies:
        copy.wait()


def load(weight, expert, after, limit):
    pieces = 8
    return pl.pallas_call(
        functools.partial(load_kernel, expert, pieces),
        in_specs=[pl.BlockSpec(memory_space=pl.ANY)] * (1 + len(after)),
        out_specs=pl.BlockSpec(memory_space=pltpu.VMEM),
        out_shape=jax.ShapeDtypeStruct(weight.shape[1:], weight.dtype),
        scratch_shapes=[pltpu.SemaphoreType.DMA((2 * pieces,))],
        compiler_params=params(limit),
        cost_estimate=pl.CostEstimate(flops=10**8, bytes_accessed=0, transcendentals=0),
        name="load",
    )(weight, *after)


def gate_up_kernel(experts, afters, chunk, rows_ref, *refs):
    weight_refs, out_refs = refs[:experts], refs[experts + afters:]
    out_ref = out_refs[0]
    if len(out_refs) > 1:
        out_refs[1][...] = jnp.zeros_like(out_refs[1])
    ff = out_ref.shape[2] // 2
    columns = pl.ds(pl.multiple_of(chunk[0] * ff, ff), ff)
    for x in range(experts):
        for k in range(2):
            out_ref[x, :, k * ff:(k + 1) * ff] = jnp.dot(
                rows_ref[x], weight_refs[x][k, :, columns], preferred_element_type=jnp.float32
            ).astype(out_ref.dtype)


def gate_up(chunk, chunks, rows, weights, dtype, done=False, after=()):
    experts, count, _ = rows.shape
    ff = weights[0].shape[2] // chunks
    return call(
        functools.partial(gate_up_kernel, experts, len(after)),
        [chunk],
        [rows, *weights],
        [jax.ShapeDtypeStruct((experts, count, 2 * ff), dtype)]
        + [jax.ShapeDtypeStruct((8, LANES), jnp.float32)] * done,
        "gate_up",
        24,
        after=after,
        cost=2,
    )


def activate_kernel(own_ref, *refs):
    other_refs, out_ref = refs[:-2], refs[-1]
    ff = out_ref.shape[2]
    for x in range(out_ref.shape[0]):
        total = own_ref[x]
        for ref in other_refs:
            total = total + ref[x].astype(jnp.float32)
        gate, up = total[:, :ff], total[:, ff:]
        out_ref[x] = (gate / (1.0 + jnp.exp(-gate)) * up).astype(out_ref.dtype)


def down_product(part_ref, weight_ref, x, chunk):
    ff = part_ref.shape[2]
    rows = pl.ds(pl.multiple_of(chunk * ff, ff), ff)
    return jnp.dot(part_ref[x], weight_ref[x, rows], preferred_element_type=jnp.float32)


def down_first_kernel(me, part_ref, weight_ref, sum_ref):
    for x in range(part_ref.shape[0]):
        sum_ref[x] = down_product(part_ref, weight_ref, x, me[0])


def down_more_kernel(index, me, before_ref, part_ref, weight_ref, sum_ref):
    for x in range(part_ref.shape[0]):
        sum_ref[x] = before_ref[x] + down_product(part_ref, weight_ref, x, me[0] ^ index)


def down_rest_kernel(indices, me, sum_ref, *refs):
    count = len(indices)
    parts, weight_ref, out_refs = refs[:count], refs[count], refs[count + 1:]
    experts, slots, _ = sum_ref.shape
    sums = []
    for x in range(experts):
        total = sum_ref[x]
        for part_ref, index in zip(parts, indices):
            total = total + down_product(part_ref, weight_ref, x, me[0] ^ index)
        sums.append(total.astype(jnp.bfloat16))
    owners = len(out_refs)
    rows = experts * slots // owners
    moved = lax.dot_general(
        regroup(experts, owners, slots // owners),
        jnp.concatenate(sums, axis=0),
        (((0,), (0,)), ((), ())),
        preferred_element_type=jnp.float32,
    )
    for t, out_ref in enumerate(out_refs):
        out_ref[...] = moved[t * rows:(t + 1) * rows].astype(out_ref.dtype)


def traded(value, axis, index):
    return lax.ppermute(value, axis, [(i, i ^ index) for i in range(lax.axis_size(axis))])


def trade(values, axis):
    out = [values[0]] + [None] * (len(values) - 1)
    for s in reversed(range(1, len(values))):
        out[s] = traded(values[s], axis, s)
    return out


def call(kernel, index, inputs, outputs, name, limit=16, after=(), cost=0):
    single = not isinstance(outputs, list)
    return pl.pallas_call(
        kernel,
        in_specs=[pl.BlockSpec(memory_space=pltpu.SMEM)] * len(index)
        + [pl.BlockSpec(memory_space=pltpu.VMEM)] * len(inputs)
        + [pl.BlockSpec(memory_space=pl.ANY)] * len(after),
        out_specs=pl.BlockSpec(memory_space=pltpu.VMEM)
        if single
        else [pl.BlockSpec(memory_space=pltpu.VMEM)] * len(outputs),
        out_shape=outputs,
        compiler_params=params(limit),
        cost_estimate=pl.CostEstimate(
            flops=cost * 10**9, bytes_accessed=0, transcendentals=0
        ),
        name=name,
    )(*index, *inputs, *after)


def experts_by_columns(held, loaded, down_weight, owners, attention):
    inner = lax.axis_size("inner")
    experts, count, _ = held.shape
    ff, width = down_weight.shape[1:]
    me = lax.axis_index("inner").astype(jnp.int32)
    level = me.reshape(1)
    others, last = [], []
    for s in reversed(range(1, inner)):
        last = gate_up(
            (me ^ s).reshape(1), inner, held, loaded, jnp.bfloat16, after=last
        )
        others.append(traded(last[0], "inner", s))
    own, done = gate_up(level, inner, held, loaded, jnp.float32, True, last)
    attended, done = attention(done)
    active = call(
        activate_kernel,
        [],
        [own, *others],
        jax.ShapeDtypeStruct((experts, count, ff // inner), jnp.bfloat16),
        "activate",
        after=[done],
    )
    parts = trade([active] * inner, "inner")
    sums_shape = jax.ShapeDtypeStruct((experts, count, width), jnp.float32)
    sums = call(down_first_kernel, [level], [active, down_weight], sums_shape, "down_first", 24)
    sums = call(
        functools.partial(down_more_kernel, 1),
        [level],
        [sums, parts[1], down_weight],
        sums_shape,
        "down_more",
        24,
    )
    back = call(
        functools.partial(down_rest_kernel, list(range(2, inner))),
        [level],
        [sums, *parts[2:], down_weight],
        [jax.ShapeDtypeStruct((experts * count // owners, width), jnp.bfloat16)] * owners,
        "down_rest",
        24,
    )
    return back, attended


def experts_by_rows(held, gate_up_weight, down_weight, owners, attention):
    experts, count, _ = held.shape
    partial = jnp.einsum("xsd,xkdf->sxkf", held, gate_up_weight, preferred_element_type=jnp.float32)
    summed = lax.psum_scatter(partial, "inner", scatter_dimension=0, tiled=True)
    active = (jax.nn.silu(summed[:, :, 0]) * summed[:, :, 1]).astype(jnp.bfloat16)
    active = lax.all_gather(active, "inner", axis=0, tiled=True)
    outputs = jnp.einsum("sxf,xfd->xsd", active, down_weight, preferred_element_type=jnp.float32)
    outputs = outputs.astype(jnp.bfloat16).reshape(experts, owners, count // owners, -1)
    back = [outputs[:, t].reshape(experts * count // owners, -1) for t in range(owners)]
    return back, attention(held)[0]


def body(
    queries,
    new_key_value,
    cached_key_value,
    parents,
    hidden,
    routes,
    gate_values,
    gate_up_weight,
    down_weight,
):
    owners, inner = lax.axis_size("expert"), lax.axis_size("inner")
    experts, _, depth, ff = gate_up_weight.shape
    rows, model = hidden.shape
    width = down_weight.shape[2]
    top = routes.shape[1]
    column = lax.axis_index("expert").astype(jnp.int32).reshape(1)
    level = lax.axis_index("inner").astype(jnp.int32).reshape(1)
    slots = experts * CAP * inner

    attention = functools.partial(attend, queries, new_key_value, cached_key_value, parents)

    slices = call(
        prepare_kernel,
        [level],
        [routes.T, gate_values.T, hidden],
        [jax.ShapeDtypeStruct((rows, depth + LANES), jnp.bfloat16)] * inner,
        "prepare",
    )
    even = ff % (inner * LANES) == 0
    loaded = [load(gate_up_weight, 0, slices[:1], 45)] if even else []
    slices = trade(slices, "inner")
    packs = call(
        functools.partial(pack_kernel, top, experts, inner, len(loaded)),
        [column, level],
        slices,
        [jax.ShapeDtypeStruct((slots, depth), jnp.bfloat16)] * owners,
        "pack",
        after=loaded,
    )
    if even:
        for x in range(1, experts):
            loaded = loaded + [load(gate_up_weight, x, [packs[0], *loaded], 40)]
    packs = trade(packs, "expert")
    held = call(
        functools.partial(select_kernel, owners),
        [],
        packs,
        jax.ShapeDtypeStruct((experts, owners * CAP * inner, depth), jnp.bfloat16),
        "select",
        24,
        after=loaded,
    )
    back, attended = (experts_by_columns if even else experts_by_rows)(
        held, loaded or gate_up_weight, down_weight, owners, attention
    )
    back = trade(back, "expert")
    weights = call(
        functools.partial(weigh_kernel, top, experts),
        [column, level],
        slices,
        jax.ShapeDtypeStruct((owners, slots, inner * rows), jnp.bfloat16),
        "weigh",
        cost=1,
    )
    pieces = call(
        combine_kernel,
        [],
        [weights, *back],
        [jax.ShapeDtypeStruct((rows, width), jnp.bfloat16)] * inner,
        "combine",
    )
    pieces = trade(pieces, "inner")
    expert_out = call(
        assemble_kernel,
        [level],
        pieces,
        jax.ShapeDtypeStruct((rows, model), jnp.bfloat16),
        "assemble",
    )
    return attended, expert_out


def solution(mesh):
    rows = ("groups", "expert", "inner")
    return jax.shard_map(
        body,
        mesh=mesh,
        in_specs=(
            P(rows, None),
            P(rows, None),
            P(rows, None, None, None),
            P(rows, None),
            P(rows, None),
            P(rows, None),
            P(rows, None),
            P("expert", None, "inner", None),
            P("expert", None, "inner"),
        ),
        out_specs=(P(rows, None), P(rows, None)),
        check_vma=False,
    )
```

```python
import functools
import math

import jax
import jax.numpy as jnp
from jax import lax
from jax.experimental import pallas as pl
from jax.experimental.pallas import tpu as pltpu
from jax.sharding import PartitionSpec as P

QUERY_HEADS = 64
KEY_HEADS = 4
HEAD_SIZE = 128
CAP = 3
LANES = 128


def params(limit, *semantics):
    return pltpu.CompilerParams(
        dimension_semantics=semantics or None, vmem_limit_bytes=limit * 1024 * 1024
    )


def attend_kernel(
    parents, q_ref, new_ref, cache_ref, after_ref, out_ref, done_ref, q_rows, new_rows, out_rows
):
    del after_ref
    done_ref[...] = jnp.zeros_like(done_ref)
    group = QUERY_HEADS // KEY_HEADS
    scale = 1.0 / math.sqrt(HEAD_SIZE)
    width = KEY_HEADS * HEAD_SIZE
    count, beams = q_ref.shape[0], cache_ref.shape[1]
    for h in range(QUERY_HEADS):
        q_rows[h * count:(h + 1) * count] = q_ref[
            :, h * HEAD_SIZE:(h + 1) * HEAD_SIZE
        ].astype(jnp.float32)
    for h in range(2 * KEY_HEADS):
        new_rows[h * count:(h + 1) * count] = new_ref[
            :, h * HEAD_SIZE:(h + 1) * HEAD_SIZE
        ].astype(jnp.float32)
    for r in range(count):
        request, parent = r // beams, parents[r]
        q = q_rows[pl.ds(r, QUERY_HEADS, stride=count), :]
        fresh = new_rows[pl.ds(r, 2 * KEY_HEADS, stride=count), :]
        scores, own = [], []
        for k in range(KEY_HEADS):
            qk = q[k * group:(k + 1) * group]
            keys = cache_ref[request, parent, :, k * HEAD_SIZE:(k + 1) * HEAD_SIZE]
            scores.append(
                lax.dot_general(
                    qk.astype(jnp.bfloat16),
                    keys,
                    (((1,), (1,)), ((), ())),
                    preferred_element_type=jnp.float32,
                )
            )
            own.append(jnp.sum(qk * fresh[k:k + 1], axis=-1, keepdims=True))
        scores = jnp.concatenate(scores, axis=0) * scale
        own = jnp.concatenate(own, axis=0) * scale
        upper = jnp.maximum(jnp.max(scores, axis=-1, keepdims=True), own)
        expo = jnp.exp(scores - upper)
        own_expo = jnp.exp(own - upper)
        total = jnp.sum(expo, axis=-1, keepdims=True) + own_expo
        probs = (expo / total).astype(jnp.bfloat16)
        own_prob = (own_expo / total).astype(jnp.bfloat16).astype(jnp.float32)
        for k in range(KEY_HEADS):
            heads = slice(k * group, (k + 1) * group)
            columns = slice(width + k * HEAD_SIZE, width + (k + 1) * HEAD_SIZE)
            result = jnp.dot(
                probs[heads], cache_ref[request, parent, :, columns], preferred_element_type=jnp.float32
            )
            out_rows[pl.ds(k * group * count + r, group, stride=count), :] = (
                result + own_prob[heads] * fresh[KEY_HEADS + k:KEY_HEADS + k + 1]
            )
    for h in range(QUERY_HEADS):
        out_ref[:, h * HEAD_SIZE:(h + 1) * HEAD_SIZE] = out_rows[
            h * count:(h + 1) * count
        ].astype(out_ref.dtype)


def attend(queries, new_key_value, cached_key_value, parents, after):
    rows = queries.shape[0]
    _, _, length, width = cached_key_value.shape
    vmem = pl.BlockSpec(memory_space=pltpu.VMEM)
    return pl.pallas_call(
        attend_kernel,
        in_specs=[pl.BlockSpec(memory_space=pltpu.SMEM), vmem, vmem, vmem]
        + [pl.BlockSpec(memory_space=pl.ANY)],
        out_specs=[vmem, vmem],
        out_shape=[
            jax.ShapeDtypeStruct(queries.shape, queries.dtype),
            jax.ShapeDtypeStruct((8, LANES), jnp.float32),
        ],
        scratch_shapes=[
            pltpu.VMEM((QUERY_HEADS * rows, HEAD_SIZE), jnp.float32),
            pltpu.VMEM((2 * KEY_HEADS * rows, HEAD_SIZE), jnp.float32),
            pltpu.VMEM((QUERY_HEADS * rows, HEAD_SIZE), jnp.float32),
        ],
        compiler_params=params(32),
        cost_estimate=pl.CostEstimate(
            flops=4 * rows * QUERY_HEADS * HEAD_SIZE * length,
            bytes_accessed=2 * rows * length * width,
            transcendentals=rows * QUERY_HEADS * length,
        ),
        name="attend",
    )(parents.reshape(rows), queries, new_key_value, cached_key_value, after)


def spread(values, lanes, first):
    top = values.shape[0]
    shape = (top, lanes)
    chosen = (
        lax.broadcasted_iota(jnp.int32, shape, 1)
        == lax.broadcasted_iota(jnp.int32, shape, 0) + first
    ).astype(jnp.float32)
    return lax.dot_general(
        values.astype(jnp.float32), chosen, (((0,), (0,)), ((), ())), preferred_element_type=jnp.float32
    )


def prepare_kernel(me, routes_ref, gates_ref, hidden_ref, *out_refs):
    width = hidden_ref.shape[1] // len(out_refs)
    top = routes_ref.shape[0]
    notes = spread(routes_ref[...], LANES, 0) + spread(gates_ref[...], LANES, top)
    notes = notes.astype(jnp.bfloat16)
    for s, out_ref in enumerate(out_refs):
        start = pl.multiple_of((me[0] ^ s) * width, width)
        out_ref[:, :width] = hidden_ref[:, pl.ds(start, width)]
        out_ref[:, width:] = notes


def turned_notes(notes, top):
    shape = (max(8, 2 * top), LANES)
    chosen = (
        lax.broadcasted_iota(jnp.int32, shape, 0) == lax.broadcasted_iota(jnp.int32, shape, 1)
    ).astype(jnp.bfloat16)
    turned = lax.dot_general(
        chosen, notes, (((1,), (1,)), ((), ())), preferred_element_type=jnp.float32
    )
    return turned[:top], turned[top:2 * top]


def placing(routes, column, level, owners, experts, sources):
    top, rows = routes.shape
    count = CAP * sources
    shape = (owners * experts * count, rows)
    slot = lax.broadcasted_iota(jnp.int32, shape, 0)
    row = lax.broadcasted_iota(jnp.int32, shape, 1)
    each = rows // sources
    block = jnp.zeros(shape, jnp.int32)
    for n in range(1, owners * experts):
        block = block + (slot >= n * count).astype(jnp.int32)
    within = slot - block * count
    rank, source = within // sources, within % sources
    expert = ((column ^ (block // experts)) * experts + block % experts).astype(jnp.float32)
    member = jnp.zeros(shape, jnp.float32)
    for t in range(top):
        member = jnp.where(routes[t:t + 1] == expert, 1.0, member)
    origin = level ^ (row // each)
    member = jnp.where(origin == source, member, 0.0)
    one = lax.broadcasted_iota(jnp.int32, (rows, rows), 0)
    other = lax.broadcasted_iota(jnp.int32, (rows, rows), 1)
    before = (one < other).astype(jnp.float32)
    ranks = jnp.dot(member, before, preferred_element_type=jnp.float32)
    return jnp.where(ranks == rank.astype(jnp.float32), member, 0.0), expert


def pack_kernel(top, experts, sources, column, level, *refs):
    held, out_refs = refs[:sources], refs[sources:]
    slots, width = out_refs[0].shape
    rows = jnp.concatenate([ref[:, :width] for ref in held], axis=0)
    notes = jnp.concatenate([ref[:, width:] for ref in held], axis=0)
    routes, _ = turned_notes(notes, top)
    place, _ = placing(routes, column[0], level[0], len(out_refs), experts, sources)
    moved = jnp.dot(place.astype(jnp.bfloat16), rows, preferred_element_type=jnp.float32)
    for t, out_ref in enumerate(out_refs):
        out_ref[...] = moved[t * slots:(t + 1) * slots].astype(out_ref.dtype)


def weigh_kernel(top, experts, column, level, *refs):
    held, out_ref = refs[:-1], refs[-1]
    owners, slots, _ = out_ref.shape
    notes = jnp.concatenate([ref[:, -LANES:] for ref in held], axis=0)
    routes, gates = turned_notes(notes, top)
    place, expert = placing(routes, column[0], level[0], owners, experts, len(held))
    weight = jnp.zeros_like(place)
    for k in range(top):
        weight = weight + jnp.where(routes[k:k + 1] == expert, gates[k:k + 1], 0.0)
    weight = weight * place
    for t in range(owners):
        out_ref[t] = weight[t * slots:(t + 1) * slots].astype(out_ref.dtype)


def combine_kernel(weight_ref, *refs):
    owners = weight_ref.shape[0]
    back, out_refs = refs[:owners], refs[owners:]
    each = out_refs[0].shape[0]
    total = 0.0
    for t in range(owners):
        total = total + lax.dot_general(
            weight_ref[t],
            back[t][...],
            (((0,), (0,)), ((), ())),
            preferred_element_type=jnp.float32,
        )
    for s, out_ref in enumerate(out_refs):
        out_ref[...] = total[s * each:(s + 1) * each].astype(out_ref.dtype)


def assemble_kernel(me, *refs):
    pieces, out_ref = refs[:-1], refs[-1]
    width = pieces[0].shape[1]
    for s, piece in enumerate(pieces):
        start = pl.multiple_of((me[0] ^ s) * width, width)
        out_ref[:, pl.ds(start, width)] = piece[...]


def regroup(experts, owners, count):
    shape = (experts * owners * count, owners * experts * count)
    row = lax.broadcasted_iota(jnp.int32, shape, 0)
    other = lax.broadcasted_iota(jnp.int32, shape, 1)
    wanted = jnp.zeros(shape, jnp.int32) + row
    for x in range(experts):
        for t in range(owners):
            first = (x * owners + t) * count
            inside = (row >= first) & (row < first + count)
            wanted = jnp.where(inside, row - first + (t * experts + x) * count, wanted)
    return (other == wanted).astype(jnp.bfloat16)


def select_kernel(owners, *refs):
    packs, out_ref = refs[:owners], refs[-1]
    experts, count, _ = out_ref.shape
    rows = jnp.concatenate([ref[...].astype(jnp.float32) for ref in packs], axis=0)
    moved = jnp.dot(
        regroup(experts, len(packs), count // len(packs)),
        rows.astype(jnp.bfloat16),
        preferred_element_type=jnp.float32,
    ).astype(out_ref.dtype)
    for x in range(experts):
        out_ref[x] = moved[x * count:(x + 1) * count]


def load_kernel(pieces, weight_hbm, after_ref, *refs):
    del after_ref
    out_refs, done_ref, sems = refs[:-2], refs[-2], refs[-1]
    done_ref[...] = jnp.zeros_like(done_ref)
    step = weight_hbm.shape[2] // pieces
    copies = [
        pltpu.make_async_copy(
            weight_hbm.at[x, k, pl.ds(n * step, step)],
            out_ref.at[k, pl.ds(n * step, step)],
            sems.at[(x * 2 + k) * pieces + n],
        )
        for x, out_ref in enumerate(out_refs)
        for k in range(2)
        for n in range(pieces)
    ]
    for copy in copies:
        copy.start()
    for copy in copies:
        copy.wait()


def load(weight, after):
    experts, pieces = weight.shape[0], 4
    return pl.pallas_call(
        functools.partial(load_kernel, pieces),
        in_specs=[pl.BlockSpec(memory_space=pl.ANY)] * 2,
        out_specs=[pl.BlockSpec(memory_space=pltpu.VMEM)] * (experts + 1),
        out_shape=[jax.ShapeDtypeStruct(weight.shape[1:], weight.dtype)] * experts
        + [jax.ShapeDtypeStruct((8, LANES), jnp.float32)],
        scratch_shapes=[pltpu.SemaphoreType.DMA((experts * 2 * pieces,))],
        compiler_params=params(40),
        cost_estimate=pl.CostEstimate(flops=10**8, bytes_accessed=0, transcendentals=0),
        name="load",
    )(weight, after)


def gate_up_kernel(experts, afters, chunk, rows_ref, *refs):
    weight_refs, out_refs = refs[:experts], refs[experts + afters:]
    out_ref = out_refs[0]
    if len(out_refs) > 1:
        out_refs[1][...] = jnp.zeros_like(out_refs[1])
    ff = out_ref.shape[2] // 2
    columns = pl.ds(pl.multiple_of(chunk[0] * ff, ff), ff)
    for x in range(experts):
        for k in range(2):
            out_ref[x, :, k * ff:(k + 1) * ff] = jnp.dot(
                rows_ref[x], weight_refs[x][k, :, columns], preferred_element_type=jnp.float32
            ).astype(out_ref.dtype)


def gate_up(chunk, chunks, rows, weights, dtype, done=False, after=()):
    experts, count, _ = rows.shape
    ff = weights[0].shape[2] // chunks
    return call(
        functools.partial(gate_up_kernel, experts, len(after)),
        [chunk],
        [rows, *weights],
        [jax.ShapeDtypeStruct((experts, count, 2 * ff), dtype)]
        + [jax.ShapeDtypeStruct((8, LANES), jnp.float32)] * done,
        "gate_up",
        24,
        after=after,
        cost=2,
    )


def activate_kernel(own_ref, *refs):
    other_refs, out_ref = refs[:-2], refs[-1]
    ff = out_ref.shape[2]
    for x in range(out_ref.shape[0]):
        total = own_ref[x]
        for ref in other_refs:
            total = total + ref[x].astype(jnp.float32)
        gate, up = total[:, :ff], total[:, ff:]
        out_ref[x] = (gate / (1.0 + jnp.exp(-gate)) * up).astype(out_ref.dtype)


def down_product(part_ref, weight_ref, x, chunk):
    ff = part_ref.shape[2]
    rows = pl.ds(pl.multiple_of(chunk * ff, ff), ff)
    return jnp.dot(part_ref[x], weight_ref[x, rows], preferred_element_type=jnp.float32)


def down_first_kernel(me, part_ref, weight_ref, sum_ref):
    for x in range(part_ref.shape[0]):
        sum_ref[x] = down_product(part_ref, weight_ref, x, me[0])


def down_more_kernel(index, me, before_ref, part_ref, weight_ref, sum_ref):
    for x in range(part_ref.shape[0]):
        sum_ref[x] = before_ref[x] + down_product(part_ref, weight_ref, x, me[0] ^ index)


def down_rest_kernel(indices, me, sum_ref, *refs):
    count = len(indices)
    parts, weight_ref, out_refs = refs[:count], refs[count], refs[count + 1:]
    experts, slots, _ = sum_ref.shape
    sums = []
    for x in range(experts):
        total = sum_ref[x]
        for part_ref, index in zip(parts, indices):
            total = total + down_product(part_ref, weight_ref, x, me[0] ^ index)
        sums.append(total.astype(jnp.bfloat16))
    owners = len(out_refs)
    rows = experts * slots // owners
    moved = lax.dot_general(
        regroup(experts, owners, slots // owners),
        jnp.concatenate(sums, axis=0),
        (((0,), (0,)), ((), ())),
        preferred_element_type=jnp.float32,
    )
    for t, out_ref in enumerate(out_refs):
        out_ref[...] = moved[t * rows:(t + 1) * rows].astype(out_ref.dtype)


def traded(value, axis, index):
    return lax.ppermute(value, axis, [(i, i ^ index) for i in range(lax.axis_size(axis))])


def trade(values, axis):
    out = [values[0]] + [None] * (len(values) - 1)
    for s in reversed(range(1, len(values))):
        out[s] = traded(values[s], axis, s)
    return out


def call(kernel, index, inputs, outputs, name, limit=16, after=(), cost=0):
    single = not isinstance(outputs, list)
    return pl.pallas_call(
        kernel,
        in_specs=[pl.BlockSpec(memory_space=pltpu.SMEM)] * len(index)
        + [pl.BlockSpec(memory_space=pltpu.VMEM)] * len(inputs)
        + [pl.BlockSpec(memory_space=pl.ANY)] * len(after),
        out_specs=pl.BlockSpec(memory_space=pltpu.VMEM)
        if single
        else [pl.BlockSpec(memory_space=pltpu.VMEM)] * len(outputs),
        out_shape=outputs,
        compiler_params=params(limit),
        cost_estimate=pl.CostEstimate(
            flops=cost * 10**9, bytes_accessed=0, transcendentals=0
        ),
        name=name,
    )(*index, *inputs, *after)


def experts_by_columns(held, loaded, down_weight, owners, attention):
    inner = lax.axis_size("inner")
    experts, count, _ = held.shape
    ff, width = down_weight.shape[1:]
    me = lax.axis_index("inner").astype(jnp.int32)
    level = me.reshape(1)
    others, last = [], []
    for s in reversed(range(1, inner)):
        last = gate_up(
            (me ^ s).reshape(1), inner, held, loaded, jnp.bfloat16, after=last
        )
        others.append(traded(last[0], "inner", s))
    own, done = gate_up(level, inner, held, loaded, jnp.float32, True, last)
    attended, done = attention(done)
    active = call(
        activate_kernel,
        [],
        [own, *others],
        jax.ShapeDtypeStruct((experts, count, ff // inner), jnp.bfloat16),
        "activate",
        after=[done],
    )
    parts = trade([active] * inner, "inner")
    sums_shape = jax.ShapeDtypeStruct((experts, count, width), jnp.float32)
    sums = call(down_first_kernel, [level], [active, down_weight], sums_shape, "down_first", 24)
    sums = call(
        functools.partial(down_more_kernel, inner - 1),
        [level],
        [sums, parts[-1], down_weight],
        sums_shape,
        "down_more",
        24,
    )
    rest = list(range(1, inner - 1))
    back = call(
        functools.partial(down_rest_kernel, rest),
        [level],
        [sums, *[parts[s] for s in rest], down_weight],
        [jax.ShapeDtypeStruct((experts * count // owners, width), jnp.bfloat16)] * owners,
        "down_rest",
        24,
    )
    return back, attended


def experts_by_rows(held, gate_up_weight, down_weight, owners, attention):
    experts, count, _ = held.shape
    partial = jnp.einsum("xsd,xkdf->sxkf", held, gate_up_weight, preferred_element_type=jnp.float32)
    summed = lax.psum_scatter(partial, "inner", scatter_dimension=0, tiled=True)
    active = (jax.nn.silu(summed[:, :, 0]) * summed[:, :, 1]).astype(jnp.bfloat16)
    active = lax.all_gather(active, "inner", axis=0, tiled=True)
    outputs = jnp.einsum("sxf,xfd->xsd", active, down_weight, preferred_element_type=jnp.float32)
    outputs = outputs.astype(jnp.bfloat16).reshape(experts, owners, count // owners, -1)
    back = [outputs[:, t].reshape(experts * count // owners, -1) for t in range(owners)]
    return back, attention(held)[0]


def body(
    queries,
    new_key_value,
    cached_key_value,
    parents,
    hidden,
    routes,
    gate_values,
    gate_up_weight,
    down_weight,
):
    owners, inner = lax.axis_size("expert"), lax.axis_size("inner")
    experts, _, depth, ff = gate_up_weight.shape
    rows, model = hidden.shape
    width = down_weight.shape[2]
    top = routes.shape[1]
    column = lax.axis_index("expert").astype(jnp.int32).reshape(1)
    level = lax.axis_index("inner").astype(jnp.int32).reshape(1)
    slots = experts * CAP * inner

    attention = functools.partial(attend, queries, new_key_value, cached_key_value, parents)

    slices = call(
        prepare_kernel,
        [level],
        [routes.T, gate_values.T, hidden],
        [jax.ShapeDtypeStruct((rows, depth + LANES), jnp.bfloat16)] * inner,
        "prepare",
    )
    even = ff % (inner * LANES) == 0
    slices = trade(slices, "inner")
    packs = call(
        functools.partial(pack_kernel, top, experts, inner),
        [column, level],
        slices,
        [jax.ShapeDtypeStruct((slots, depth), jnp.bfloat16)] * owners,
        "pack",
    )
    *loaded, done = load(gate_up_weight, packs[0]) if even else [None]
    packs = trade(packs, "expert")
    held = call(
        functools.partial(select_kernel, owners),
        [],
        packs,
        jax.ShapeDtypeStruct((experts, owners * CAP * inner, depth), jnp.bfloat16),
        "select",
        24,
        after=[done] if even else [],
    )
    back, attended = (experts_by_columns if even else experts_by_rows)(
        held, loaded or gate_up_weight, down_weight, owners, attention
    )
    back = trade(back, "expert")
    weights = call(
        functools.partial(weigh_kernel, top, experts),
        [column, level],
        slices,
        jax.ShapeDtypeStruct((owners, slots, inner * rows), jnp.bfloat16),
        "weigh",
        cost=1,
    )
    pieces = call(
        combine_kernel,
        [],
        [weights, *back],
        [jax.ShapeDtypeStruct((rows, width), jnp.bfloat16)] * inner,
        "combine",
    )
    pieces = trade(pieces, "inner")
    expert_out = call(
        assemble_kernel,
        [level],
        pieces,
        jax.ShapeDtypeStruct((rows, model), jnp.bfloat16),
        "assemble",
    )
    return attended, expert_out


def solution(mesh):
    rows = ("groups", "expert", "inner")
    return jax.shard_map(
        body,
        mesh=mesh,
        in_specs=(
            P(rows, None),
            P(rows, None),
            P(rows, None, None, None),
            P(rows, None),
            P(rows, None),
            P(rows, None),
            P(rows, None),
            P("expert", None, "inner", None),
            P("expert", None, "inner"),
        ),
        out_specs=(P(rows, None), P(rows, None)),
        check_vma=False,
    )
```

```python
import functools
import math

import jax
import jax.numpy as jnp
from jax import lax
from jax.experimental import pallas as pl
from jax.experimental.pallas import tpu as pltpu
from jax.sharding import PartitionSpec as P

QUERY_HEADS = 64
KEY_HEADS = 4
HEAD_SIZE = 128
CAP = 3
LANES = 128


def params(limit, *semantics):
    return pltpu.CompilerParams(
        dimension_semantics=semantics or None, vmem_limit_bytes=int(limit * 1024 * 1024)
    )


def attend_kernel(
    parents, q_ref, new_ref, cache_ref, after_ref, out_ref, done_ref, q_rows, new_rows, out_rows
):
    del after_ref
    done_ref[...] = jnp.zeros_like(done_ref)
    group = QUERY_HEADS // KEY_HEADS
    scale = 1.0 / math.sqrt(HEAD_SIZE)
    width = KEY_HEADS * HEAD_SIZE
    count, beams = q_ref.shape[0], cache_ref.shape[1]
    for h in range(QUERY_HEADS):
        q_rows[h * count:(h + 1) * count] = q_ref[
            :, h * HEAD_SIZE:(h + 1) * HEAD_SIZE
        ].astype(jnp.float32)
    for h in range(2 * KEY_HEADS):
        new_rows[h * count:(h + 1) * count] = new_ref[
            :, h * HEAD_SIZE:(h + 1) * HEAD_SIZE
        ].astype(jnp.float32)
    for r in range(count):
        request, parent = r // beams, parents[r]
        q = q_rows[pl.ds(r, QUERY_HEADS, stride=count), :]
        fresh = new_rows[pl.ds(r, 2 * KEY_HEADS, stride=count), :]
        scores, own = [], []
        for k in range(KEY_HEADS):
            qk = q[k * group:(k + 1) * group]
            keys = cache_ref[request, parent, :, k * HEAD_SIZE:(k + 1) * HEAD_SIZE]
            scores.append(
                lax.dot_general(
                    qk.astype(jnp.bfloat16),
                    keys,
                    (((1,), (1,)), ((), ())),
                    preferred_element_type=jnp.float32,
                )
            )
            own.append(jnp.sum(qk * fresh[k:k + 1], axis=-1, keepdims=True))
        scores = jnp.concatenate(scores, axis=0) * scale
        own = jnp.concatenate(own, axis=0) * scale
        upper = jnp.maximum(jnp.max(scores, axis=-1, keepdims=True), own)
        expo = jnp.exp(scores - upper)
        own_expo = jnp.exp(own - upper)
        total = jnp.sum(expo, axis=-1, keepdims=True) + own_expo
        probs = (expo / total).astype(jnp.bfloat16)
        own_prob = (own_expo / total).astype(jnp.bfloat16).astype(jnp.float32)
        for k in range(KEY_HEADS):
            heads = slice(k * group, (k + 1) * group)
            columns = slice(width + k * HEAD_SIZE, width + (k + 1) * HEAD_SIZE)
            result = jnp.dot(
                probs[heads], cache_ref[request, parent, :, columns], preferred_element_type=jnp.float32
            )
            out_rows[pl.ds(k * group * count + r, group, stride=count), :] = (
                result + own_prob[heads] * fresh[KEY_HEADS + k:KEY_HEADS + k + 1]
            )
    for h in range(QUERY_HEADS):
        out_ref[:, h * HEAD_SIZE:(h + 1) * HEAD_SIZE] = out_rows[
            h * count:(h + 1) * count
        ].astype(out_ref.dtype)


def attend(queries, new_key_value, cached_key_value, parents, after):
    rows = queries.shape[0]
    _, _, length, width = cached_key_value.shape
    vmem = pl.BlockSpec(memory_space=pltpu.VMEM)
    return pl.pallas_call(
        attend_kernel,
        in_specs=[pl.BlockSpec(memory_space=pltpu.SMEM), vmem, vmem, vmem]
        + [pl.BlockSpec(memory_space=pl.ANY)],
        out_specs=[vmem, vmem],
        out_shape=[
            jax.ShapeDtypeStruct(queries.shape, queries.dtype),
            jax.ShapeDtypeStruct((8, LANES), jnp.float32),
        ],
        scratch_shapes=[
            pltpu.VMEM((QUERY_HEADS * rows, HEAD_SIZE), jnp.float32),
            pltpu.VMEM((2 * KEY_HEADS * rows, HEAD_SIZE), jnp.float32),
            pltpu.VMEM((QUERY_HEADS * rows, HEAD_SIZE), jnp.float32),
        ],
        compiler_params=params(32),
        cost_estimate=pl.CostEstimate(
            flops=4 * rows * QUERY_HEADS * HEAD_SIZE * length,
            bytes_accessed=2 * rows * length * width,
            transcendentals=rows * QUERY_HEADS * length,
        ),
        name="attend",
    )(parents.reshape(rows), queries, new_key_value, cached_key_value, after)


def spread(values, lanes, first):
    top = values.shape[0]
    shape = (top, lanes)
    chosen = (
        lax.broadcasted_iota(jnp.int32, shape, 1)
        == lax.broadcasted_iota(jnp.int32, shape, 0) + first
    ).astype(jnp.float32)
    return lax.dot_general(
        values.astype(jnp.float32), chosen, (((0,), (0,)), ((), ())), preferred_element_type=jnp.float32
    )


def prepare_kernel(indices, me, routes_ref, gates_ref, hidden_ref, *out_refs):
    width = out_refs[0].shape[1] - LANES
    top = routes_ref.shape[0]
    notes = spread(routes_ref[...], LANES, 0) + spread(gates_ref[...], LANES, top)
    notes = notes.astype(jnp.bfloat16)
    for s, out_ref in zip(indices, out_refs):
        start = pl.multiple_of((me[0] ^ s) * width, width)
        out_ref[:, :width] = hidden_ref[:, pl.ds(start, width)]
        out_ref[:, width:] = notes


def turned_notes(notes, top):
    shape = (max(8, 2 * top), LANES)
    chosen = (
        lax.broadcasted_iota(jnp.int32, shape, 0) == lax.broadcasted_iota(jnp.int32, shape, 1)
    ).astype(jnp.bfloat16)
    turned = lax.dot_general(
        chosen, notes, (((1,), (1,)), ((), ())), preferred_element_type=jnp.float32
    )
    return turned[:top], turned[top:2 * top]


def placing(routes, column, level, owners, experts, sources):
    top, rows = routes.shape
    count = CAP * sources
    shape = (owners * experts * count, rows)
    slot = lax.broadcasted_iota(jnp.int32, shape, 0)
    row = lax.broadcasted_iota(jnp.int32, shape, 1)
    each = rows // sources
    block = jnp.zeros(shape, jnp.int32)
    for n in range(1, owners * experts):
        block = block + (slot >= n * count).astype(jnp.int32)
    within = slot - block * count
    rank, source = within // sources, within % sources
    expert = ((column ^ (block // experts)) * experts + block % experts).astype(jnp.float32)
    member = jnp.zeros(shape, jnp.float32)
    for t in range(top):
        member = jnp.where(routes[t:t + 1] == expert, 1.0, member)
    origin = level ^ (row // each)
    member = jnp.where(origin == source, member, 0.0)
    one = lax.broadcasted_iota(jnp.int32, (rows, rows), 0)
    other = lax.broadcasted_iota(jnp.int32, (rows, rows), 1)
    before = (one < other).astype(jnp.float32)
    ranks = jnp.dot(member, before, preferred_element_type=jnp.float32)
    return jnp.where(ranks == rank.astype(jnp.float32), member, 0.0), expert


def pack_kernel(top, experts, sources, column, level, *refs):
    held, out_refs = refs[:sources], refs[sources:]
    slots, width = out_refs[0].shape
    rows = jnp.concatenate([ref[:, :width] for ref in held], axis=0)
    notes = jnp.concatenate([ref[:, width:] for ref in held], axis=0)
    routes, _ = turned_notes(notes, top)
    place, _ = placing(routes, column[0], level[0], len(out_refs), experts, sources)
    moved = jnp.dot(place.astype(jnp.bfloat16), rows, preferred_element_type=jnp.float32)
    for t, out_ref in enumerate(out_refs):
        out_ref[...] = moved[t * slots:(t + 1) * slots].astype(out_ref.dtype)


def weigh_kernel(top, experts, column, level, *refs):
    held, out_ref = refs[:-1], refs[-1]
    owners, slots, _ = out_ref.shape
    notes = jnp.concatenate([ref[:, -LANES:] for ref in held], axis=0)
    routes, gates = turned_notes(notes, top)
    place, expert = placing(routes, column[0], level[0], owners, experts, len(held))
    weight = jnp.zeros_like(place)
    for k in range(top):
        weight = weight + jnp.where(routes[k:k + 1] == expert, gates[k:k + 1], 0.0)
    weight = weight * place
    for t in range(owners):
        out_ref[t] = weight[t * slots:(t + 1) * slots].astype(out_ref.dtype)


def combine_kernel(weight_ref, *refs):
    owners = weight_ref.shape[0]
    back, out_refs = refs[:owners], refs[owners:]
    each = out_refs[0].shape[0]
    total = 0.0
    for t in range(owners):
        total = total + lax.dot_general(
            weight_ref[t],
            back[t][...],
            (((0,), (0,)), ((), ())),
            preferred_element_type=jnp.float32,
        )
    for s, out_ref in enumerate(out_refs):
        out_ref[...] = total[s * each:(s + 1) * each].astype(out_ref.dtype)


def assemble_kernel(me, *refs):
    pieces, out_ref = refs[:-1], refs[-1]
    width = pieces[0].shape[1]
    for s, piece in enumerate(pieces):
        start = pl.multiple_of((me[0] ^ s) * width, width)
        out_ref[:, pl.ds(start, width)] = piece[...]


def regroup(experts, owners, count):
    shape = (experts * owners * count, owners * experts * count)
    row = lax.broadcasted_iota(jnp.int32, shape, 0)
    other = lax.broadcasted_iota(jnp.int32, shape, 1)
    wanted = jnp.zeros(shape, jnp.int32) + row
    for x in range(experts):
        for t in range(owners):
            first = (x * owners + t) * count
            inside = (row >= first) & (row < first + count)
            wanted = jnp.where(inside, row - first + (t * experts + x) * count, wanted)
    return (other == wanted).astype(jnp.bfloat16)


def select_kernel(owners, *refs):
    packs, out_ref = refs[:owners], refs[-1]
    experts, count, _ = out_ref.shape
    rows = jnp.concatenate([ref[...].astype(jnp.float32) for ref in packs], axis=0)
    moved = jnp.dot(
        regroup(experts, len(packs), count // len(packs)),
        rows.astype(jnp.bfloat16),
        preferred_element_type=jnp.float32,
    ).astype(out_ref.dtype)
    for x in range(experts):
        out_ref[x] = moved[x * count:(x + 1) * count]


def load_kernel(pieces, weight_hbm, after_ref, *refs):
    del after_ref
    out_refs, done_ref, sems = refs[:-2], refs[-2], refs[-1]
    done_ref[...] = jnp.zeros_like(done_ref)
    step = weight_hbm.shape[2] // pieces
    copies = [
        pltpu.make_async_copy(
            weight_hbm.at[x, k, pl.ds(n * step, step)],
            out_ref.at[k, pl.ds(n * step, step)],
            sems.at[(x * 2 + k) * pieces + n],
        )
        for x, out_ref in enumerate(out_refs)
        for k in range(2)
        for n in range(pieces)
    ]
    for copy in copies:
        copy.start()
    for copy in copies:
        copy.wait()


def load(weight, after):
    experts, pieces = weight.shape[0], 4
    return pl.pallas_call(
        functools.partial(load_kernel, pieces),
        in_specs=[pl.BlockSpec(memory_space=pl.ANY)] * 2,
        out_specs=[pl.BlockSpec(memory_space=pltpu.VMEM)] * (experts + 1),
        out_shape=[jax.ShapeDtypeStruct(weight.shape[1:], weight.dtype)] * experts
        + [jax.ShapeDtypeStruct((8, LANES), jnp.float32)],
        scratch_shapes=[pltpu.SemaphoreType.DMA((experts * 2 * pieces,))],
        compiler_params=params(40),
        cost_estimate=pl.CostEstimate(flops=10**8, bytes_accessed=0, transcendentals=0),
        name="load",
    )(weight, after)


def gate_up_kernel(experts, afters, chunk, rows_ref, *refs):
    weight_refs, out_refs = refs[:experts], refs[experts + afters:]
    out_ref = out_refs[0]
    if len(out_refs) > 1:
        out_refs[1][...] = jnp.zeros_like(out_refs[1])
    ff = out_ref.shape[2] // 2
    columns = pl.ds(pl.multiple_of(chunk[0] * ff, ff), ff)
    for x in range(experts):
        for k in range(2):
            out_ref[x, :, k * ff:(k + 1) * ff] = jnp.dot(
                rows_ref[x], weight_refs[x][k, :, columns], preferred_element_type=jnp.float32
            ).astype(out_ref.dtype)


def gate_up(chunk, chunks, rows, weights, dtype, done=False, after=()):
    experts, count, _ = rows.shape
    ff = weights[0].shape[2] // chunks
    return call(
        functools.partial(gate_up_kernel, experts, len(after)),
        [chunk],
        [rows, *weights],
        [jax.ShapeDtypeStruct((experts, count, 2 * ff), dtype)]
        + [jax.ShapeDtypeStruct((8, LANES), jnp.float32)] * done,
        "gate_up",
        24,
        after=after,
        cost=2,
    )


def activate_kernel(own_ref, *refs):
    other_refs, out_ref = refs[:-2], refs[-1]
    ff = out_ref.shape[2]
    for x in range(out_ref.shape[0]):
        total = own_ref[x]
        for ref in other_refs:
            total = total + ref[x].astype(jnp.float32)
        gate, up = total[:, :ff], total[:, ff:]
        out_ref[x] = (gate / (1.0 + jnp.exp(-gate)) * up).astype(out_ref.dtype)


def down_product(part_ref, weight_ref, x, chunk):
    ff = part_ref.shape[2]
    rows = pl.ds(pl.multiple_of(chunk * ff, ff), ff)
    return jnp.dot(part_ref[x], weight_ref[x, rows], preferred_element_type=jnp.float32)


def down_first_kernel(me, part_ref, weight_ref, sum_ref):
    for x in range(part_ref.shape[0]):
        sum_ref[x] = down_product(part_ref, weight_ref, x, me[0])


def down_more_kernel(index, me, before_ref, part_ref, weight_ref, sum_ref):
    for x in range(part_ref.shape[0]):
        sum_ref[x] = before_ref[x] + down_product(part_ref, weight_ref, x, me[0] ^ index)


def down_rest_kernel(indices, me, sum_ref, *refs):
    count = len(indices)
    parts, weight_ref, out_refs = refs[:count], refs[count], refs[count + 1:]
    experts, slots, _ = sum_ref.shape
    sums = []
    for x in range(experts):
        total = sum_ref[x]
        for part_ref, index in zip(parts, indices):
            total = total + down_product(part_ref, weight_ref, x, me[0] ^ index)
        sums.append(total.astype(jnp.bfloat16))
    owners = len(out_refs)
    rows = experts * slots // owners
    moved = lax.dot_general(
        regroup(experts, owners, slots // owners),
        jnp.concatenate(sums, axis=0),
        (((0,), (0,)), ((), ())),
        preferred_element_type=jnp.float32,
    )
    for t, out_ref in enumerate(out_refs):
        out_ref[...] = moved[t * rows:(t + 1) * rows].astype(out_ref.dtype)


def traded(value, axis, index):
    return lax.ppermute(value, axis, [(i, i ^ index) for i in range(lax.axis_size(axis))])


def trade(values, axis):
    out = [values[0]] + [None] * (len(values) - 1)
    for s in reversed(range(1, len(values))):
        out[s] = traded(values[s], axis, s)
    return out


def call(kernel, index, inputs, outputs, name, limit=16, after=(), cost=0):
    single = not isinstance(outputs, list)
    return pl.pallas_call(
        kernel,
        in_specs=[pl.BlockSpec(memory_space=pltpu.SMEM)] * len(index)
        + [pl.BlockSpec(memory_space=pltpu.VMEM)] * len(inputs)
        + [pl.BlockSpec(memory_space=pl.ANY)] * len(after),
        out_specs=pl.BlockSpec(memory_space=pltpu.VMEM)
        if single
        else [pl.BlockSpec(memory_space=pltpu.VMEM)] * len(outputs),
        out_shape=outputs,
        compiler_params=params(limit),
        cost_estimate=pl.CostEstimate(
            flops=cost * 10**9, bytes_accessed=0, transcendentals=0
        ),
        name=name,
    )(*index, *inputs, *after)


def experts_by_columns(held, loaded, down_weight, owners, attention):
    inner = lax.axis_size("inner")
    experts, count, _ = held.shape
    ff, width = down_weight.shape[1:]
    me = lax.axis_index("inner").astype(jnp.int32)
    level = me.reshape(1)
    others, last = [], []
    for s in reversed(range(1, inner)):
        last = gate_up(
            (me ^ s).reshape(1), inner, held, loaded, jnp.bfloat16, after=last
        )
        others.append(traded(last[0], "inner", s))
    own, done = gate_up(level, inner, held, loaded, jnp.float32, True, last)
    attended, done = attention(done)
    active = call(
        activate_kernel,
        [],
        [own, *others],
        jax.ShapeDtypeStruct((experts, count, ff // inner), jnp.bfloat16),
        "activate",
        after=[done],
    )
    parts = trade([active] * inner, "inner")
    sums_shape = jax.ShapeDtypeStruct((experts, count, width), jnp.float32)
    sums = call(down_first_kernel, [level], [active, down_weight], sums_shape, "down_first", 24)
    sums = call(
        functools.partial(down_more_kernel, inner - 1),
        [level],
        [sums, parts[-1], down_weight],
        sums_shape,
        "down_more",
        24,
    )
    rest = list(range(1, inner - 1))
    back = call(
        functools.partial(down_rest_kernel, rest),
        [level],
        [sums, *[parts[s] for s in rest], down_weight],
        [jax.ShapeDtypeStruct((experts * count // owners, width), jnp.bfloat16)] * owners,
        "down_rest",
        24,
    )
    return back, attended


def experts_by_rows(held, gate_up_weight, down_weight, owners, attention):
    experts, count, _ = held.shape
    partial = jnp.einsum("xsd,xkdf->sxkf", held, gate_up_weight, preferred_element_type=jnp.float32)
    summed = lax.psum_scatter(partial, "inner", scatter_dimension=0, tiled=True)
    active = (jax.nn.silu(summed[:, :, 0]) * summed[:, :, 1]).astype(jnp.bfloat16)
    active = lax.all_gather(active, "inner", axis=0, tiled=True)
    outputs = jnp.einsum("sxf,xfd->xsd", active, down_weight, preferred_element_type=jnp.float32)
    outputs = outputs.astype(jnp.bfloat16).reshape(experts, owners, count // owners, -1)
    back = [outputs[:, t].reshape(experts * count // owners, -1) for t in range(owners)]
    return back, attention(held)[0]


def body(
    queries,
    new_key_value,
    cached_key_value,
    parents,
    hidden,
    routes,
    gate_values,
    gate_up_weight,
    down_weight,
):
    owners, inner = lax.axis_size("expert"), lax.axis_size("inner")
    experts, _, depth, ff = gate_up_weight.shape
    rows, model = hidden.shape
    width = down_weight.shape[2]
    top = routes.shape[1]
    column = lax.axis_index("expert").astype(jnp.int32).reshape(1)
    level = lax.axis_index("inner").astype(jnp.int32).reshape(1)
    slots = experts * CAP * inner

    attention = functools.partial(attend, queries, new_key_value, cached_key_value, parents)

    even = ff % (inner * LANES) == 0
    shape = jax.ShapeDtypeStruct((rows, depth + LANES), jnp.bfloat16)
    arrays = [routes.T, gate_values.T, hidden]
    sent = call(
        functools.partial(prepare_kernel, range(1, inner)),
        [level],
        arrays,
        [shape] * (inner - 1),
        "prepare",
        66633728 / 1024 / 1024,
    )
    (kept,) = call(
        functools.partial(prepare_kernel, [0]), [level], arrays, [shape], "keep", cost=1
    )
    slices = [kept, *sent]
    slices = trade(slices, "inner")
    packs = call(
        functools.partial(pack_kernel, top, experts, inner),
        [column, level],
        slices,
        [jax.ShapeDtypeStruct((slots, depth), jnp.bfloat16)] * owners,
        "pack",
    )
    *loaded, done = load(gate_up_weight, packs[0]) if even else [None]
    packs = trade(packs, "expert")
    held = call(
        functools.partial(select_kernel, owners),
        [],
        packs,
        jax.ShapeDtypeStruct((experts, owners * CAP * inner, depth), jnp.bfloat16),
        "select",
        24,
        after=[done] if even else [],
    )
    back, attended = (experts_by_columns if even else experts_by_rows)(
        held, loaded or gate_up_weight, down_weight, owners, attention
    )
    back = trade(back, "expert")
    weights = call(
        functools.partial(weigh_kernel, top, experts),
        [column, level],
        slices,
        jax.ShapeDtypeStruct((owners, slots, inner * rows), jnp.bfloat16),
        "weigh",
        cost=1,
    )
    pieces = call(
        combine_kernel,
        [],
        [weights, *back],
        [jax.ShapeDtypeStruct((rows, width), jnp.bfloat16)] * inner,
        "combine",
    )
    pieces = trade(pieces, "inner")
    expert_out = call(
        assemble_kernel,
        [level],
        pieces,
        jax.ShapeDtypeStruct((rows, model), jnp.bfloat16),
        "assemble",
    )
    return attended, expert_out


def solution(mesh):
    rows = ("groups", "expert", "inner")
    return jax.shard_map(
        body,
        mesh=mesh,
        in_specs=(
            P(rows, None),
            P(rows, None),
            P(rows, None, None, None),
            P(rows, None),
            P(rows, None),
            P(rows, None),
            P(rows, None),
            P("expert", None, "inner", None),
            P("expert", None, "inner"),
        ),
        out_specs=(P(rows, None), P(rows, None)),
        check_vma=False,
    )
```

```python
import functools
import math

import jax
import jax.numpy as jnp
from jax import lax
from jax.experimental import pallas as pl
from jax.experimental.pallas import tpu as pltpu
from jax.sharding import PartitionSpec as P

QUERY_HEADS = 64
KEY_HEADS = 4
HEAD_SIZE = 128
CAP = 3
LANES = 128


def params(limit, *semantics):
    return pltpu.CompilerParams(
        dimension_semantics=semantics or None, vmem_limit_bytes=int(limit * 1024 * 1024)
    )


def attend_kernel(
    parents, q_ref, new_ref, cache_ref, after_ref, out_ref, done_ref, q_rows, new_rows, out_rows
):
    del after_ref
    done_ref[...] = jnp.zeros_like(done_ref)
    group = QUERY_HEADS // KEY_HEADS
    scale = 1.0 / math.sqrt(HEAD_SIZE)
    width = KEY_HEADS * HEAD_SIZE
    count, beams = q_ref.shape[0], cache_ref.shape[1]
    for h in range(QUERY_HEADS):
        q_rows[h * count:(h + 1) * count] = q_ref[
            :, h * HEAD_SIZE:(h + 1) * HEAD_SIZE
        ].astype(jnp.float32)
    for h in range(2 * KEY_HEADS):
        new_rows[h * count:(h + 1) * count] = new_ref[
            :, h * HEAD_SIZE:(h + 1) * HEAD_SIZE
        ].astype(jnp.float32)
    for r in range(count):
        request, parent = r // beams, parents[r]
        q = q_rows[pl.ds(r, QUERY_HEADS, stride=count), :]
        fresh = new_rows[pl.ds(r, 2 * KEY_HEADS, stride=count), :]
        scores, own = [], []
        for k in range(KEY_HEADS):
            qk = q[k * group:(k + 1) * group]
            keys = cache_ref[request, parent, :, k * HEAD_SIZE:(k + 1) * HEAD_SIZE]
            scores.append(
                lax.dot_general(
                    qk.astype(jnp.bfloat16),
                    keys,
                    (((1,), (1,)), ((), ())),
                    preferred_element_type=jnp.float32,
                )
            )
            own.append(jnp.sum(qk * fresh[k:k + 1], axis=-1, keepdims=True))
        scores = jnp.concatenate(scores, axis=0) * scale
        own = jnp.concatenate(own, axis=0) * scale
        upper = jnp.maximum(jnp.max(scores, axis=-1, keepdims=True), own)
        expo = jnp.exp(scores - upper)
        own_expo = jnp.exp(own - upper)
        total = jnp.sum(expo, axis=-1, keepdims=True) + own_expo
        probs = (expo / total).astype(jnp.bfloat16)
        own_prob = (own_expo / total).astype(jnp.bfloat16).astype(jnp.float32)
        for k in range(KEY_HEADS):
            heads = slice(k * group, (k + 1) * group)
            columns = slice(width + k * HEAD_SIZE, width + (k + 1) * HEAD_SIZE)
            result = jnp.dot(
                probs[heads], cache_ref[request, parent, :, columns], preferred_element_type=jnp.float32
            )
            out_rows[pl.ds(k * group * count + r, group, stride=count), :] = (
                result + own_prob[heads] * fresh[KEY_HEADS + k:KEY_HEADS + k + 1]
            )
    for h in range(QUERY_HEADS):
        out_ref[:, h * HEAD_SIZE:(h + 1) * HEAD_SIZE] = out_rows[
            h * count:(h + 1) * count
        ].astype(out_ref.dtype)


def attend(queries, new_key_value, cached_key_value, parents, after):
    rows = queries.shape[0]
    _, _, length, width = cached_key_value.shape
    vmem = pl.BlockSpec(memory_space=pltpu.VMEM)
    return pl.pallas_call(
        attend_kernel,
        in_specs=[pl.BlockSpec(memory_space=pltpu.SMEM), vmem, vmem, vmem]
        + [pl.BlockSpec(memory_space=pl.ANY)],
        out_specs=[vmem, vmem],
        out_shape=[
            jax.ShapeDtypeStruct(queries.shape, queries.dtype),
            jax.ShapeDtypeStruct((8, LANES), jnp.float32),
        ],
        scratch_shapes=[
            pltpu.VMEM(((QUERY_HEADS + 1) * rows, HEAD_SIZE), jnp.float32),
            pltpu.VMEM(((2 * KEY_HEADS + 1) * rows, HEAD_SIZE), jnp.float32),
            pltpu.VMEM(((QUERY_HEADS + 1) * rows, HEAD_SIZE), jnp.float32),
        ],
        compiler_params=params(32),
        cost_estimate=pl.CostEstimate(
            flops=4 * rows * QUERY_HEADS * HEAD_SIZE * length,
            bytes_accessed=2 * rows * length * width,
            transcendentals=rows * QUERY_HEADS * length,
        ),
        name="attend",
    )(parents.reshape(rows), queries, new_key_value, cached_key_value, after)


def spread(values, lanes, first):
    top = values.shape[0]
    shape = (top, lanes)
    chosen = (
        lax.broadcasted_iota(jnp.int32, shape, 1)
        == lax.broadcasted_iota(jnp.int32, shape, 0) + first
    ).astype(jnp.float32)
    return lax.dot_general(
        values.astype(jnp.float32), chosen, (((0,), (0,)), ((), ())), preferred_element_type=jnp.float32
    )


def prepare_kernel(indices, me, routes_ref, gates_ref, hidden_ref, *out_refs):
    width = out_refs[0].shape[1] - LANES
    top = routes_ref.shape[0]
    notes = spread(routes_ref[...], LANES, 0) + spread(gates_ref[...], LANES, top)
    notes = notes.astype(jnp.bfloat16)
    for s, out_ref in zip(indices, out_refs):
        start = pl.multiple_of((me[0] ^ s) * width, width)
        out_ref[:, :width] = hidden_ref[:, pl.ds(start, width)]
        out_ref[:, width:] = notes


def turned_notes(notes, top):
    shape = (max(8, 2 * top), LANES)
    chosen = (
        lax.broadcasted_iota(jnp.int32, shape, 0) == lax.broadcasted_iota(jnp.int32, shape, 1)
    ).astype(jnp.bfloat16)
    turned = lax.dot_general(
        chosen, notes, (((1,), (1,)), ((), ())), preferred_element_type=jnp.float32
    )
    return turned[:top], turned[top:2 * top]


def placing(routes, column, level, owners, experts, sources):
    top, rows = routes.shape
    count = CAP * sources
    shape = (owners * experts * count, rows)
    slot = lax.broadcasted_iota(jnp.int32, shape, 0)
    row = lax.broadcasted_iota(jnp.int32, shape, 1)
    each = rows // sources
    block = jnp.zeros(shape, jnp.int32)
    for n in range(1, owners * experts):
        block = block + (slot >= n * count).astype(jnp.int32)
    within = slot - block * count
    rank, source = within // sources, within % sources
    expert = ((column ^ (block // experts)) * experts + block % experts).astype(jnp.float32)
    member = jnp.zeros(shape, jnp.float32)
    for t in range(top):
        member = jnp.where(routes[t:t + 1] == expert, 1.0, member)
    origin = level ^ (row // each)
    member = jnp.where(origin == source, member, 0.0)
    one = lax.broadcasted_iota(jnp.int32, (rows, rows), 0)
    other = lax.broadcasted_iota(jnp.int32, (rows, rows), 1)
    before = (one < other).astype(jnp.float32)
    ranks = jnp.dot(member, before, preferred_element_type=jnp.float32)
    return jnp.where(ranks == rank.astype(jnp.float32), member, 0.0), expert


def pack_kernel(top, experts, sources, column, level, *refs):
    held, out_refs = refs[:sources], refs[sources:]
    slots, width = out_refs[0].shape
    rows = jnp.concatenate([ref[:, :width] for ref in held], axis=0)
    notes = jnp.concatenate([ref[:, width:] for ref in held], axis=0)
    routes, _ = turned_notes(notes, top)
    place, _ = placing(routes, column[0], level[0], len(out_refs), experts, sources)
    moved = jnp.dot(place.astype(jnp.bfloat16), rows, preferred_element_type=jnp.float32)
    for t, out_ref in enumerate(out_refs):
        out_ref[...] = moved[t * slots:(t + 1) * slots].astype(out_ref.dtype)


def weigh_kernel(top, experts, column, level, *refs):
    held, out_ref = refs[:-1], refs[-1]
    owners, slots, _ = out_ref.shape
    notes = jnp.concatenate([ref[:, -LANES:] for ref in held], axis=0)
    routes, gates = turned_notes(notes, top)
    place, expert = placing(routes, column[0], level[0], owners, experts, len(held))
    weight = jnp.zeros_like(place)
    for k in range(top):
        weight = weight + jnp.where(routes[k:k + 1] == expert, gates[k:k + 1], 0.0)
    weight = weight * place
    for t in range(owners):
        out_ref[t] = weight[t * slots:(t + 1) * slots].astype(out_ref.dtype)


def combine_kernel(weight_ref, *refs):
    owners = weight_ref.shape[0]
    back, out_refs = refs[:owners], refs[owners:]
    each = out_refs[0].shape[0]
    total = 0.0
    for t in range(owners):
        total = total + lax.dot_general(
            weight_ref[t],
            back[t][...],
            (((0,), (0,)), ((), ())),
            preferred_element_type=jnp.float32,
        )
    for s, out_ref in enumerate(out_refs):
        out_ref[...] = total[s * each:(s + 1) * each].astype(out_ref.dtype)


def assemble_kernel(me, *refs):
    pieces, out_ref = refs[:-1], refs[-1]
    width = pieces[0].shape[1]
    for s, piece in enumerate(pieces):
        start = pl.multiple_of((me[0] ^ s) * width, width)
        out_ref[:, pl.ds(start, width)] = piece[...]


def regroup(experts, owners, count):
    shape = (experts * owners * count, owners * experts * count)
    row = lax.broadcasted_iota(jnp.int32, shape, 0)
    other = lax.broadcasted_iota(jnp.int32, shape, 1)
    wanted = jnp.zeros(shape, jnp.int32) + row
    for x in range(experts):
        for t in range(owners):
            first = (x * owners + t) * count
            inside = (row >= first) & (row < first + count)
            wanted = jnp.where(inside, row - first + (t * experts + x) * count, wanted)
    return (other == wanted).astype(jnp.bfloat16)


def select_kernel(owners, *refs):
    packs, out_ref = refs[:owners], refs[-1]
    experts, count, _ = out_ref.shape
    rows = jnp.concatenate([ref[...].astype(jnp.float32) for ref in packs], axis=0)
    moved = jnp.dot(
        regroup(experts, len(packs), count // len(packs)),
        rows.astype(jnp.bfloat16),
        preferred_element_type=jnp.float32,
    ).astype(out_ref.dtype)
    for x in range(experts):
        out_ref[x] = moved[x * count:(x + 1) * count]


def load_kernel(pieces, weight_hbm, after_ref, *refs):
    del after_ref
    out_refs, done_ref, sems = refs[:-2], refs[-2], refs[-1]
    done_ref[...] = jnp.zeros_like(done_ref)
    step = weight_hbm.shape[2] // pieces
    copies = [
        pltpu.make_async_copy(
            weight_hbm.at[x, k, pl.ds(n * step, step)],
            out_ref.at[k, pl.ds(n * step, step)],
            sems.at[(x * 2 + k) * pieces + n],
        )
        for x, out_ref in enumerate(out_refs)
        for k in range(2)
        for n in range(pieces)
    ]
    for copy in copies:
        copy.start()
    for copy in copies:
        copy.wait()


def load(weight, after):
    experts, pieces = weight.shape[0], 4
    return pl.pallas_call(
        functools.partial(load_kernel, pieces),
        in_specs=[pl.BlockSpec(memory_space=pl.ANY)] * 2,
        out_specs=[pl.BlockSpec(memory_space=pltpu.VMEM)] * (experts + 1),
        out_shape=[jax.ShapeDtypeStruct(weight.shape[1:], weight.dtype)] * experts
        + [jax.ShapeDtypeStruct((8, LANES), jnp.float32)],
        scratch_shapes=[pltpu.SemaphoreType.DMA((experts * 2 * pieces,))],
        compiler_params=params(40),
        cost_estimate=pl.CostEstimate(flops=10**8, bytes_accessed=0, transcendentals=0),
        name="load",
    )(weight, after)


def gate_up_kernel(experts, afters, chunk, rows_ref, *refs):
    weight_refs, out_refs = refs[:experts], refs[experts + afters:]
    out_ref = out_refs[0]
    if len(out_refs) > 1:
        out_refs[1][...] = jnp.zeros_like(out_refs[1])
    ff = out_ref.shape[2] // 2
    columns = pl.ds(pl.multiple_of(chunk[0] * ff, ff), ff)
    for x in range(experts):
        for k in range(2):
            out_ref[x, :, k * ff:(k + 1) * ff] = jnp.dot(
                rows_ref[x], weight_refs[x][k, :, columns], preferred_element_type=jnp.float32
            ).astype(out_ref.dtype)


def gate_up(chunk, chunks, rows, weights, dtype, done=False, after=()):
    experts, count, _ = rows.shape
    ff = weights[0].shape[2] // chunks
    return call(
        functools.partial(gate_up_kernel, experts, len(after)),
        [chunk],
        [rows, *weights],
        [jax.ShapeDtypeStruct((experts, count, 2 * ff), dtype)]
        + [jax.ShapeDtypeStruct((8, LANES), jnp.float32)] * done,
        "gate_up",
        24,
        after=after,
        cost=2,
    )


def activate_kernel(own_ref, *refs):
    other_refs, out_ref = refs[:-2], refs[-1]
    ff = out_ref.shape[2]
    for x in range(out_ref.shape[0]):
        total = own_ref[x]
        for ref in other_refs:
            total = total + ref[x].astype(jnp.float32)
        gate, up = total[:, :ff], total[:, ff:]
        out_ref[x] = (gate / (1.0 + jnp.exp(-gate)) * up).astype(out_ref.dtype)


def down_product(part_ref, weight_ref, x, chunk):
    ff = part_ref.shape[2]
    rows = pl.ds(pl.multiple_of(chunk * ff, ff), ff)
    return jnp.dot(part_ref[x], weight_ref[x, rows], preferred_element_type=jnp.float32)


def down_first_kernel(me, part_ref, weight_ref, sum_ref):
    for x in range(part_ref.shape[0]):
        sum_ref[x] = down_product(part_ref, weight_ref, x, me[0])


def down_more_kernel(index, me, before_ref, part_ref, weight_ref, sum_ref):
    for x in range(part_ref.shape[0]):
        sum_ref[x] = before_ref[x] + down_product(part_ref, weight_ref, x, me[0] ^ index)


def down_rest_kernel(indices, me, sum_ref, *refs):
    count = len(indices)
    parts, weight_ref, out_refs = refs[:count], refs[count], refs[count + 1:]
    experts, slots, _ = sum_ref.shape
    sums = []
    for x in range(experts):
        total = sum_ref[x]
        for part_ref, index in zip(parts, indices):
            total = total + down_product(part_ref, weight_ref, x, me[0] ^ index)
        sums.append(total.astype(jnp.bfloat16))
    owners = len(out_refs)
    rows = experts * slots // owners
    moved = lax.dot_general(
        regroup(experts, owners, slots // owners),
        jnp.concatenate(sums, axis=0),
        (((0,), (0,)), ((), ())),
        preferred_element_type=jnp.float32,
    )
    for t, out_ref in enumerate(out_refs):
        out_ref[...] = moved[t * rows:(t + 1) * rows].astype(out_ref.dtype)


def traded(value, axis, index):
    return lax.ppermute(value, axis, [(i, i ^ index) for i in range(lax.axis_size(axis))])


def trade(values, axis):
    out = [values[0]] + [None] * (len(values) - 1)
    for s in reversed(range(1, len(values))):
        out[s] = traded(values[s], axis, s)
    return out


def call(kernel, index, inputs, outputs, name, limit=16, after=(), cost=0):
    single = not isinstance(outputs, list)
    return pl.pallas_call(
        kernel,
        in_specs=[pl.BlockSpec(memory_space=pltpu.SMEM)] * len(index)
        + [pl.BlockSpec(memory_space=pltpu.VMEM)] * len(inputs)
        + [pl.BlockSpec(memory_space=pl.ANY)] * len(after),
        out_specs=pl.BlockSpec(memory_space=pltpu.VMEM)
        if single
        else [pl.BlockSpec(memory_space=pltpu.VMEM)] * len(outputs),
        out_shape=outputs,
        compiler_params=params(limit),
        cost_estimate=pl.CostEstimate(
            flops=cost * 10**9, bytes_accessed=0, transcendentals=0
        ),
        name=name,
    )(*index, *inputs, *after)


def experts_by_columns(held, loaded, down_weight, owners, attention):
    inner = lax.axis_size("inner")
    experts, count, _ = held.shape
    ff, width = down_weight.shape[1:]
    me = lax.axis_index("inner").astype(jnp.int32)
    level = me.reshape(1)
    others, last = [], []
    for s in reversed(range(1, inner)):
        last = gate_up(
            (me ^ s).reshape(1), inner, held, loaded, jnp.bfloat16, after=last
        )
        others.append(traded(last[0], "inner", s))
    own, done = gate_up(level, inner, held, loaded, jnp.float32, True, last)
    attended, done = attention(done)
    active = call(
        activate_kernel,
        [],
        [own, *others],
        jax.ShapeDtypeStruct((experts, count, ff // inner), jnp.bfloat16),
        "activate",
        after=[done],
    )
    parts = trade([active] * inner, "inner")
    sums_shape = jax.ShapeDtypeStruct((experts, count, width), jnp.float32)
    sums = call(down_first_kernel, [level], [active, down_weight], sums_shape, "down_first", 24)
    sums = call(
        functools.partial(down_more_kernel, inner - 1),
        [level],
        [sums, parts[-1], down_weight],
        sums_shape,
        "down_more",
        24,
    )
    rest = list(range(1, inner - 1))
    back = call(
        functools.partial(down_rest_kernel, rest),
        [level],
        [sums, *[parts[s] for s in rest], down_weight],
        [jax.ShapeDtypeStruct((experts * count // owners, width), jnp.bfloat16)] * owners,
        "down_rest",
        24,
    )
    return back, attended


def experts_by_rows(held, gate_up_weight, down_weight, owners, attention):
    experts, count, _ = held.shape
    partial = jnp.einsum("xsd,xkdf->sxkf", held, gate_up_weight, preferred_element_type=jnp.float32)
    summed = lax.psum_scatter(partial, "inner", scatter_dimension=0, tiled=True)
    active = (jax.nn.silu(summed[:, :, 0]) * summed[:, :, 1]).astype(jnp.bfloat16)
    active = lax.all_gather(active, "inner", axis=0, tiled=True)
    outputs = jnp.einsum("sxf,xfd->xsd", active, down_weight, preferred_element_type=jnp.float32)
    outputs = outputs.astype(jnp.bfloat16).reshape(experts, owners, count // owners, -1)
    back = [outputs[:, t].reshape(experts * count // owners, -1) for t in range(owners)]
    return back, attention(held)[0]


def body(
    queries,
    new_key_value,
    cached_key_value,
    parents,
    hidden,
    routes,
    gate_values,
    gate_up_weight,
    down_weight,
):
    owners, inner = lax.axis_size("expert"), lax.axis_size("inner")
    experts, _, depth, ff = gate_up_weight.shape
    rows, model = hidden.shape
    width = down_weight.shape[2]
    top = routes.shape[1]
    column = lax.axis_index("expert").astype(jnp.int32).reshape(1)
    level = lax.axis_index("inner").astype(jnp.int32).reshape(1)
    slots = experts * CAP * inner

    attention = functools.partial(attend, queries, new_key_value, cached_key_value, parents)

    even = ff % (inner * LANES) == 0
    shape = jax.ShapeDtypeStruct((rows, depth + LANES), jnp.bfloat16)
    arrays = [routes.T, gate_values.T, hidden]
    sent = call(
        functools.partial(prepare_kernel, range(1, inner)),
        [level],
        arrays,
        [shape] * (inner - 1),
        "prepare",
        66633728 / 1024 / 1024,
    )
    (kept,) = call(
        functools.partial(prepare_kernel, [0]), [level], arrays, [shape], "keep", cost=1
    )
    slices = [kept, *sent]
    slices = trade(slices, "inner")
    packs = call(
        functools.partial(pack_kernel, top, experts, inner),
        [column, level],
        slices,
        [jax.ShapeDtypeStruct((slots, depth), jnp.bfloat16)] * owners,
        "pack",
    )
    *loaded, done = load(gate_up_weight, packs[0]) if even else [None]
    packs = trade(packs, "expert")
    held = call(
        functools.partial(select_kernel, owners),
        [],
        packs,
        jax.ShapeDtypeStruct((experts, owners * CAP * inner, depth), jnp.bfloat16),
        "select",
        24,
        after=[done] if even else [],
    )
    back, attended = (experts_by_columns if even else experts_by_rows)(
        held, loaded or gate_up_weight, down_weight, owners, attention
    )
    back = trade(back, "expert")
    weights = call(
        functools.partial(weigh_kernel, top, experts),
        [column, level],
        slices,
        jax.ShapeDtypeStruct((owners, slots, inner * rows), jnp.bfloat16),
        "weigh",
        cost=1,
    )
    pieces = call(
        combine_kernel,
        [],
        [weights, *back],
        [jax.ShapeDtypeStruct((rows, width), jnp.bfloat16)] * inner,
        "combine",
    )
    pieces = trade(pieces, "inner")
    expert_out = call(
        assemble_kernel,
        [level],
        pieces,
        jax.ShapeDtypeStruct((rows, model), jnp.bfloat16),
        "assemble",
    )
    return attended, expert_out


def solution(mesh):
    rows = ("groups", "expert", "inner")
    return jax.shard_map(
        body,
        mesh=mesh,
        in_specs=(
            P(rows, None),
            P(rows, None),
            P(rows, None, None, None),
            P(rows, None),
            P(rows, None),
            P(rows, None),
            P(rows, None),
            P("expert", None, "inner", None),
            P("expert", None, "inner"),
        ),
        out_specs=(P(rows, None), P(rows, None)),
        check_vma=False,
    )
```

```python
import functools
import math

import jax
import jax.numpy as jnp
from jax import lax
from jax.experimental import pallas as pl
from jax.experimental.pallas import tpu as pltpu
from jax.sharding import PartitionSpec as P

QUERY_HEADS = 64
KEY_HEADS = 4
HEAD_SIZE = 128
CAP = 3
LANES = 128


def params(limit, *semantics):
    return pltpu.CompilerParams(
        dimension_semantics=semantics or None, vmem_limit_bytes=int(limit * 1024 * 1024)
    )


def attend_kernel(
    parents, q_ref, new_ref, cache_ref, after_ref, out_ref, done_ref, q_rows, new_rows, out_rows
):
    del after_ref
    done_ref[...] = jnp.zeros_like(done_ref)
    group = QUERY_HEADS // KEY_HEADS
    scale = 1.0 / math.sqrt(HEAD_SIZE)
    width = KEY_HEADS * HEAD_SIZE
    count, beams = q_ref.shape[0], cache_ref.shape[1]
    for h in range(QUERY_HEADS):
        q_rows[h * count:(h + 1) * count] = q_ref[
            :, h * HEAD_SIZE:(h + 1) * HEAD_SIZE
        ].astype(jnp.float32)
    for h in range(2 * KEY_HEADS):
        new_rows[h * count:(h + 1) * count] = new_ref[
            :, h * HEAD_SIZE:(h + 1) * HEAD_SIZE
        ].astype(jnp.float32)
    for r in range(count):
        request, parent = r // beams, parents[r]
        q = q_rows[pl.ds(r, QUERY_HEADS, stride=count), :]
        fresh = new_rows[pl.ds(r, 2 * KEY_HEADS, stride=count), :]
        scores, own = [], []
        for k in range(KEY_HEADS):
            qk = q[k * group:(k + 1) * group]
            keys = cache_ref[request, parent, :, k * HEAD_SIZE:(k + 1) * HEAD_SIZE]
            scores.append(
                lax.dot_general(
                    qk.astype(jnp.bfloat16),
                    keys,
                    (((1,), (1,)), ((), ())),
                    preferred_element_type=jnp.float32,
                )
            )
            own.append(jnp.sum(qk * fresh[k:k + 1], axis=-1, keepdims=True))
        scores = jnp.concatenate(scores, axis=0) * scale
        own = jnp.concatenate(own, axis=0) * scale
        upper = jnp.maximum(jnp.max(scores, axis=-1, keepdims=True), own)
        expo = jnp.exp(scores - upper)
        own_expo = jnp.exp(own - upper)
        total = jnp.sum(expo, axis=-1, keepdims=True) + own_expo
        probs = (expo / total).astype(jnp.bfloat16)
        own_prob = (own_expo / total).astype(jnp.bfloat16).astype(jnp.float32)
        for k in range(KEY_HEADS):
            heads = slice(k * group, (k + 1) * group)
            columns = slice(width + k * HEAD_SIZE, width + (k + 1) * HEAD_SIZE)
            result = jnp.dot(
                probs[heads], cache_ref[request, parent, :, columns], preferred_element_type=jnp.float32
            )
            out_rows[pl.ds(k * group * count + r, group, stride=count), :] = (
                result + own_prob[heads] * fresh[KEY_HEADS + k:KEY_HEADS + k + 1]
            )
    for h in range(QUERY_HEADS):
        out_ref[:, h * HEAD_SIZE:(h + 1) * HEAD_SIZE] = out_rows[
            h * count:(h + 1) * count
        ].astype(out_ref.dtype)


def attend(queries, new_key_value, cached_key_value, parents, after):
    rows = queries.shape[0]
    _, _, length, width = cached_key_value.shape
    vmem = pl.BlockSpec(memory_space=pltpu.VMEM)
    return pl.pallas_call(
        attend_kernel,
        in_specs=[pl.BlockSpec(memory_space=pltpu.SMEM), vmem, vmem, vmem]
        + [pl.BlockSpec(memory_space=pl.ANY)],
        out_specs=[vmem, vmem],
        out_shape=[
            jax.ShapeDtypeStruct(queries.shape, queries.dtype),
            jax.ShapeDtypeStruct((8, LANES), jnp.float32),
        ],
        scratch_shapes=[
            pltpu.VMEM(((QUERY_HEADS + 1) * rows, HEAD_SIZE), jnp.float32),
            pltpu.VMEM(((2 * KEY_HEADS + 1) * rows, HEAD_SIZE), jnp.float32),
            pltpu.VMEM(((QUERY_HEADS + 1) * rows, HEAD_SIZE), jnp.float32),
        ],
        compiler_params=params(32),
        cost_estimate=pl.CostEstimate(
            flops=4 * rows * QUERY_HEADS * HEAD_SIZE * length,
            bytes_accessed=2 * rows * length * width,
            transcendentals=rows * QUERY_HEADS * length,
        ),
        name="attend",
    )(parents.reshape(rows), queries, new_key_value, cached_key_value, after)


def spread(values, lanes, first):
    top = values.shape[0]
    shape = (top, lanes)
    chosen = (
        lax.broadcasted_iota(jnp.int32, shape, 1)
        == lax.broadcasted_iota(jnp.int32, shape, 0) + first
    ).astype(jnp.float32)
    return lax.dot_general(
        values.astype(jnp.float32), chosen, (((0,), (0,)), ((), ())), preferred_element_type=jnp.float32
    )


def prepare_kernel(indices, me, routes_ref, gates_ref, hidden_ref, *out_refs):
    width = out_refs[0].shape[1] - LANES
    top = routes_ref.shape[0]
    notes = spread(routes_ref[...], LANES, 0) + spread(gates_ref[...], LANES, top)
    notes = notes.astype(jnp.bfloat16)
    for s, out_ref in zip(indices, out_refs):
        start = pl.multiple_of((me[0] ^ s) * width, width)
        out_ref[:, :width] = hidden_ref[:, pl.ds(start, width)]
        out_ref[:, width:] = notes


def turned_notes(notes, top):
    shape = (max(8, 2 * top), LANES)
    chosen = (
        lax.broadcasted_iota(jnp.int32, shape, 0) == lax.broadcasted_iota(jnp.int32, shape, 1)
    ).astype(jnp.bfloat16)
    turned = lax.dot_general(
        chosen, notes, (((1,), (1,)), ((), ())), preferred_element_type=jnp.float32
    )
    return turned[:top], turned[top:2 * top]


def placing(routes, column, level, owners, experts, sources):
    top, rows = routes.shape
    count = CAP * sources
    shape = (owners * experts * count, rows)
    slot = lax.broadcasted_iota(jnp.int32, shape, 0)
    row = lax.broadcasted_iota(jnp.int32, shape, 1)
    each = rows // sources
    block = jnp.zeros(shape, jnp.int32)
    for n in range(1, owners * experts):
        block = block + (slot >= n * count).astype(jnp.int32)
    within = slot - block * count
    rank, source = within // sources, within % sources
    expert = ((column ^ (block // experts)) * experts + block % experts).astype(jnp.float32)
    member = jnp.zeros(shape, jnp.float32)
    for t in range(top):
        member = jnp.where(routes[t:t + 1] == expert, 1.0, member)
    origin = level ^ (row // each)
    member = jnp.where(origin == source, member, 0.0)
    one = lax.broadcasted_iota(jnp.int32, (rows, rows), 0)
    other = lax.broadcasted_iota(jnp.int32, (rows, rows), 1)
    before = (one < other).astype(jnp.float32)
    ranks = jnp.dot(member, before, preferred_element_type=jnp.float32)
    return jnp.where(ranks == rank.astype(jnp.float32), member, 0.0), expert


def pack_kernel(top, experts, sources, column, level, *refs):
    held, out_refs = refs[:sources], refs[sources:]
    slots, width = out_refs[0].shape
    rows = jnp.concatenate([ref[:, :width] for ref in held], axis=0)
    notes = jnp.concatenate([ref[:, width:] for ref in held], axis=0)
    routes, _ = turned_notes(notes, top)
    place, _ = placing(routes, column[0], level[0], len(out_refs), experts, sources)
    moved = jnp.dot(place.astype(jnp.bfloat16), rows, preferred_element_type=jnp.float32)
    for t, out_ref in enumerate(out_refs):
        out_ref[...] = moved[t * slots:(t + 1) * slots].astype(out_ref.dtype)


def weigh_kernel(top, experts, column, level, *refs):
    held, out_ref = refs[:-1], refs[-1]
    owners, slots, _ = out_ref.shape
    notes = jnp.concatenate([ref[:, -LANES:] for ref in held], axis=0)
    routes, gates = turned_notes(notes, top)
    place, expert = placing(routes, column[0], level[0], owners, experts, len(held))
    weight = jnp.zeros_like(place)
    for k in range(top):
        weight = weight + jnp.where(routes[k:k + 1] == expert, gates[k:k + 1], 0.0)
    weight = weight * place
    for t in range(owners):
        out_ref[t] = weight[t * slots:(t + 1) * slots].astype(out_ref.dtype)


def combine_kernel(weight_ref, *refs):
    owners = weight_ref.shape[0]
    back, out_refs = refs[:owners], refs[owners:]
    each = out_refs[0].shape[0]
    total = 0.0
    for t in range(owners):
        total = total + lax.dot_general(
            weight_ref[t],
            back[t][...],
            (((0,), (0,)), ((), ())),
            preferred_element_type=jnp.float32,
        )
    for s, out_ref in enumerate(out_refs):
        out_ref[...] = total[s * each:(s + 1) * each].astype(out_ref.dtype)


def assemble_kernel(me, *refs):
    pieces, out_ref = refs[:-1], refs[-1]
    width = pieces[0].shape[1]
    for s, piece in enumerate(pieces):
        start = pl.multiple_of((me[0] ^ s) * width, width)
        out_ref[:, pl.ds(start, width)] = piece[...]


def regroup(experts, owners, count):
    shape = (experts * owners * count, owners * experts * count)
    row = lax.broadcasted_iota(jnp.int32, shape, 0)
    other = lax.broadcasted_iota(jnp.int32, shape, 1)
    wanted = jnp.zeros(shape, jnp.int32) + row
    for x in range(experts):
        for t in range(owners):
            first = (x * owners + t) * count
            inside = (row >= first) & (row < first + count)
            wanted = jnp.where(inside, row - first + (t * experts + x) * count, wanted)
    return (other == wanted).astype(jnp.bfloat16)


def select_kernel(owners, *refs):
    packs, out_ref = refs[:owners], refs[-1]
    experts, count, _ = out_ref.shape
    rows = jnp.concatenate([ref[...].astype(jnp.float32) for ref in packs], axis=0)
    moved = jnp.dot(
        regroup(experts, len(packs), count // len(packs)),
        rows.astype(jnp.bfloat16),
        preferred_element_type=jnp.float32,
    ).astype(out_ref.dtype)
    for x in range(experts):
        out_ref[x] = moved[x * count:(x + 1) * count]


def load_kernel(pieces, weight_hbm, after_ref, *refs):
    del after_ref
    out_refs, done_ref, sems = refs[:-2], refs[-2], refs[-1]
    done_ref[...] = jnp.zeros_like(done_ref)
    step = weight_hbm.shape[2] // pieces
    copies = [
        pltpu.make_async_copy(
            weight_hbm.at[x, k, pl.ds(n * step, step)],
            out_ref.at[k, pl.ds(n * step, step)],
            sems.at[(x * 2 + k) * pieces + n],
        )
        for x, out_ref in enumerate(out_refs)
        for k in range(2)
        for n in range(pieces)
    ]
    for copy in copies:
        copy.start()
    for copy in copies:
        copy.wait()


def load(weight, after):
    experts, pieces = weight.shape[0], 4
    return pl.pallas_call(
        functools.partial(load_kernel, pieces),
        in_specs=[pl.BlockSpec(memory_space=pl.ANY)] * 2,
        out_specs=[pl.BlockSpec(memory_space=pltpu.VMEM)] * (experts + 1),
        out_shape=[jax.ShapeDtypeStruct(weight.shape[1:], weight.dtype)] * experts
        + [jax.ShapeDtypeStruct((8, LANES), jnp.float32)],
        scratch_shapes=[pltpu.SemaphoreType.DMA((experts * 2 * pieces,))],
        compiler_params=params(40),
        cost_estimate=pl.CostEstimate(flops=10**8, bytes_accessed=0, transcendentals=0),
        name="load",
    )(weight, after)


def gate_up_kernel(experts, afters, chunk, rows_ref, *refs):
    weight_refs, out_refs = refs[:experts], refs[experts + afters:]
    out_ref = out_refs[0]
    if len(out_refs) > 1:
        out_refs[1][...] = jnp.zeros_like(out_refs[1])
    ff = out_ref.shape[2] // 2
    columns = pl.ds(pl.multiple_of(chunk[0] * ff, ff), ff)
    for x in range(experts):
        for k in range(2):
            out_ref[x, :, k * ff:(k + 1) * ff] = jnp.dot(
                rows_ref[x], weight_refs[x][k, :, columns], preferred_element_type=jnp.float32
            ).astype(out_ref.dtype)


def gate_up(chunk, chunks, rows, weights, dtype, done=False, after=()):
    experts, count, _ = rows.shape
    ff = weights[0].shape[2] // chunks
    return call(
        functools.partial(gate_up_kernel, experts, len(after)),
        [chunk],
        [rows, *weights],
        [jax.ShapeDtypeStruct((experts, count, 2 * ff), dtype)]
        + [jax.ShapeDtypeStruct((8, LANES), jnp.float32)] * done,
        "gate_up",
        24,
        after=after,
        cost=2,
    )


def activate_kernel(own_ref, *refs):
    other_refs, out_ref = refs[:-2], refs[-1]
    ff = out_ref.shape[2]
    for x in range(out_ref.shape[0]):
        total = own_ref[x]
        for ref in other_refs:
            total = total + ref[x].astype(jnp.float32)
        gate, up = total[:, :ff], total[:, ff:]
        out_ref[x] = (gate / (1.0 + jnp.exp(-gate)) * up).astype(out_ref.dtype)


def down_product(part_ref, weight_ref, x, chunk):
    ff = part_ref.shape[2]
    rows = pl.ds(pl.multiple_of(chunk * ff, ff), ff)
    return jnp.dot(part_ref[x], weight_ref[x, rows], preferred_element_type=jnp.float32)


def down_first_kernel(me, part_ref, weight_ref, sum_ref):
    for x in range(part_ref.shape[0]):
        sum_ref[x] = down_product(part_ref, weight_ref, x, me[0])


def down_more_kernel(index, me, before_ref, part_ref, weight_ref, sum_ref):
    for x in range(part_ref.shape[0]):
        sum_ref[x] = before_ref[x] + down_product(part_ref, weight_ref, x, me[0] ^ index)


def down_rest_kernel(indices, me, sum_ref, *refs):
    count = len(indices)
    parts, weight_ref, out_refs = refs[:count], refs[count], refs[count + 1:]
    experts, slots, _ = sum_ref.shape
    sums = []
    for x in range(experts):
        total = sum_ref[x]
        for part_ref, index in zip(parts, indices):
            total = total + down_product(part_ref, weight_ref, x, me[0] ^ index)
        sums.append(total.astype(jnp.bfloat16))
    owners = len(out_refs)
    rows = experts * slots // owners
    moved = lax.dot_general(
        regroup(experts, owners, slots // owners),
        jnp.concatenate(sums, axis=0),
        (((0,), (0,)), ((), ())),
        preferred_element_type=jnp.float32,
    )
    for t, out_ref in enumerate(out_refs):
        out_ref[...] = moved[t * rows:(t + 1) * rows].astype(out_ref.dtype)


def traded(value, axis, index):
    return lax.ppermute(value, axis, [(i, i ^ index) for i in range(lax.axis_size(axis))])


def trade(values, axis):
    out = [values[0]] + [None] * (len(values) - 1)
    for s in reversed(range(1, len(values))):
        out[s] = traded(values[s], axis, s)
    return out


def call(kernel, index, inputs, outputs, name, limit=16, after=(), cost=0):
    single = not isinstance(outputs, list)
    return pl.pallas_call(
        kernel,
        in_specs=[pl.BlockSpec(memory_space=pltpu.SMEM)] * len(index)
        + [pl.BlockSpec(memory_space=pltpu.VMEM)] * len(inputs)
        + [pl.BlockSpec(memory_space=pl.ANY)] * len(after),
        out_specs=pl.BlockSpec(memory_space=pltpu.VMEM)
        if single
        else [pl.BlockSpec(memory_space=pltpu.VMEM)] * len(outputs),
        out_shape=outputs,
        compiler_params=params(limit),
        cost_estimate=pl.CostEstimate(
            flops=cost * 10**9, bytes_accessed=0, transcendentals=0
        ),
        name=name,
    )(*index, *inputs, *after)


def experts_by_columns(held, loaded, down_weight, owners, attention):
    inner = lax.axis_size("inner")
    experts, count, _ = held.shape
    ff, width = down_weight.shape[1:]
    me = lax.axis_index("inner").astype(jnp.int32)
    level = me.reshape(1)
    others, last = [], []
    for s in reversed(range(1, inner)):
        last = gate_up(
            (me ^ s).reshape(1), inner, held, loaded, jnp.bfloat16, after=last
        )
        others.append(traded(last[0], "inner", s))
    own, done = gate_up(level, inner, held, loaded, jnp.float32, True, last)
    attended, done = attention(done)
    active = call(
        activate_kernel,
        [],
        [own, *others],
        jax.ShapeDtypeStruct((experts, count, ff // inner), jnp.bfloat16),
        "activate",
        after=[done],
    )
    parts = trade([active] * inner, "inner")
    sums_shape = jax.ShapeDtypeStruct((experts, count, width), jnp.float32)
    sums = call(down_first_kernel, [level], [active, down_weight], sums_shape, "down_first", 24)
    for index in [inner - 1, *range(1, inner - 2)]:
        sums = call(
            functools.partial(down_more_kernel, index),
            [level],
            [sums, parts[index], down_weight],
            sums_shape,
            "down_more",
            24,
        )
    rest = [inner - 2]
    back = call(
        functools.partial(down_rest_kernel, rest),
        [level],
        [sums, *[parts[s] for s in rest], down_weight],
        [jax.ShapeDtypeStruct((experts * count // owners, width), jnp.bfloat16)] * owners,
        "down_rest",
        24,
    )
    return back, attended


def experts_by_rows(held, gate_up_weight, down_weight, owners, attention):
    experts, count, _ = held.shape
    partial = jnp.einsum("xsd,xkdf->sxkf", held, gate_up_weight, preferred_element_type=jnp.float32)
    summed = lax.psum_scatter(partial, "inner", scatter_dimension=0, tiled=True)
    active = (jax.nn.silu(summed[:, :, 0]) * summed[:, :, 1]).astype(jnp.bfloat16)
    active = lax.all_gather(active, "inner", axis=0, tiled=True)
    outputs = jnp.einsum("sxf,xfd->xsd", active, down_weight, preferred_element_type=jnp.float32)
    outputs = outputs.astype(jnp.bfloat16).reshape(experts, owners, count // owners, -1)
    back = [outputs[:, t].reshape(experts * count // owners, -1) for t in range(owners)]
    return back, attention(held)[0]


def body(
    queries,
    new_key_value,
    cached_key_value,
    parents,
    hidden,
    routes,
    gate_values,
    gate_up_weight,
    down_weight,
):
    owners, inner = lax.axis_size("expert"), lax.axis_size("inner")
    experts, _, depth, ff = gate_up_weight.shape
    rows, model = hidden.shape
    width = down_weight.shape[2]
    top = routes.shape[1]
    column = lax.axis_index("expert").astype(jnp.int32).reshape(1)
    level = lax.axis_index("inner").astype(jnp.int32).reshape(1)
    slots = experts * CAP * inner

    attention = functools.partial(attend, queries, new_key_value, cached_key_value, parents)

    even = ff % (inner * LANES) == 0
    shape = jax.ShapeDtypeStruct((rows, depth + LANES), jnp.bfloat16)
    arrays = [routes.T, gate_values.T, hidden]
    sent = call(
        functools.partial(prepare_kernel, range(1, inner)),
        [level],
        arrays,
        [shape] * (inner - 1),
        "prepare",
        66633728 / 1024 / 1024,
    )
    (kept,) = call(
        functools.partial(prepare_kernel, [0]), [level], arrays, [shape], "keep", cost=1
    )
    slices = [kept, *sent]
    slices = trade(slices, "inner")
    packs = call(
        functools.partial(pack_kernel, top, experts, inner),
        [column, level],
        slices,
        [jax.ShapeDtypeStruct((slots, depth), jnp.bfloat16)] * owners,
        "pack",
    )
    *loaded, done = load(gate_up_weight, packs[0]) if even else [None]
    packs = trade(packs, "expert")
    held = call(
        functools.partial(select_kernel, owners),
        [],
        packs,
        jax.ShapeDtypeStruct((experts, owners * CAP * inner, depth), jnp.bfloat16),
        "select",
        24,
        after=[done] if even else [],
    )
    back, attended = (experts_by_columns if even else experts_by_rows)(
        held, loaded or gate_up_weight, down_weight, owners, attention
    )
    back = trade(back, "expert")
    weights = call(
        functools.partial(weigh_kernel, top, experts),
        [column, level],
        slices,
        jax.ShapeDtypeStruct((owners, slots, inner * rows), jnp.bfloat16),
        "weigh",
        cost=1,
    )
    pieces = call(
        combine_kernel,
        [],
        [weights, *back],
        [jax.ShapeDtypeStruct((rows, width), jnp.bfloat16)] * inner,
        "combine",
    )
    pieces = trade(pieces, "inner")
    expert_out = call(
        assemble_kernel,
        [level],
        pieces,
        jax.ShapeDtypeStruct((rows, model), jnp.bfloat16),
        "assemble",
    )
    return attended, expert_out


def solution(mesh):
    rows = ("groups", "expert", "inner")
    return jax.shard_map(
        body,
        mesh=mesh,
        in_specs=(
            P(rows, None),
            P(rows, None),
            P(rows, None, None, None),
            P(rows, None),
            P(rows, None),
            P(rows, None),
            P(rows, None),
            P("expert", None, "inner", None),
            P("expert", None, "inner"),
        ),
        out_specs=(P(rows, None), P(rows, None)),
        check_vma=False,
    )
```
